32 devices in a mesh: seq: 8 (over z, x), dp: 4 (over y, core).
Axes of the slice: x: 2, y: 2, z: 4, core: 2. Of those that a mesh axis runs over, the one named last changes fastest.
Arguments:
- block_input: bfloat16 [8, 1024, 1536], P('dp', 'seq'), may hold values from -6 to 6
- cotangent: bfloat16 [8, 1024, 1536], P('dp', 'seq'), may hold values from -6 to 6
- lengths: int32 [8], P('dp'), may hold values from 256 to 1024, as said below
- qkvo_weight: float32 [1536, 6144], P(('seq', 'dp')), may hold values from -0.15625 to 0.15625
- proj_weight: float32 [1536, 1536], P(('seq', 'dp')), may hold values from -2.5 to 2.5
- gateup_weight: float32 [1536, 8192], P(('seq', 'dp')), may hold values from -0.15625 to 0.15625
- down_weight: float32 [4096, 1536], P(('seq', 'dp')), may hold values from -0.09375 to 0.09375
- forget_weight: float32 [1536, 24], replicated, may hold values from -0.15625 to 0.15625
- norm_params: float32 [3224], replicated, may hold values from 0.49 to 12
- qkvo_mean: float32 [1536, 6144], P(('seq', 'dp')), may hold values from -0.00030517578 to 0.00030517578
- qkvo_square: float32 [1536, 6144], P(('seq', 'dp')), may hold values from 1.7257696e-09 to 6.837955e-09
- proj_mean: float32 [1536, 1536], P(('seq', 'dp')), may hold values from -5.340576e-05 to 5.340576e-05
- proj_square: float32 [1536, 1536], P(('seq', 'dp')), may hold values from 5.39303e-11 to 2.136861e-10
- gateup_mean: float32 [1536, 8192], P(('seq', 'dp')), may hold values from -0.00030517578 to 0.00030517578
- gateup_square: float32 [1536, 8192], P(('seq', 'dp')), may hold values from 1.7257696e-09 to 6.837955e-09
- down_mean: float32 [4096, 1536], P(('seq', 'dp')), may hold values from -0.00030517578 to 0.00030517578
- down_square: float32 [4096, 1536], P(('seq', 'dp')), may hold values from 1.7257696e-09 to 6.837955e-09
- forget_mean: float32 [1536, 24], replicated, may hold values from -0.00030517578 to 0.00030517578
- forget_square: float32 [1536, 24], replicated, may hold values from 1.7257696e-09 to 6.837955e-09
- params_mean: float32 [3224], replicated, may hold values from -0.0012207031 to 0.0012207031
- params_square: float32 [3224], replicated, may hold values from 2.7677437e-08 to 1.1070975e-07
Outputs:
- block_output: bfloat16 [8, 1024, 1536], P('dp', 'seq')
- input_grad: float32 [8, 1024, 1536], P('dp', 'seq')
- grad_norm: float32 [], replicated
- new_qkvo: float32 [1536, 6144], P(('seq', 'dp'))
- new_qkvo_mean: float32 [1536, 6144], P(('seq', 'dp'))
- new_qkvo_square: float32 [1536, 6144], P(('seq', 'dp'))
- new_proj: float32 [1536, 1536], P(('seq', 'dp'))
- new_proj_mean: float32 [1536, 1536], P(('seq', 'dp'))
- new_proj_square: float32 [1536, 1536], P(('seq', 'dp'))
- new_gateup: float32 [1536, 8192], P(('seq', 'dp'))
- new_gateup_mean: float32 [1536, 8192], P(('seq', 'dp'))
- new_gateup_square: float32 [1536, 8192], P(('seq', 'dp'))
- new_down: float32 [4096, 1536], P(('seq', 'dp'))
- new_down_mean: float32 [4096, 1536], P(('seq', 'dp'))
- new_down_square: float32 [4096, 1536], P(('seq', 'dp'))
- new_forget: float32 [1536, 24], replicated
- new_forget_mean: float32 [1536, 24], replicated
- new_forget_square: float32 [1536, 24], replicated
- new_params: float32 [3224], replicated
- new_params_mean: float32 [3224], replicated
- new_params_square: float32 [3224], replicated
The draws below stay inside these ranges and needn't reach their ends.
Inputs may be any that keep to these rules, and one draw needn't show every extreme that they name: `lengths`: among the 2 sequences of each index of dp, one, drawn from the seed, has length 1024.
All inputs are finite; a program needn't handle non-finite values.
Results may differ from the reference program's by a relative error of at most 0.015.
Values may be sent and summed in bfloat16 or wider, within the bound.
A program may use at most 384 MiB of HBM per device.

```python
import math
import jax
import jax.numpy as jnp
from jax import lax

D = 1536
H = 24
HD = 64
FF = 4096
ROWS = 2
STEP = 10
SEQ_LEN = 1024
SEQS = 8
SMALL = 3224
NPARAMS = 30710936
N_DP = 4


def draw_lengths(key, part):
    key = jax.random.fold_in(key, 5)
    key_len, key_pick = jax.random.split(key)
    drawn_len = jax.random.randint(key_len, (SEQS,), SEQ_LEN // 4, SEQ_LEN, dtype=jnp.int32)
    pick_row = jax.random.randint(key_pick, (N_DP,), 0, ROWS, dtype=jnp.int32)
    full_rows = jnp.arange(N_DP, dtype=jnp.int32) * ROWS + pick_row
    is_full = jnp.any(jnp.arange(SEQS, dtype=jnp.int32)[:, None] == full_rows[None, :], axis=1)
    return jnp.where(is_full, SEQ_LEN, drawn_len).astype(jnp.int32)


def draw_norm_params(key, part):
    key = jax.random.fold_in(key, 11)
    keys_all = jax.random.split(key, 5)
    ramp = jnp.arange(D, dtype=jnp.float32) / D
    start_gain = 0.75
    end_gain = 1.3
    lower_frac = 0.0
    slope = start_gain * (end_gain / start_gain) ** ramp
    gain_attn = slope * jax.random.uniform(keys_all[0], (D,), jnp.float32, 0.8, 1.25)
    gain_ffn = slope * jax.random.uniform(keys_all[1], (D,), jnp.float32, 0.8, 1.25)
    gain_query = jax.random.uniform(keys_all[2], (HD,), jnp.float32, 0.9, 1.5)
    gain_key = jax.random.uniform(keys_all[3], (HD,), jnp.float32, 0.9, 1.5)
    fast_end = math.log(40.0)
    slow_end = math.log(4.0 * SEQ_LEN)
    fractions = jax.random.uniform(keys_all[4], (H,), jnp.float32, lower_frac, 1.0)
    bias_forget = fast_end + (slow_end - fast_end) * fractions
    return jnp.concatenate([gain_attn, gain_ffn, gain_query, gain_key, bias_forget]).astype(jnp.float32)


def shard_levels(rng, shape, pieces, low, top_value):
    factor_of, own = 1.0, jax.random.fold_in(rng, 6)
    for position, parts in pieces:
        draws = jnp.exp(jax.random.uniform(jax.random.fold_in(own, position), (parts,), jnp.float32, low / len(pieces), top_value / len(pieces)))
        factor_of = factor_of * jnp.repeat(draws, shape[position] // parts).reshape([-1 if axis == position else 1 for axis in range(len(shape))])
    return factor_of


def bell_draw(rng, extent, width, reach, shards=(), kind=jnp.bfloat16):
    drawn = width * jax.random.normal(rng, extent, jnp.float32)
    if shards:
        drawn = drawn * shard_levels(rng, extent, shards, -0.22, 0.18)
    return jnp.clip(drawn, -reach, reach).astype(kind)


def setup_inputs(seed: int = 0) -> dict:
    keys = jax.random.split(jax.random.key(seed), 22)
    block_input = bell_draw(keys[0], (SEQS, SEQ_LEN, D), 1.0, 6.0, ((0, 4), (1, 8)))
    cotangent = bell_draw(keys[1], (SEQS, SEQ_LEN, D), 1.0, 6.0, ((0, 4), (1, 8)))
    lengths = draw_lengths(jax.random.fold_in(keys[21], 71), 0)
    qkvo_weight = bell_draw(keys[3], (D, 4 * D), D ** -0.5, 0.15625, ((0, 32),), jnp.float32)
    proj_weight = bell_draw(keys[4], (D, D), (max(D // 256, 2)) ** -0.5, 2.5, ((0, 32),), jnp.float32)
    gateup_weight = bell_draw(keys[5], (D, 2 * FF), D ** -0.5, 0.15625, ((0, 32),), jnp.float32)
    down_weight = bell_draw(keys[6], (FF, D), FF ** -0.5, 0.09375, ((0, 32),), jnp.float32)
    forget_weight = bell_draw(keys[7], (D, H), D ** -0.5, 0.15625, (), jnp.float32)
    norm_params = draw_norm_params(jax.random.fold_in(keys[21], 71), 0)
    qkvo_mean = bell_draw(keys[9], (D, 4 * D), (0.11 / NPARAMS ** 0.5), 0.00030517578, ((0, 32),), jnp.float32)
    qkvo_square = jnp.clip(jnp.exp(math.log(6.837955091043568e-09) - 1.3768156 * jax.random.uniform(keys[10], (D, 4 * D), jnp.float32) ** shard_levels(keys[10], (D, 4 * D), ((0, 32),), -0.2, 0.2)), 1.7257696383055077e-09, 6.837955091043568e-09)
    proj_mean = bell_draw(keys[11], (D, D), (0.11 * min(32 / SEQ_LEN, 1) ** 0.5 / NPARAMS ** 0.5), 5.340576171875e-05, ((0, 32),), jnp.float32)
    proj_square = jnp.clip(jnp.exp(math.log(2.136860965951115e-10) - 1.3768156 * jax.random.uniform(keys[12], (D, D), jnp.float32) ** shard_levels(keys[12], (D, D), ((0, 32),), -0.2, 0.2)), 5.3930301197047115e-11, 2.136860965951115e-10)
    gateup_mean = bell_draw(keys[13], (D, 2 * FF), (0.11 / NPARAMS ** 0.5), 0.00030517578, ((0, 32),), jnp.float32)
    gateup_square = jnp.clip(jnp.exp(math.log(6.837955091043568e-09) - 1.3768156 * jax.random.uniform(keys[14], (D, 2 * FF), jnp.float32) ** shard_levels(keys[14], (D, 2 * FF), ((0, 32),), -0.2, 0.2)), 1.7257696383055077e-09, 6.837955091043568e-09)
    down_mean = bell_draw(keys[15], (FF, D), (0.11 / NPARAMS ** 0.5), 0.00030517578, ((0, 32),), jnp.float32)
    down_square = jnp.clip(jnp.exp(math.log(6.837955091043568e-09) - 1.3768156 * jax.random.uniform(keys[16], (FF, D), jnp.float32) ** shard_levels(keys[16], (FF, D), ((0, 32),), -0.2, 0.2)), 1.7257696383055077e-09, 6.837955091043568e-09)
    forget_mean = bell_draw(keys[17], (D, H), (0.11 / NPARAMS ** 0.5), 0.00030517578, (), jnp.float32)
    forget_square = jnp.clip(jnp.exp(jax.random.uniform(keys[18], (D, H), jnp.float32, math.log(1.7257696383055077e-09), math.log(6.837955091043568e-09))), 1.7257696383055077e-09, 6.837955091043568e-09)
    params_mean = bell_draw(keys[19], (SMALL,), (0.44 / NPARAMS ** 0.5), 0.0012207031, (), jnp.float32)
    params_square = jnp.clip(jnp.exp(jax.random.uniform(keys[20], (SMALL,), jnp.float32, math.log(2.7677437230977375e-08), math.log(1.107097489239095e-07))), 2.7677437230977375e-08, 1.107097489239095e-07)
    return {"block_input": block_input, "cotangent": cotangent, "lengths": lengths, "qkvo_weight": qkvo_weight, "proj_weight": proj_weight, "gateup_weight": gateup_weight, "down_weight": down_weight, "forget_weight": forget_weight, "norm_params": norm_params, "qkvo_mean": qkvo_mean, "qkvo_square": qkvo_square, "proj_mean": proj_mean, "proj_square": proj_square, "gateup_mean": gateup_mean, "gateup_square": gateup_square, "down_mean": down_mean, "down_square": down_square, "forget_mean": forget_mean, "forget_square": forget_square, "params_mean": params_mean, "params_square": params_square}


@jax.custom_vjp
def low(v):
    return lax.optimization_barrier(v.astype(jnp.bfloat16)).astype(jnp.float32)

@jax.custom_vjp
def low_back(v):
    return v

def low_keep(v):
    return (low(v), None)

def low_pass(kept, grad):
    return (grad,)

def back_keep(v):
    return (v, None)

def back_low(kept, grad):
    return (low(grad),)
low.defvjp(low_keep, low_pass)
low_back.defvjp(back_keep, back_low)
eps_norm = 1e-06
beta_one = 0.9
beta_two = 0.95
rate_dense = 0.06
rate_small = 0.6
decay_dense = 0.1
adam_eps = 1e-08
neg_large = -1e+30
highest = lax.Precision.HIGHEST

def rms_scale(values, gain_vec):
    return values * lax.rsqrt(lax.optimization_barrier(jnp.mean(values * values, axis=-1, keepdims=True)) + eps_norm) * gain_vec

def matmul(left, right):
    return jnp.dot(left, right, precision=highest, preferred_element_type=jnp.float32)

def attend_row(arrays):
    queries, keys_row, values_row, cumul, length = arrays
    seq_total = queries.shape[0]
    block_rows = min(512, seq_total)
    key_pos = jnp.arange(seq_total, dtype=jnp.int32)
    key_live = key_pos < length

    def one_block(block_start):
        query_block = lax.dynamic_slice_in_dim(queries, block_start, block_rows, 0)
        cumul_block = lax.dynamic_slice_in_dim(cumul, block_start, block_rows, 0)
        query_pos = block_start + jnp.arange(block_rows, dtype=jnp.int32)
        scores = jnp.einsum('qhd,khd->hqk', query_block, keys_row, precision=highest) * HD ** (-0.5)
        scores = scores + cumul_block.T[:, :, None] - cumul.T[:, None, :]
        allowed = (key_pos[None, :] <= query_pos[:, None]) & key_live[None, :]
        scores = low_back(jnp.where(allowed[None], scores, neg_large))
        log_total = jax.nn.logsumexp(scores, axis=-1, keepdims=True)
        attn_probs = low(jnp.exp(scores - log_total))
        return jnp.einsum('hqk,khd->qhd', attn_probs, values_row, precision=highest)
    starts = jnp.arange(seq_total // block_rows, dtype=jnp.int32) * block_rows
    blocks = lax.map(jax.checkpoint(one_block), starts)
    return blocks.reshape(seq_total, queries.shape[1], queries.shape[2])

def forward(inputs, qkvo_in, proj_in, gateup_in, down_in, forget_in, params, lengths):
    seq_count = inputs.shape[0]
    seq_total = inputs.shape[1]
    gain_attn = params[:D]
    gain_ffn = params[D:2 * D]
    gain_query = params[2 * D:2 * D + HD]
    gain_key = params[2 * D + HD:2 * D + 2 * HD]
    bias_forget = params[2 * D + 2 * HD:]
    rows_all = inputs.reshape(-1, D)
    normed = low(rms_scale(rows_all, gain_attn))
    projected = low_back(matmul(normed, qkvo_in))
    logits = matmul(normed, forget_in) + bias_forget
    query_raw, key_raw, value_raw, gate_raw = jnp.split(projected, 4, axis=1)
    queries = low(rms_scale(query_raw.reshape(-1, H, HD), gain_query))
    keys_all = low(rms_scale(key_raw.reshape(-1, H, HD), gain_key))
    values_all = low(value_raw.reshape(-1, H, HD))
    cumul = jnp.cumsum(jax.nn.log_sigmoid(logits).reshape(seq_count, seq_total, H), axis=1)
    head_shape = (seq_count, seq_total, H, HD)
    attended = lax.map(attend_row, (queries.reshape(head_shape), keys_all.reshape(head_shape), values_all.reshape(head_shape), cumul, lengths))
    attended = low_back(attended.reshape(-1, D))
    mixed = low(attended * jax.nn.sigmoid(gate_raw))
    middle = rows_all + low_back(matmul(mixed, proj_in))
    normed_two = low(rms_scale(middle, gain_ffn))
    gateup = low_back(matmul(normed_two, gateup_in))
    hidden = low(jax.nn.silu(gateup[:, :FF]) * gateup[:, FF:])
    result = middle + low_back(matmul(hidden, down_in))
    return result.reshape(seq_count, seq_total, D)

def adam_update(weight, gradient, mean_old, square_old, learn_rate, decay_rate):
    mean_new = beta_one * mean_old + (1.0 - beta_one) * gradient
    square_new = beta_two * square_old + (1.0 - beta_two) * gradient * gradient
    moved = mean_new / (1.0 - beta_one ** STEP) / (jnp.sqrt(square_new / (1.0 - beta_two ** STEP)) + adam_eps)
    return (weight - learn_rate * (moved + decay_rate * weight), mean_new, square_new)

def reference(block_input, cotangent, lengths, qkvo_weight, proj_weight, gateup_weight, down_weight, forget_weight, norm_params, qkvo_mean, qkvo_square, proj_mean, proj_square, gateup_mean, gateup_square, down_mean, down_square, forget_mean, forget_square, params_mean, params_square):
    inputs = block_input.astype(jnp.float32)
    rate_proj = rate_dense * (D / max(D // 256, 2)) ** 0.5

    def layer(inputs_in, qkvo_in, proj_in, gateup_in, down_in, forget_in, params_in):
        return forward(inputs_in, qkvo_in, proj_in, gateup_in, down_in, forget_in, params_in, lengths)
    result, pullback = jax.vjp(layer, inputs, low(qkvo_weight), low(proj_weight), low(gateup_weight), low(down_weight), forget_weight, norm_params)
    positions = jnp.arange(block_input.shape[1], dtype=jnp.int32)
    valid = (positions[None, :] < lengths[:, None]).astype(jnp.float32)
    gradients = pullback(cotangent.astype(jnp.float32) * valid[:, :, None])
    squares = jnp.float32(0.0)
    for gradient in gradients[1:]:
        squares = squares + jnp.sum(gradient * gradient)
    grad_norm = jnp.sqrt(squares)
    clip_factor = 1.0 / jnp.maximum(grad_norm, 1.0)
    qkvo_new, qkvo_m, qkvo_v = adam_update(qkvo_weight, gradients[1] * clip_factor, qkvo_mean, qkvo_square, rate_dense, decay_dense)
    proj_new, proj_m, proj_v = adam_update(proj_weight, gradients[2] * clip_factor, proj_mean, proj_square, rate_proj, decay_dense)
    gateup_new, gateup_m, gateup_v = adam_update(gateup_weight, gradients[3] * clip_factor, gateup_mean, gateup_square, rate_dense, decay_dense)
    down_new, down_m, down_v = adam_update(down_weight, gradients[4] * clip_factor, down_mean, down_square, rate_dense, decay_dense)
    forget_new, forget_m, forget_v = adam_update(forget_weight, gradients[5] * clip_factor, forget_mean, forget_square, rate_dense, decay_dense)
    params_new, params_m, params_v = adam_update(norm_params, gradients[6] * clip_factor, params_mean, params_square, rate_small, 0.0)
    return (result.astype(jnp.bfloat16), gradients[0], grad_norm, qkvo_new, qkvo_m, qkvo_v, proj_new, proj_m, proj_v, gateup_new, gateup_m, gateup_v, down_new, down_m, down_v, forget_new, forget_m, forget_v, params_new, params_m, params_v)
```

```python
import functools

import jax
import jax.numpy as jnp
from jax import lax
from jax.experimental import pallas as pl
from jax.experimental.pallas import tpu as pltpu
from jax.sharding import Mesh
from jax.sharding import PartitionSpec as P

D = 1536
H = 24
HD = 64
FF = 4096
STEP = 10


eps_norm = 1e-06
beta_one = 0.9
beta_two = 0.95
rate_dense = 0.06
rate_small = 0.6
decay_dense = 0.1
adam_eps = 1e-08
neg_large = -1e30
highest = lax.Precision.HIGHEST


def entering(value, axis, join, neutral, backward):
    count, mine = (lax.axis_size(axis), lax.axis_index(axis))
    pieces = lax.all_gather(value, axis)
    if backward:
        pieces = pieces[::-1]
        mine = count - 1 - mine
    running = jnp.full_like(value, 0) + jnp.asarray(neutral, value.dtype)

    def hop(position, running):
        longer = join(running, pieces[position])
        return jnp.where(position < mine, longer, running)

    return lax.fori_loop(0, count - 1, hop, running)


def rms_scale(values, gain_vec):
    return (
        values * lax.rsqrt(jnp.mean(values * values, axis=-1, keepdims=True) + eps_norm) * gain_vec
    )


def heads_in(projected, logits, gain_query, gain_key):
    token_count = projected.shape[0]
    query_raw, key_raw, value_raw, gate_raw = jnp.split(projected, 4, axis=1)
    queries = rms_scale(query_raw.reshape(token_count, H, HD), gain_query)
    keys_out = rms_scale(key_raw.reshape(token_count, H, HD), gain_key)
    return (
        queries,
        keys_out,
        value_raw.reshape(token_count, H, HD),
        jax.nn.sigmoid(gate_raw),
        jax.nn.log_sigmoid(logits),
    )


def swiglu(gateup):
    return jax.nn.silu(gateup[:, :FF]) * gateup[:, FF:]


def add_terms(earlier, later):
    return earlier + later


def contract_rows(left, right):
    return lax.dot_general(
        left, right, (((0,), (0,)), ((), ())), preferred_element_type=jnp.float32
    )


def contract_cols(left, right):
    return lax.dot_general(
        left, right, (((1,), (1,)), ((), ())), preferred_element_type=jnp.float32
    )


def sub_width(piece_len, block_len):
    pieces = piece_len // block_len
    group_size = 1
    while group_size * 2 * block_len <= 256 and pieces % (group_size * 2) == 0:
        group_size = group_size * 2
    return group_size * block_len


def scores_of(query_part, key_part, cumul_query, cumul_key):
    raw_dots = jnp.einsum(
        "rqhd,rkhd->rhqk", query_part, key_part, preferred_element_type=jnp.float32
    )
    return raw_dots * HD ** (-0.5) + cumul_query[:, :, :, None] - cumul_key[:, :, None, :]


def allowed_of(query_pos, key_pos, lengths):
    causal = key_pos[None, None, :] <= query_pos[None, :, None]
    inside = key_pos[None, None, :] < lengths[:, None, None]
    return (causal & inside)[:, None]


def adam_update(weight, gradient, mean_old, square_old, learn_rate, decay_rate):
    mean_new = beta_one * mean_old + (1.0 - beta_one) * gradient
    square_new = beta_two * square_old + (1.0 - beta_two) * gradient * gradient
    moved = (
        mean_new
        / (1.0 - beta_one**STEP)
        / (jnp.sqrt(square_new / (1.0 - beta_two**STEP)) + adam_eps)
    )
    return (weight - learn_rate * (moved + decay_rate * weight), mean_new, square_new)


def general_device(
    block_input,
    cotangent,
    lengths,
    qkvo_weight,
    proj_weight,
    gateup_weight,
    down_weight,
    forget_weight,
    norm_params,
    qkvo_mean,
    qkvo_square,
    proj_mean,
    proj_square,
    gateup_mean,
    gateup_square,
    down_mean,
    down_square,
    forget_mean,
    forget_square,
    params_mean,
    params_square,
):
    rows_here = block_input.shape[0]
    block_len = block_input.shape[1]
    token_count = rows_here * block_len
    cycle_index = lax.axis_index("seq")
    my_start = cycle_index * block_len
    positions = my_start + jnp.arange(block_len, dtype=jnp.int32)
    last_pos = my_start + block_len - 1
    longest = jnp.max(lengths)
    head_shape = (rows_here, block_len, H, HD)
    scale_dot = HD ** (-0.5)
    rate_proj = rate_dense * (D / max(D // 256, 2)) ** 0.5
    qkvo_full, proj_full, gateup_full, down_full = (
        lax.all_gather(qkvo_weight.astype(jnp.bfloat16), ("seq", "dp"), axis=0, tiled=True),
        lax.all_gather(proj_weight.astype(jnp.bfloat16), ("seq", "dp"), axis=0, tiled=True),
        lax.all_gather(gateup_weight.astype(jnp.bfloat16), ("seq", "dp"), axis=0, tiled=True),
        lax.all_gather(down_weight.astype(jnp.bfloat16), ("seq", "dp"), axis=0, tiled=True),
    )
    gain_attn = norm_params[:D]
    gain_ffn = norm_params[D : 2 * D]
    gain_query = norm_params[2 * D : 2 * D + HD]
    gain_key = norm_params[2 * D + HD : 2 * D + 2 * HD]
    bias_forget = norm_params[2 * D + 2 * HD :]
    inputs = block_input.astype(jnp.float32).reshape(token_count, D)
    normed, norm_pull = jax.vjp(rms_scale, inputs, gain_attn)
    normed_low = normed.astype(jnp.bfloat16)
    normed_back = normed_low.astype(jnp.float32)
    projected = jnp.dot(normed_low, qkvo_full, preferred_element_type=jnp.float32)
    logits = jnp.dot(normed_back, forget_weight, precision=highest) + bias_forget
    head_values, heads_pull = jax.vjp(heads_in, projected, logits, gain_query, gain_key)
    queries, keys_out, values_out, outgate, log_forget = head_values
    query_low = queries.astype(jnp.bfloat16).reshape(head_shape)
    key_low = keys_out.astype(jnp.bfloat16).reshape(head_shape)
    value_low = values_out.astype(jnp.bfloat16).reshape(head_shape)
    local_cumul = jnp.cumsum(log_forget.reshape(rows_here, block_len, H), axis=1)
    offset = entering(
        local_cumul[:, -1, :], "seq", add_terms, jnp.zeros((rows_here, H), jnp.float32), False
    )
    cumul = local_cumul + offset[:, None, :]
    cumul_all = lax.all_gather(cumul, "seq", axis=1, tiled=True)
    cumul_own = cumul.transpose(0, 2, 1)
    start_state = (
        jnp.full((rows_here, H, block_len), neg_large, jnp.float32),
        jnp.zeros((rows_here, H, block_len), jnp.float32),
        jnp.zeros((rows_here, H, block_len, HD), jnp.float32),
    )
    key_piece = lax.all_gather(key_low, "seq", axis=1, tiled=True)
    value_piece = lax.all_gather(value_low, "seq", axis=1, tiled=True)
    piece_len = key_piece.shape[1]
    sub_len = sub_width(piece_len, block_len)

    def forward_update(sub_index, state_now):
        key_start = sub_index * sub_len

        def forward_compute(state_run):
            run_max, run_sum, run_acc = state_run
            key_block = lax.dynamic_slice_in_dim(key_piece, sub_index * sub_len, sub_len, 1)
            value_block = lax.dynamic_slice_in_dim(value_piece, sub_index * sub_len, sub_len, 1)
            cumul_block = lax.dynamic_slice_in_dim(cumul_all, key_start, sub_len, 1).transpose(
                0, 2, 1
            )
            key_pos = key_start + jnp.arange(sub_len, dtype=jnp.int32)
            allowed = allowed_of(positions, key_pos, lengths)
            scores = jnp.where(
                allowed, scores_of(query_low, key_block, cumul_own, cumul_block), neg_large
            )
            new_max = jnp.maximum(run_max, jnp.max(scores, axis=-1))
            factor = jnp.exp(run_max - new_max)
            attn_probs = jnp.where(allowed, jnp.exp(scores - new_max[..., None]), 0.0)
            run_sum = run_sum * factor + jnp.sum(attn_probs, axis=-1)
            run_acc = run_acc * factor[..., None] + jnp.einsum(
                "rhqk,rkhd->rhqd",
                attn_probs.astype(jnp.bfloat16),
                value_block,
                preferred_element_type=jnp.float32,
            )
            return (new_max, run_sum, run_acc)

        is_live = (key_start <= last_pos) & (key_start < longest)
        return lax.cond(is_live, forward_compute, lambda state_run: state_run, state_now)

    run_max, run_sum, run_acc = lax.fori_loop(0, piece_len // sub_len, forward_update, start_state)
    attended = run_acc / run_sum[..., None]
    log_total = run_max + jnp.log(run_sum)
    attended_rows = attended.transpose(0, 2, 1, 3).reshape(token_count, D)
    mixed_low = (attended_rows * outgate).astype(jnp.bfloat16)
    middle = inputs + jnp.dot(mixed_low, proj_full, preferred_element_type=jnp.float32)
    normed_two, norm_two_pull = jax.vjp(rms_scale, middle, gain_ffn)
    normed_two_low = normed_two.astype(jnp.bfloat16)
    gateup = jnp.dot(normed_two_low, gateup_full, preferred_element_type=jnp.float32)
    hidden, swiglu_pull = jax.vjp(swiglu, gateup)
    hidden_low = hidden.astype(jnp.bfloat16)
    result = middle + jnp.dot(hidden_low, down_full, preferred_element_type=jnp.float32)
    block_output = result.astype(jnp.bfloat16).reshape(rows_here, block_len, D)
    valid = (positions[None, :] < lengths[:, None]).astype(jnp.float32)
    grad_out = (cotangent.astype(jnp.float32) * valid[:, :, None]).reshape(token_count, D)
    grad_out_low = grad_out.astype(jnp.bfloat16)
    grad_down_w = contract_rows(hidden_low, grad_out_low)
    grad_hidden = contract_cols(grad_out_low, down_full)
    grad_gateup_low = swiglu_pull(grad_hidden)[0].astype(jnp.bfloat16)
    grad_gateup_w = contract_rows(normed_two_low, grad_gateup_low)
    grad_normed_two = contract_cols(grad_gateup_low, gateup_full)
    grad_middle_part, grad_gain_ffn = norm_two_pull(grad_normed_two)
    grad_middle = grad_out + grad_middle_part
    grad_middle_low = grad_middle.astype(jnp.bfloat16)
    grad_proj_w = contract_rows(mixed_low, grad_middle_low)
    grad_mixed = contract_cols(grad_middle_low, proj_full)
    grad_outgate = grad_mixed * attended_rows
    grad_att_low = (grad_mixed * outgate).astype(jnp.bfloat16).reshape(head_shape)
    delta = jnp.sum(
        grad_att_low.astype(jnp.float32) * attended.transpose(0, 2, 1, 3), axis=-1
    ).transpose(0, 2, 1)
    lse_all, delta_all = (
        lax.all_gather(log_total, "seq", axis=2, tiled=True),
        lax.all_gather(delta, "seq", axis=2, tiled=True),
    )
    query_state = (
        jnp.zeros((rows_here, H, block_len, HD), jnp.float32),
        jnp.zeros((rows_here, H, block_len), jnp.float32),
    )
    query_key_piece = lax.all_gather(key_low, "seq", axis=1, tiled=True)
    query_value_piece = lax.all_gather(value_low, "seq", axis=1, tiled=True)
    piece_len = query_key_piece.shape[1]
    query_sub_len = sub_width(piece_len, block_len)

    def query_update(sub_index, state_now):
        key_start = sub_index * query_sub_len

        def query_compute(state_run):
            grad_query, grad_cq = state_run
            key_block = lax.dynamic_slice_in_dim(
                query_key_piece, sub_index * query_sub_len, query_sub_len, 1
            )
            value_block = lax.dynamic_slice_in_dim(
                query_value_piece, sub_index * query_sub_len, query_sub_len, 1
            )
            cumul_block = lax.dynamic_slice_in_dim(
                cumul_all, key_start, query_sub_len, 1
            ).transpose(0, 2, 1)
            key_pos = key_start + jnp.arange(query_sub_len, dtype=jnp.int32)
            allowed = allowed_of(positions, key_pos, lengths)
            scores = jnp.where(
                allowed, scores_of(query_low, key_block, cumul_own, cumul_block), neg_large
            )
            attn_probs = jnp.where(allowed, jnp.exp(scores - log_total[..., None]), 0.0)
            grad_probs = jnp.einsum(
                "rqhd,rkhd->rhqk", grad_att_low, value_block, preferred_element_type=jnp.float32
            )
            scores_low = (attn_probs * (grad_probs - delta[..., None])).astype(jnp.bfloat16)
            grad_query = (
                grad_query
                + jnp.einsum(
                    "rhqk,rkhd->rhqd", scores_low, key_block, preferred_element_type=jnp.float32
                )
                * scale_dot
            )
            grad_cq = grad_cq + jnp.sum(scores_low.astype(jnp.float32), axis=-1)
            return (grad_query, grad_cq)

        is_live = (key_start <= last_pos) & (key_start < longest)
        return lax.cond(is_live, query_compute, lambda state_run: state_run, state_now)

    grad_query, grad_cq = lax.fori_loop(0, piece_len // query_sub_len, query_update, query_state)
    key_state = (
        jnp.zeros((rows_here, H, block_len, HD), jnp.float32),
        jnp.zeros((rows_here, H, block_len, HD), jnp.float32),
        jnp.zeros((rows_here, H, block_len), jnp.float32),
    )
    query_piece = lax.all_gather(query_low, "seq", axis=1, tiled=True)
    dout_piece = lax.all_gather(grad_att_low, "seq", axis=1, tiled=True)
    piece_len = query_piece.shape[1]
    key_sub_len = sub_width(piece_len, block_len)

    def key_update(sub_index, state_now):
        query_start = sub_index * key_sub_len

        def key_compute(state_run):
            grad_key, grad_value, grad_ck = state_run
            query_block = lax.dynamic_slice_in_dim(
                query_piece, sub_index * key_sub_len, key_sub_len, 1
            )
            dout_block = lax.dynamic_slice_in_dim(
                dout_piece, sub_index * key_sub_len, key_sub_len, 1
            )
            lse_block = lax.dynamic_slice_in_dim(lse_all, query_start, key_sub_len, 2)
            delta_block = lax.dynamic_slice_in_dim(delta_all, query_start, key_sub_len, 2)
            cumul_block = lax.dynamic_slice_in_dim(
                cumul_all, query_start, key_sub_len, 1
            ).transpose(0, 2, 1)
            query_pos = query_start + jnp.arange(key_sub_len, dtype=jnp.int32)
            allowed = allowed_of(query_pos, positions, lengths)
            scores = jnp.where(
                allowed, scores_of(query_block, key_low, cumul_block, cumul_own), neg_large
            )
            attn_probs = jnp.where(allowed, jnp.exp(scores - lse_block[..., None]), 0.0)
            grad_value = grad_value + jnp.einsum(
                "rhqk,rqhd->rhkd",
                attn_probs.astype(jnp.bfloat16),
                dout_block,
                preferred_element_type=jnp.float32,
            )
            grad_probs = jnp.einsum(
                "rqhd,rkhd->rhqk", dout_block, value_low, preferred_element_type=jnp.float32
            )
            scores_low = (attn_probs * (grad_probs - delta_block[..., None])).astype(jnp.bfloat16)
            grad_key = (
                grad_key
                + jnp.einsum(
                    "rhqk,rqhd->rhkd", scores_low, query_block, preferred_element_type=jnp.float32
                )
                * scale_dot
            )
            grad_ck = grad_ck - jnp.sum(scores_low.astype(jnp.float32), axis=2)
            return (grad_key, grad_value, grad_ck)

        is_live = query_start + key_sub_len - 1 >= my_start
        return lax.cond(is_live, key_compute, lambda state_run: state_run, state_now)

    grad_key, grad_value, grad_ck = lax.fori_loop(
        0, piece_len // key_sub_len, key_update, key_state
    )
    grad_cumul = (grad_cq + grad_ck).transpose(0, 2, 1)
    local_suffix = jnp.flip(jnp.cumsum(jnp.flip(grad_cumul, axis=1), axis=1), axis=1)
    suffix = entering(
        local_suffix[:, 0, :], "seq", add_terms, jnp.zeros((rows_here, H), jnp.float32), True
    )
    grad_log_forget = (local_suffix + suffix[:, None, :]).reshape(token_count, H)
    grad_queries = grad_query.transpose(0, 2, 1, 3).reshape(token_count, H, HD)
    grad_keys = grad_key.transpose(0, 2, 1, 3).reshape(token_count, H, HD)
    grad_values = grad_value.transpose(0, 2, 1, 3).reshape(token_count, H, HD)
    grad_projected, grad_logits, grad_gain_query, grad_gain_key = heads_pull(
        (grad_queries, grad_keys, grad_values, grad_outgate, grad_log_forget)
    )
    grad_projected_low = grad_projected.astype(jnp.bfloat16)
    grad_qkvo_w = contract_rows(normed_low, grad_projected_low)
    grad_forget_w = lax.dot_general(
        normed_back,
        grad_logits,
        (((0,), (0,)), ((), ())),
        precision=highest,
        preferred_element_type=jnp.float32,
    )
    grad_bias = jnp.sum(grad_logits, axis=0)
    grad_normed = contract_cols(grad_projected_low, qkvo_full) + jnp.dot(
        grad_logits, forget_weight.T, precision=highest
    )
    grad_inputs_part, grad_gain_attn = norm_pull(grad_normed)
    input_grad = (grad_middle + grad_inputs_part).reshape(rows_here, block_len, D)
    qkvo_shard, proj_shard, gateup_shard, down_shard = (
        lax.psum_scatter(grad_qkvo_w, ("seq", "dp"), scatter_dimension=0, tiled=True),
        lax.psum_scatter(grad_proj_w, ("seq", "dp"), scatter_dimension=0, tiled=True),
        lax.psum_scatter(grad_gateup_w, ("seq", "dp"), scatter_dimension=0, tiled=True),
        lax.psum_scatter(grad_down_w, ("seq", "dp"), scatter_dimension=0, tiled=True),
    )
    shard_squares = (
        jnp.sum(qkvo_shard * qkvo_shard)
        + jnp.sum(proj_shard * proj_shard)
        + jnp.sum(gateup_shard * gateup_shard)
        + jnp.sum(down_shard * down_shard)
    )
    small_grads = jnp.concatenate(
        [grad_gain_attn, grad_gain_ffn, grad_gain_query, grad_gain_key, grad_bias]
    )
    small_total, forget_total, square_total = lax.psum(
        (small_grads, grad_forget_w, shard_squares), ("seq", "dp")
    )
    grad_norm = jnp.sqrt(
        square_total + jnp.sum(small_total * small_total) + jnp.sum(forget_total * forget_total)
    )
    clip_factor = 1.0 / jnp.maximum(grad_norm, 1.0)
    qkvo_new, qkvo_m, qkvo_v = adam_update(
        qkvo_weight, qkvo_shard * clip_factor, qkvo_mean, qkvo_square, rate_dense, decay_dense
    )
    proj_new, proj_m, proj_v = adam_update(
        proj_weight, proj_shard * clip_factor, proj_mean, proj_square, rate_proj, decay_dense
    )
    gateup_new, gateup_m, gateup_v = adam_update(
        gateup_weight,
        gateup_shard * clip_factor,
        gateup_mean,
        gateup_square,
        rate_dense,
        decay_dense,
    )
    down_new, down_m, down_v = adam_update(
        down_weight, down_shard * clip_factor, down_mean, down_square, rate_dense, decay_dense
    )
    forget_new, forget_m, forget_v = adam_update(
        forget_weight,
        forget_total * clip_factor,
        forget_mean,
        forget_square,
        rate_dense,
        decay_dense,
    )
    params_new, params_m, params_v = adam_update(
        norm_params, small_total * clip_factor, params_mean, params_square, rate_small, 0.0
    )
    return (
        block_output,
        input_grad,
        grad_norm,
        qkvo_new,
        qkvo_m,
        qkvo_v,
        proj_new,
        proj_m,
        proj_v,
        gateup_new,
        gateup_m,
        gateup_v,
        down_new,
        down_m,
        down_v,
        forget_new,
        forget_m,
        forget_v,
        params_new,
        params_m,
        params_v,
    )


QB = 256
HEADS = 3
HW = HEADS * HD
PAD = 256
SEQ = 1024
LOW = jnp.bfloat16
F32 = jnp.float32
scale_dot = HD**-0.5
DEV = pl.DeviceIdType.MESH
ANY = pl.BlockSpec(memory_space=pl.ANY)
VM = pl.BlockSpec(memory_space=pltpu.VMEM)
SM = pl.BlockSpec(memory_space=pltpu.SMEM)
DMA = pltpu.SemaphoreType.DMA
PAIRS = ((0, 0), (0, 1), (0, 2), (1, 0), (1, 1), (2, 0))


def shape_of(shape, dtype=F32):
    return jax.ShapeDtypeStruct(shape, dtype)


def dot_nt(a, b):
    return lax.dot_general(a, b, (((1,), (1,)), ((), ())), preferred_element_type=F32)


def dot_tn(a, b):
    return lax.dot_general(a, b, (((0,), (0,)), ((), ())), preferred_element_type=F32)


def dot_nn(a, b):
    return jnp.dot(a, b, preferred_element_type=F32)


def place():
    return tuple(lax.axis_index(a) for a in ("z", "x", "y", "c"))


def other(index, differs):
    return 1 - index if differs else index


def group_peer(d, x, y, c):
    px, py, pc = other(x, d & 4), other(y, d & 2), other(c, d & 1)
    return {"x": px, "y": py, "c": pc}, px * 4 + py * 2 + pc


def greet(z, x, y, c, column=False, line=False, plane=False):
    barrier = pltpu.get_barrier_semaphore()

    def signal(peer):
        pl.semaphore_signal(barrier, inc=1, device_id=peer, device_id_type=DEV)

    for d in range(1, 8):
        signal(group_peer(d, x, y, c)[0])
    count = 7
    if column:
        away = z // 2 - c
        count = count + 1 + away * away
        for r in range(2):
            pl.when(jnp.logical_not((away == 0) & (2 * c + r == z)))(
                functools.partial(signal, {"z": 2 * c + r, "c": z // 2})
            )
    if line:
        count = count + 1 + z * (3 - z) // 2
        pl.when(z < 3)(functools.partial(signal, {"z": z + 1}))
        pl.when(z > 0)(functools.partial(signal, {"z": z - 1}))
    if plane:
        count = count + 3
        for d in range(1, 4):
            signal({"z": lax.rem(z + d, 4)})
    pl.semaphore_wait(barrier, count)


def remote(src, dst, send_sem, recv_sem, peer):
    return pltpu.make_async_remote_copy(
        src_ref=src, dst_ref=dst, send_sem=send_sem, recv_sem=recv_sem, device_id=peer, device_id_type=DEV
    )


VMEM_BYTES = 63 * 1024 * 1024


def comm_params(collective_id):
    return pltpu.CompilerParams(collective_id=collective_id, has_side_effects=True, vmem_limit_bytes=VMEM_BYTES)


def swap_start(src, dst, send_sem, recv_sem, local_sem, x, y, c):
    me = x * 4 + y * 2 + c
    own = pltpu.make_async_copy(src.at[me], dst.at[me], local_sem)
    own.start()
    copies = []
    for d in (4, 2, 6, 5, 3, 7, 1):
        peer, number = group_peer(d, x, y, c)
        copy = remote(src.at[number], dst.at[me], send_sem.at[d], recv_sem.at[d], peer)
        copy.start()
        copies.append(copy)
    return own, copies


def swap_wait(started):
    own, copies = started
    own.wait()
    for copy in copies:
        copy.wait()


def swap_sems():
    return [DMA((8,)), DMA((8,)), DMA]


def column_start(src, dst, send, recv, local, z, c):
    slot = lax.rem(z, 2)
    for r in range(2):
        keep = (z // 2 == c) & (2 * c + r == z)

        @pl.when(keep)
        def _():
            pltpu.make_async_copy(src.at[r], dst.at[slot], local).start()

        @pl.when(jnp.logical_not(keep))
        def _():
            peer = {"z": 2 * c + r, "c": z // 2}
            remote(src.at[r], dst.at[slot], send.at[r], recv.at[slot], peer).start()


def column_wait(src, dst, send, recv, local, z, c):
    slot = lax.rem(z, 2)
    for r in range(2):
        keep = (z // 2 == c) & (2 * c + r == z)
        peer = {"z": 2 * c + r, "c": z // 2}

        @pl.when(keep)
        def _():
            pltpu.make_async_copy(src.at[r], dst.at[slot], local).wait()

        @pl.when(jnp.logical_not(keep))
        def _():
            remote(src.at[r], dst.at[slot], send.at[r], recv.at[slot], peer).wait_send()
            remote(src.at[r], dst.at[r], send.at[r], recv.at[r], peer).wait_recv()


def column_sems():
    return [DMA((2,)), DMA((2,)), DMA]


class LineGather:
    def __init__(self, own_at, dst_at, chunks, sems, z):
        self.own_at, self.dst_at, self.chunks, self.z = own_at, dst_at, chunks, z
        self.sems = sems

    def copy(self, k, h, up):
        send, recv = self.sems[0:2] if up else self.sems[2:4]
        block = self.z - k if up else self.z + k
        src = self.own_at(h) if k == 0 else self.dst_at(block, h)
        n = k * self.chunks + h
        peer = {"z": self.z + 1 if up else self.z - 1}
        return remote(src, self.dst_at(block, h), send.at[n], recv.at[n], peer)

    def cases(self, k, up):
        z = self.z
        if up:
            return (z < 3) & (z >= k), z >= k + 1
        return (z > 0) & (z + k <= 3), z + k + 1 <= 3

    def send(self, k):
        for h in range(self.chunks):
            for up in (True, False):
                if k > 0:
                    self.wait_one(k - 1, h, up)

                @pl.when(self.cases(k, up)[0])
                def _():
                    self.copy(k, h, up).start()

    def wait_one(self, k, h, up):
        @pl.when(self.cases(k, up)[1])
        def _():
            self.copy(k, h, up).wait_recv()

    def finish(self):
        for h in range(self.chunks):
            for up in (True, False):
                self.wait_one(2, h, up)
        for k in range(3):
            for h in range(self.chunks):
                for up in (True, False):

                    @pl.when(self.cases(k, up)[0])
                    def _():
                        self.copy(k, h, up).wait_send()


def line_sems(chunks):
    return [DMA((3 * chunks,))] * 4


class LineReduce:
    def __init__(self, part, chunk, chunks, land_up, land_down, sems, z):
        self.part, self.chunk, self.chunks, self.z = part, chunk, chunks, z
        self.lands = {True: land_up, False: land_down}
        self.sems = {True: sems[0:2], False: sems[2:4]}

    def copy(self, m, h, up):
        dest = 3 - m if up else m
        send, recv = self.sems[up]
        n = m * self.chunks + h
        peer = {"z": self.z + 1 if up else self.z - 1}
        land = self.lands[up].at[(m, *self.chunk(h))]
        return remote(self.part.at[(dest, *self.chunk(h))], land, send.at[n], recv.at[n], peer)

    def add(self, m, h, up):
        dest = 3 - m if up else m
        at = self.chunk(h)
        here, come = (dest, *at), (m, *at)
        total = self.part[here].astype(F32) + self.lands[up][come].astype(F32)
        self.part[here] = total.astype(LOW)

    def begin(self, m):
        for up in (True, False):

            @pl.when(self.z == (0 if up else 3))
            def _():
                for h in range(self.chunks):
                    self.copy(m, h, up).start()

    def phase(self, p, chunks=None):
        chunks = range(self.chunks) if chunks is None else chunks
        if p == 0:
            for m in range(3):
                self.begin(m)
            return
        for m in range(3):
            for hops in range(1, 4 - m):
                if p != hops + m:
                    continue
                for up in (True, False):

                    @pl.when(self.z == (hops if up else 3 - hops))
                    def _():
                        for h in chunks:
                            self.copy(m, h, up).wait_recv()
                            self.add(m, h, up)
                            if hops < 3 - m:
                                self.copy(m, h, up).start()

    def finish(self):
        for m in range(3):
            for h in range(self.chunks):
                for up in (True, False):
                    dest = 3 - m if up else m

                    @pl.when(self.z < dest if up else self.z > dest)
                    def _():
                        self.copy(m, h, up).wait_send()


class Gather:
    def __init__(self, src_at, dst_at, sems, x, y, c):
        send_x, recv_x, send_y, recv_y, send_c, recv_c, local = sems
        ox, oy = 1 - x, 1 - y
        xp, yp, cp = {"x": ox}, {"y": oy}, {"c": 1 - c}

        def own(j, send, recv, peer):
            return remote(src_at(j), dst_at(x, y, c, j), send.at[j], recv.at[j], peer)

        def onward(px, py, j, k, send, recv, peer):
            block = dst_at(px, py, c, j)
            return remote(block, block, send.at[k], recv.at[k], peer)

        self.x = [own(j, send_x, recv_x, xp) for j in range(2)]
        self.y = [own(j, send_y, recv_y, yp) for j in range(2)]
        self.c = [own(j, send_c, recv_c, cp) for j in range(2)]
        self.local = [pltpu.make_async_copy(src_at(j), dst_at(x, y, c, j), local.at[j]) for j in range(2)]
        self.diag_y = onward(ox, y, 0, 2, send_y, recv_y, yp)
        self.diag_x = onward(x, oy, 1, 2, send_x, recv_x, xp)
        order = ((ox, y, 0), (x, oy, 1), (ox, y, 1), (x, oy, 0), (ox, oy, 0), (ox, oy, 1))
        self.pass_c = [onward(*p, k + 2, send_c, recv_c, cp) for k, p in enumerate(order)]

    def start(self):
        for copy in (self.x[0], self.y[1], self.x[1], self.y[0], self.c[0], self.c[1], *self.local):
            copy.start()

    def forward(self):
        self.x[0].wait_recv()
        self.diag_y.start()
        self.pass_c[0].start()
        self.y[1].wait_recv()
        self.diag_x.start()
        self.pass_c[1].start()

    def forward_rest(self):
        self.x[1].wait_recv()
        self.pass_c[2].start()
        self.y[0].wait_recv()
        self.pass_c[3].start()

    def finish(self):
        self.diag_y.wait_recv()
        self.pass_c[4].start()
        self.diag_x.wait_recv()
        self.pass_c[5].start()
        for copy in (*self.x, *self.y, *self.c, self.diag_x, self.diag_y, *self.pass_c):
            copy.wait_send()
        for copy in (*self.c, *self.pass_c):
            copy.wait_recv()
        for copy in self.local:
            copy.wait()


def gather_sems():
    return [DMA((3,)), DMA((3,)), DMA((3,)), DMA((3,)), DMA((8,)), DMA((8,)), DMA((2,))]


def natural(ref):
    return lambda x, y, c, j: ref.at[y, c, j, x]


class Scatter:
    def __init__(self, product, bufs, sems, x, y, c):
        self.product, self.own_c = product, c
        self.to_core, self.from_core, self.to_x, self.from_x, self.to_y, self.from_y, self.kept = bufs
        send_c, recv_c, send_x, recv_x, send_y, recv_y = sems
        ox, oy = 1 - x, 1 - y
        xp, yp, cp = {"x": ox}, {"y": oy}, {"c": 1 - c}
        self.places = ((ox, oy), (ox, y), (x, oy), (x, y))

        def copies(src, dst, send, recv, peer, count):
            return [remote(src.at[k], dst.at[k], send.at[k], recv.at[k], peer) for k in range(count)]

        self.c = [
            remote(self.to_core.at[k % 2], self.from_core.at[k], send_c.at[k], recv_c.at[k], cp) for k in range(4)
        ]
        self.x = copies(self.to_x, self.from_x, send_x, recv_x, xp, 3)
        self.y = copies(self.to_y, self.from_y, send_y, recv_y, yp, 3)

    def to_partner(self, k):
        if k >= 2:
            self.c[k - 2].wait_send()
        self.to_core[k % 2] = self.product(*self.places[k], 1 - self.own_c).astype(LOW)
        self.c[k].start()

    def summed(self, k):
        own = self.product(*self.places[k], self.own_c)
        self.c[k].wait_recv()
        return own + self.from_core[k].astype(F32)

    def close(self, k):
        total = self.summed(k)
        if k == 0:
            self.to_x[0] = total[0].astype(LOW)
            self.x[0].start()
            self.to_y[0] = total[1].astype(LOW)
            self.y[0].start()
        elif k == 1:
            self.to_x[1] = total[0].astype(LOW)
            self.x[1].start()
            self.kept[0] = total[1]
        elif k == 2:
            self.to_y[1] = total[1].astype(LOW)
            self.y[1].start()
            self.kept[1] = total[0]
        else:
            self.y[0].wait_recv()
            self.to_x[2] = (self.kept[0] + self.from_y[0].astype(F32)).astype(LOW)
            self.x[2].start()
            self.x[0].wait_recv()
            self.to_y[2] = (self.kept[1] + self.from_x[0].astype(F32)).astype(LOW)
            self.y[2].start()
            self.kept[0], self.kept[1] = total[0], total[1]

    def stage(self, k):
        if k < 4:
            self.to_partner(k)
        if k > 0:
            self.close(k - 1)

    def result(self):
        self.x[1].wait_recv()
        first = self.kept[0] + self.from_x[1].astype(F32)
        self.y[1].wait_recv()
        second = self.kept[1] + self.from_y[1].astype(F32)
        self.y[2].wait_recv()
        first = first + self.from_y[2].astype(F32)
        self.x[2].wait_recv()
        second = second + self.from_x[2].astype(F32)
        for copy in (*self.c[2:], *self.x, *self.y):
            copy.wait_send()
        return first, second


def scatter_scratch(rows, width):
    return (
        [pltpu.VMEM((2, 2, rows, width), LOW), pltpu.VMEM((4, 2, rows, width), LOW)]
        + [pltpu.VMEM((3, rows, width), LOW)] * 4
        + [pltpu.VMEM((2, rows, width), F32)]
    )


def scatter_sems():
    return [DMA((4,)), DMA((4,)), DMA((3,)), DMA((3,)), DMA((3,)), DMA((3,))]


def exchange_start(in_ref, zbuf, sems, z):
    send, recv = sems
    zbuf[pl.ds(z, 1)] = in_ref[...][None]
    copies = []
    for i in range(3):
        copies.append(remote(in_ref, zbuf.at[z], send.at[i], recv.at[i], {"z": lax.rem(z + i + 1, 4)}))
        copies[i].start()
    return copies


def exchange_end(copies, zbuf, zsum, gbuf, sems, x, y, c):
    send, recv = sems
    me = x * 4 + y * 2 + c
    for copy in copies:
        copy.wait()
    zsum[...] = zbuf[0] + zbuf[1] + zbuf[2] + zbuf[3]
    gbuf[pl.ds(me, 1)] = zsum[...][None]
    copies = []
    for i in range(7):
        peer = group_peer(i + 1, x, y, c)[0]
        copies.append(remote(zsum, gbuf.at[me], send.at[i], recv.at[i], peer))
        copies[i].start()
    for copy in copies:
        copy.wait()


def exchange_total(in_ref, zbuf, zsum, gbuf, sems, z, x, y, c):
    copies = exchange_start(in_ref, zbuf, sems[0:2], z)
    exchange_end(copies, zbuf, zsum, gbuf, sems[2:4], x, y, c)


def exchange_scratch(rows, width):
    return [pltpu.VMEM((4, rows, width), F32), pltpu.VMEM((rows, width), F32)]


def exchange_sems():
    return [DMA((3,)), DMA((3,)), DMA((7,)), DMA((7,))]


def add_blocks(gbuf, rows):
    total = gbuf[0, rows]
    for i in range(1, 8):
        total = total + gbuf[i, rows]
    return total


def norm_kernel(
    q_part, gu_ref, proj_ref, down_ref, small_ref,
    q_out, gu_out, proj_out, norm_ref, q_swapped, landed, square, zbuf, zsum, gbuf, *sems,
):
    z, x, y, c = place()
    greet(z, x, y, c, plane=True)
    q_swap = swap_start(q_part, q_swapped, *sems[0:3], x, y, c)
    over_z = []
    for i in range(3):
        dest = lax.rem(z + i + 1, 4)
        over_z.append(remote(proj_ref.at[dest], landed.at[i], sems[7].at[i], sems[8].at[i], {"z": dest}))
        over_z[i].start()

    def squares(values):
        return jnp.sum(jnp.sum(values * values, axis=0, keepdims=True), axis=1, keepdims=True)

    sums = squares(add_blocks(small_ref, slice(0, 3)))
    for i in range(8):
        sums = sums + squares(small_ref[i, 3:6])
    shards = squares(down_ref[...].astype(F32))
    for t in range(8):
        grads = gu_ref[t]
        shards = shards + squares(grads.astype(F32))
        for b in range(8):
            column = (b * 8 + t) * 128
            gu_out[:, column : column + 128] = grads[:, b * 128 : b * 128 + 128]
    swap_wait(q_swap)
    for u in range(8):
        shards = shards + squares(q_swapped[u].astype(F32))
    for copy in over_z:
        copy.wait()
    mine = proj_ref[pl.ds(z, 1)][0].astype(F32)
    for i in range(3):
        mine = mine + landed[i].astype(F32)
    proj_out[...] = mine
    shards = shards + squares(mine)
    square[...] = jnp.broadcast_to(shards, (8, 128))
    exchange = exchange_start(square, zbuf, sems[3:5], z)
    half = lanes(2 * HW) < HW
    for u in range(4):
        even, odd = q_swapped[2 * u].astype(F32), q_swapped[2 * u + 1].astype(F32)
        for m in range(2):
            a, b = even[:, 2 * HW * m : 2 * HW * (m + 1)], odd[:, 2 * HW * m : 2 * HW * (m + 1)]
            first = jnp.where(half, a, pltpu.roll(b, HW, 1)).astype(LOW)
            second = jnp.where(half, pltpu.roll(a, HW, 1), b).astype(LOW)
            column = 2 * m * D + 2 * HW * u
            q_out[:, column : column + 2 * HW] = first
            q_out[:, column + D : column + D + 2 * HW] = second
    exchange_end(exchange, zbuf, zsum, gbuf, sems[5:7], x, y, c)
    norm_ref[...] = jnp.sqrt(add_blocks(gbuf, slice(0, 8)) + sums)


def norm_layer(q_part, gu_part, proj_part, down_shard, small, collective_id):
    return pl.pallas_call(
        norm_kernel,
        out_shape=[shape_of((48, 4 * D), LOW), shape_of((48, 2 * FF), LOW), shape_of((48, D)), shape_of((8, 128))],
        in_specs=[ANY] + [VM] * 4,
        out_specs=[VM] * 4,
        scratch_shapes=[
            pltpu.VMEM((8, 48, 4 * HW), LOW), pltpu.VMEM((3, 48, D), LOW), pltpu.VMEM((8, 128), F32)
        ]
        + exchange_scratch(8, 128) + [pltpu.VMEM((8, 8, 128), F32)]
        + swap_sems() + exchange_sems() + [DMA((3,)), DMA((3,))],
        compiler_params=comm_params(collective_id),
        name="norm_layer",
    )(q_part, gu_part, proj_part, down_shard, small)


ADAM_STEP = 512


def adam_kernel(rates, norm_ref, small_ref, grad_ref, out_ref, *refs):
    count = len(rates)
    grads, refs = refs[:count], refs[count:]
    olds, refs = refs[: 3 * count], refs[3 * count :]
    few, refs = refs[:6], refs[6:]
    grad_wide, out_copy, refs = refs[0], refs[1], refs[2:]
    news, refs = refs[: 3 * count], refs[3 * count :]
    few_new, refs = refs[:6], refs[6:]
    grad_bufs, refs = refs[:count], refs[count:]
    bufs, refs = refs[: 3 * count], refs[3 * count :]
    grad_sem, in_sem, out_sem = refs
    loads = [pltpu.make_async_copy(grads[i], grad_bufs[i], grad_sem.at[i]) for i in range(count)]
    reads = [pltpu.make_async_copy(olds[i], bufs[i], in_sem.at[i]) for i in range(3 * count)]
    writes = [pltpu.make_async_copy(bufs[i], news[i], out_sem.at[i]) for i in range(3 * count)]
    for i in range(count):
        loads[i].start()
        for k in range(3):
            reads[3 * i + k].start()
    clip = 1.0 / jnp.maximum(norm_ref[:1, :1], 1.0)
    for i in range(count):
        loads[i].wait()
        for k in range(3):
            reads[3 * i + k].wait()
        w_ref, m_ref, v_ref = bufs[3 * i : 3 * i + 3]

        @pl.loop(0, w_ref.shape[1] // ADAM_STEP)
        def _(n):
            at = (slice(None), pl.ds(pl.multiple_of(n * ADAM_STEP, ADAM_STEP), ADAM_STEP))
            gradient = grad_bufs[i][at].astype(F32) * clip
            w_ref[at], m_ref[at], v_ref[at] = adam_update(
                w_ref[at], gradient, m_ref[at], v_ref[at], rates[i], decay_dense
            )

        for k in range(3):
            writes[3 * i + k].start()
    grad_wide[...] = grad_ref[...].astype(F32)
    out_copy[...] = out_ref[...]
    for t in range(8):
        for h in range(HEADS):
            at = slice(t * HEADS + h, t * HEADS + h + 1)
            updated = adam_update(
                few[0][at], small_ref[t, 3 + h : 4 + h] * clip, few[1][at], few[2][at], rate_dense, decay_dense
            )
            for k in range(3):
                few_new[k][at] = updated[k]
    small = add_blocks(small_ref, slice(0, 3))
    small = jnp.concatenate([small[0:1], small[1:2], small[2:3]], axis=1)[:, : few[3].shape[1]]
    updated = adam_update(few[3][...], small * clip, few[4][...], few[5][...], rate_small, 0.0)
    for k in range(3):
        few_new[3 + k][...] = updated[k]
    for write in writes:
        write.wait()


def adam_layer(rates, norm, small, input_grad, block_output, grads, olds, few):
    count = len(rates)
    return pl.pallas_call(
        functools.partial(adam_kernel, rates),
        out_shape=[shape_of(input_grad.shape), shape_of(block_output.shape, LOW)]
        + [shape_of(a.shape) for a in (*olds, *few)],
        in_specs=[VM] * 4 + [ANY] * (4 * count) + [VM] * 6,
        out_specs=[VM, VM] + [ANY] * (3 * count) + [VM] * 6,
        scratch_shapes=[pltpu.VMEM(a.shape, a.dtype) for a in grads]
        + [pltpu.VMEM(a.shape, F32) for a in olds]
        + [DMA((count,)), DMA((3 * count,)), DMA((3 * count,))],
        compiler_params=pltpu.CompilerParams(vmem_limit_bytes=VMEM_BYTES),
        name="adam",
    )(norm, small, input_grad, block_output, *grads, *olds, *few)


def row_scale(values):
    return lax.rsqrt(jnp.mean(values * values, axis=-1, keepdims=True) + eps_norm)


def norm_back(grad, values, gain_vec):
    r = row_scale(values)
    u = grad * gain_vec
    by_values = r * u - values * (r * r * r) * jnp.mean(values * u, axis=-1, keepdims=True)
    return by_values, jnp.sum(grad * values * r, axis=0, keepdims=True)


def open_kernel(
    x_ref, lens_ref, params_ref, forget_ref, wq_ref, wg_ref, wp_ref,
    xo_ref, lo_ref, normed_ref, qkvo_ref, gu_ref, wf_ref, proj_ref,
    normed_own, wq_low, wg_low, wp_low, len_tile, *sems,
):
    z, x, y, c = place()
    t = x * 4 + y * 2 + c
    greet(z, x, y, c, column=True, line=True)
    column_start(x_ref, xo_ref, *sems[0:3], z, c)
    half = lanes(2 * HW) < HW
    for u in range(4):
        for m in range(2):
            column = 2 * m * D + 2 * HW * u
            a, b = wq_ref[:, column : column + 2 * HW], wq_ref[:, column + D : column + D + 2 * HW]
            at = slice(2 * HW * m, 2 * HW * (m + 1))
            wq_low[2 * u, :, at] = jnp.where(half, a, pltpu.roll(b, HW, 1)).astype(LOW)
            wq_low[2 * u + 1, :, at] = jnp.where(half, pltpu.roll(a, HW, 1), b).astype(LOW)
    qkvo_swap = swap_start(wq_low, qkvo_ref.at[z], *sems[3:6], x, y, c)
    row = lax.broadcasted_iota(jnp.int32, (8, 128), 0)
    tile = jnp.where(row == 0, lens_ref[0].astype(F32), lens_ref[1].astype(F32))
    for d in range(8):
        len_tile[d] = tile
    lens = swap_start(len_tile, lo_ref, *sems[6:9], x, y, c)
    wp_low[...] = wp_ref[...].astype(LOW)
    own_proj = pltpu.make_async_copy(wp_low, proj_ref.at[z], sems[9])
    own_proj.start()
    for d in range(8):
        for b in range(8):
            column = (b * 8 + d) * 128
            wg_low[d, :, b * 128 : b * 128 + 128] = wg_ref[:, column : column + 128].astype(LOW)
    proj = LineGather(lambda h: wp_low, lambda k, h: proj_ref.at[k], 1, sems[10:14], z)
    qkvo = LineGather(
        lambda h: qkvo_ref.at[z, 4 * h : 4 * h + 4], lambda k, h: qkvo_ref.at[k, 4 * h : 4 * h + 4], 2,
        sems[14:18], z,
    )
    swap_wait(qkvo_swap)
    qkvo.send(0)
    proj.send(0)
    sub = lax.broadcasted_iota(jnp.int32, (8, D), 0)
    mine = jnp.zeros((8, D), F32)
    for d in range(8):
        for h in range(HEADS):
            mine = jnp.where((sub == h) & (t == d), forget_ref[d * HEADS + h : d * HEADS + h + 1], mine)
    parts = pieces_of(mine)
    wf_ref[...] = columns_of(jnp.concatenate([parts[b] for _, b in PAIRS], axis=0)).astype(LOW)
    column_wait(x_ref, xo_ref, *sems[0:3], z, c)
    for j in range(2):
        rows = xo_ref[j].astype(F32)
        normed_own[j] = (rows * row_scale(rows) * params_ref[:, :D]).astype(LOW)
    normed = Gather(lambda j: normed_own.at[j], natural(normed_ref), sems[18:25], x, y, c)
    normed.start()
    gu_swap = swap_start(wg_low, gu_ref, *sems[25:28], x, y, c)
    qkvo.send(1)
    proj.send(1)
    normed.forward()
    normed.forward_rest()
    qkvo.send(2)
    proj.send(2)
    normed.finish()
    qkvo.finish()
    proj.finish()
    own_proj.wait()
    swap_wait(gu_swap)
    swap_wait(lens)


def open_layer(x, lengths, params, forget, qkvo_weight, gateup_weight, proj_weight, collective_id):
    return pl.pallas_call(
        open_kernel,
        out_shape=[
            shape_of(x.shape, LOW),
            shape_of((8, 8, 128)),
            shape_of((2, 2, 2, 2, 128, D), LOW),
            shape_of((4, 8, 48, 4 * HW), LOW),
            shape_of((8, 48, 1024), LOW),
            shape_of((D, 128), LOW),
            shape_of((4, 48, D), LOW),
        ],
        in_specs=[ANY, SM, VM, VM, VM, VM, VM],
        out_specs=[VM] + [ANY] * 4 + [VM, ANY],
        scratch_shapes=[
            pltpu.VMEM((2, 128, D), LOW), pltpu.VMEM((8, 48, 4 * HW), LOW), pltpu.VMEM((8, 48, 1024), LOW),
            pltpu.VMEM((48, D), LOW), pltpu.VMEM((8, 8, 128), F32),
        ]
        + column_sems() + swap_sems() * 2 + [DMA] + line_sems(1) + line_sems(2) + gather_sems() + swap_sems(),
        compiler_params=comm_params(collective_id),
        name="open_layer",
    )(x, lengths, params, forget, qkvo_weight, gateup_weight, proj_weight)


def length_of(len_ref, z, x, sequence):
    tile = len_ref[pl.ds(x * 4 + sequence * 2 + z // 2, 1)][0]
    row = lax.broadcasted_iota(jnp.int32, (8, 128), 0) == lax.rem(z, 2)
    return jnp.sum(jnp.where(row, tile, 0.0), axis=0, keepdims=True)[:, :1]


def head_gain(params_ref, key):
    both = params_ref[:, 2 * D : 2 * D + 128]
    both = pltpu.roll(both, HD, 1) if key else both
    one = jnp.concatenate([jnp.where(lanes(128) < HD, both, 0.0), jnp.zeros((1, 128), F32)], axis=1)
    return one + pltpu.roll(one, HD, 1) + pltpu.roll(one, 2 * HD, 1)


def lanes(width):
    return lax.broadcasted_iota(jnp.int32, (1, width), 1)


def head_mask(h):
    lane = lanes(PAD)
    return (lane >= h * HD) & (lane < (h + 1) * HD)


def split_halves(pair):
    valid = lanes(PAD) < HW
    first = jnp.where(valid, pair[:, :PAD], 0.0)
    second = jnp.where(valid, pltpu.roll(pair, HW, 1)[:, :PAD], 0.0)
    return first, second


def join_halves(first, second):
    tail = jnp.zeros((first.shape[0], 128), F32)
    first = jnp.concatenate([first, tail], axis=1)
    second = pltpu.roll(jnp.concatenate([second, tail], axis=1), HW, 1)
    return jnp.where(lanes(2 * HW) < HW, first, second)


def head_sums(values):
    row = lax.broadcasted_iota(jnp.int32, (PAD, PAD), 0) // HD
    column = lax.broadcasted_iota(jnp.int32, (PAD, PAD), 1) // HD
    ones = jnp.where(row == column, 1.0, 0.0).astype(LOW)
    high = values.astype(LOW)
    return dot_nn(high, ones) + dot_nn((values - high.astype(F32)).astype(LOW), ones)


def head_scale(values):
    return lax.rsqrt(head_sums(values * values) / HD + eps_norm)


def head_norm_back(grad, values, gain_vec):
    r = head_scale(values)
    u = grad * gain_vec
    by_values = r * u - values * (r * r * r) * (head_sums(values * u) / HD)
    return by_values, jnp.sum(grad * values * r, axis=0, keepdims=True)


def running_sum(rows, backward):
    lane = lanes(SEQ)
    step = 1
    while step < SEQ:
        if backward:
            rows = rows + jnp.where(lane < SEQ - step, pltpu.roll(rows, SEQ - step, 1), 0.0)
        else:
            rows = rows + jnp.where(lane >= step, pltpu.roll(rows, step, 1), 0.0)
        step *= 2
    return rows


def columns_of(rows):
    return jnp.concatenate([rows, jnp.zeros((128 - rows.shape[0], rows.shape[1]), F32)], axis=0).T


def pieces_of(value):
    high = value.astype(LOW).astype(F32)
    middle = (value - high).astype(LOW).astype(F32)
    return high, middle, value - high - middle


def segments(i):
    return (((0, i * QB, False),) if i else ()) + ((i * QB, QB, True),)


def causal(scores):
    query = lax.broadcasted_iota(jnp.int32, (QB, QB), 0)
    key = lax.broadcasted_iota(jnp.int32, (QB, QB), 1)
    return jnp.where(key <= query, scores, neg_large)


EARLY = 2


def forward_kernel(
    params_smem, len_ref, normed_ref, wq_ref, wf_ref, params_ref, wp_ref, wd_ref, gu_ref, ct_ref,
    raw_ref, q_ref, k_ref, v_ref, att_ref, col_ref, crow_ref, logit_ref, mixed_ref, projall_ref,
    down_ref, gu_first_ref, gout_ref, ct_own, wd_low, *sems,
):
    z, x, y, c = place()
    s = pl.program_id(0)
    length = length_of(len_ref, z, x, s)

    def piece(px, py, pc, j):
        return projall_ref.at[2 * j : 2 * j + 2, px * 4 + py * 2 + pc]

    proj = Gather(lambda j: wp_ref.at[2 * j : 2 * j + 2], piece, sems[:7], x, y, c)
    gout = Gather(lambda j: ct_own.at[j], natural(gout_ref), sems[7:14], x, y, c)
    down = LineGather(lambda h: wd_low, lambda k, h: down_ref.at[k], 1, sems[14:18], z)
    gateup = LineGather(lambda h: gu_ref.at[0:EARLY], lambda k, h: gu_first_ref.at[k], 1, sems[18:22], z)
    own_down = pltpu.make_async_copy(wd_low, down_ref.at[z], sems[22])
    own_gateup = pltpu.make_async_copy(gu_ref.at[0:EARLY], gu_first_ref.at[z], sems[23])

    def begin():
        greet(z, x, y, c, column=True, line=True)
        column_start(ct_ref, ct_own, *sems[24:27], z, c)
        proj.start()
        wd_low[...] = wd_ref[...].astype(LOW)
        own_down.start()
        own_gateup.start()

    def turn():
        column_wait(ct_ref, ct_own, *sems[24:27], z, c)
        own_length = length_of(len_ref, z, x, y)
        for j in range(2):
            position = (2 * (2 * c + j) + x) * 128 + lax.broadcasted_iota(jnp.int32, (128, 1), 0)
            valid = position.astype(F32) < own_length
            ct_own[j] = jnp.where(valid, ct_own[j].astype(F32), 0.0).astype(LOW)
        gout.start()
        down.send(0)
        gateup.send(0)

    def end():
        gout.finish()
        down.finish()
        gateup.finish()
        own_down.wait()
        own_gateup.wait()

    hooks = {
        (0, 0): begin, (0, 2): proj.forward, (0, 8): proj.forward_rest, (0, 10): turn, (0, 15): proj.finish,
        (1, 1): lambda: down.send(1), (1, 2): gout.forward, (1, 4): lambda: gateup.send(1),
        (1, 8): gout.forward_rest, (1, 10): lambda: down.send(2), (1, 13): lambda: gateup.send(2), (1, 15): end,
    }

    def hook(n):
        for step in range(2):
            if (step, n) in hooks:
                pl.when(s == step)(hooks[step, n])

    hook(0)
    normed = normed_ref[0]
    raw = dot_nn(normed, wq_ref[...])
    raw_ref[0] = raw
    hook(1)
    q_raw, k_raw = split_halves(raw[:, : 2 * HW])
    v, gate = split_halves(raw[:, 2 * HW :])
    q = (q_raw * head_scale(q_raw) * head_gain(params_ref, False)).astype(LOW) * jnp.asarray(scale_dot, LOW)
    k = (k_raw * head_scale(k_raw) * head_gain(params_ref, True)).astype(LOW)
    v = v.astype(LOW)
    q_ref[0], k_ref[0], v_ref[0] = q, k, v
    pieces = dot_nn(normed, wf_ref[...]).T
    sub = lax.broadcasted_iota(jnp.int32, (8, 1), 0)
    bias = jnp.zeros((8, 1), F32)
    for h in range(HEADS):
        first_bias = 2 * D + 2 * HD + (x * 4 + y * 2 + c) * HEADS
        bias = jnp.where(sub == h, params_smem[first_bias + h], bias)
    logits = pieces[0:8] + pieces[8:16] + pieces[16:24] + bias
    logit_ref[0] = logits
    log_forget = jnp.minimum(logits, 0.0) - jnp.log1p(jnp.exp(-jnp.abs(logits)))
    inside = lanes(SEQ).astype(F32) < length
    crow = jnp.where(inside, running_sum(log_forget, False), -neg_large)
    crow_ref[0] = crow
    hook(2)
    for i in range(SEQ // QB):
        rows = slice(i * QB, (i + 1) * QB)
        att = jnp.zeros((QB, PAD), F32)
        for h in range(HEADS):
            mh = head_mask(h)
            qh = jnp.where(mh, q[rows], jnp.zeros((), LOW))
            parts = []
            for start, count, own in segments(i):
                keys = slice(start, start + count)
                scores = dot_nt(qh, k[keys]) - crow[h : h + 1, keys]
                parts.append((keys, causal(scores) if own else scores))
            tops = [jnp.max(scores, axis=-1, keepdims=True) for _, scores in parts]
            top = functools.reduce(jnp.maximum, tops)
            total = jnp.zeros((QB, 1), F32)
            out = jnp.zeros((QB, PAD), F32)
            for keys, scores in parts:
                p = jnp.exp(scores - top)
                total = total + jnp.sum(p, axis=-1, keepdims=True)
                out = out + dot_nn(p.astype(LOW), v[keys])
            att = jnp.where(mh, out / total, att)
            col_ref[0, rows, h : h + 1] = -(top + jnp.log(total))
            hook(3 + i * HEADS + h)
        att_ref[0, rows, :] = att
    mixed = att_ref[0] * jax.nn.sigmoid(gate)
    for cc in range(2):
        for xx in range(2):
            first, second = (mixed[(cc * 4 + 2 * j + xx) * 128 :][:128] for j in range(2))
            mixed_ref[xx, 0, cc] = join_halves(first, second).astype(LOW)
    hook(15)


def seq_spec(rows, width, buffers=2):
    return pl.BlockSpec((1, rows, width), lambda s: (s, 0, 0), pipeline_mode=pl.Buffered(buffers))


def packed_spec(buffers=2):
    return pl.BlockSpec(
        (2, 1, 2, 128, 2 * HW), lambda s: (0, s, 0, 0, 0), pipeline_mode=pl.Buffered(buffers)
    )


def attention_forward(params, lens, normed, wq, wf, proj_mine, down_weight, gateup_mine, cotangent, collective_id):
    return pl.pallas_call(
        forward_kernel,
        grid=(2,),
        in_specs=[SM, VM, seq_spec(SEQ, D), VM, VM, VM, ANY, VM, ANY, ANY],
        out_specs=[seq_spec(SEQ, 4 * HW)]
        + [seq_spec(SEQ, PAD)] * 4
        + [seq_spec(SEQ, 8), seq_spec(8, SEQ), seq_spec(8, SEQ), packed_spec()]
        + [ANY] * 4,
        out_shape=[shape_of((2, SEQ, 4 * HW))]
        + [shape_of((2, SEQ, PAD), LOW)] * 3
        + [shape_of((2, SEQ, PAD))]
        + [shape_of((2, SEQ, 8))]
        + [shape_of((2, 8, SEQ))] * 2
        + [shape_of((2, 2, 2, 128, 2 * HW), LOW), shape_of((4, 8, 48, D), LOW), shape_of((4, 128, D), LOW)]
        + [shape_of((4, EARLY, 48, 1024), LOW), shape_of((2, 2, 2, 2, 128, D), LOW)],
        scratch_shapes=[pltpu.VMEM((2, 128, D), LOW), pltpu.VMEM((128, D), LOW)]
        + gather_sems() * 2 + line_sems(1) * 2 + [DMA, DMA] + column_sems(),
        compiler_params=comm_params(collective_id),
        name="attention_forward",
    )(params[0], lens, normed, wq, wf, params, proj_mine, down_weight, gateup_mine, cotangent)


def ffn_kernel(
    packed_mixed_ref, proj_any, x_ref, params_ref, gu_mine_ref, gu_first_ref, gout_any, down_any,
    mixed_ref, middle_ref, hidden_ref, gmid_ref, gmid_low_ref, gain_out_ref, swapped_ref, gu_grad_ref, down_grad_ref,
    mixed_swapped, n2_own, n2_ref, gout_ref, down_ref, proj_ref, gu_all, ggu_ref, packed, down_part,
    land_up, land_down, *rest,
):
    bufs, sems = rest[:7], rest[7:]
    z, x, y, c = place()
    loads = [
        pltpu.make_async_copy(proj_any, proj_ref, sems[13].at[0]),
        pltpu.make_async_copy(gu_first_ref, gu_all.at[:, 0:EARLY], sems[13].at[1]),
        pltpu.make_async_copy(gu_mine_ref.at[EARLY:8], gu_all.at[z, EARLY:8], sems[13].at[2]),
        pltpu.make_async_copy(down_any, down_ref, sems[13].at[3]),
        pltpu.make_async_copy(gout_any, gout_ref, sems[13].at[4]),
    ]
    for load in loads:
        load.start()
    greet(z, x, y, c, line=True)
    mixed_swap = swap_start(packed_mixed_ref, mixed_swapped, *sems[14:17], x, y, c)
    line = LineGather(
        lambda h: gu_mine_ref.at[EARLY:8], lambda k, h: gu_all.at[k, EARLY:8], 1, sems[17:21], z
    )
    line.send(0)
    swap_wait(mixed_swap)
    half = lanes(2 * HW) < HW
    for u in range(4):
        even, odd = mixed_swapped[2 * u].astype(F32), mixed_swapped[2 * u + 1].astype(F32)
        columns = slice(2 * HW * u, 2 * HW * (u + 1))
        mixed_ref[0, :, columns] = jnp.where(half, even, pltpu.roll(odd, HW, 1)).astype(LOW)
        mixed_ref[1, :, columns] = jnp.where(half, pltpu.roll(even, HW, 1), odd).astype(LOW)
    loads[0].wait()
    middle = dot_nn(mixed_ref[...].reshape(256, D), proj_ref[...]) + x_ref[...].reshape(256, D).astype(F32)
    middle_ref[...] = middle.reshape(2, 128, D)
    n2_own[...] = (middle * row_scale(middle) * params_ref[:, D : 2 * D]).astype(LOW).reshape(2, 128, D)
    gather = Gather(lambda j: n2_own.at[j], natural(n2_ref), sems[21:28], x, y, c)
    gather.start()
    line.send(1)
    gather.forward()
    line.send(2)
    gather.forward_rest()
    gather.finish()
    line.finish()
    for load in loads[1:]:
        load.wait()
    down_grads = LineReduce(down_part, lambda h: (), 1, land_up, land_down, sems[9:13], z)
    gu_ref = gu_all
    def product(px, py, pc):
        rows = n2_ref[py, pc, :, px].reshape(256, D)
        gateup = dot_nn(rows, gu_ref[...].reshape(D, 1024))
        gate, up = gateup[:, :512], gateup[:, 512:]
        s = jax.nn.sigmoid(gate)
        silu = gate * s
        hidden_ref[py, pc, :, px] = (silu * up).astype(LOW).reshape(2, 128, 512)
        grad_hidden = dot_nt(gout_ref[py, pc, :, px].reshape(256, D), down_ref[...])
        by_gate = grad_hidden * up * (s + silu * (1.0 - s))
        grads = jnp.concatenate([by_gate, grad_hidden * silu], axis=1).astype(LOW)
        ggu_ref[py, pc, :, px] = grads.reshape(2, 128, 1024)
        return dot_nt(grads, gu_ref[...].reshape(D, 1024)).reshape(2, 128, D)

    scatter = Scatter(product, bufs, sems[:6], x, y, c)
    for k in range(4):
        scatter.to_partner(k)
        scatter.close(k)
    tokens = 2 * SEQ
    for d in (3, 0, 2, 1):
        columns = hidden_ref[:, :, :, :, :, d * 128 : d * 128 + 128].reshape(tokens, 128)
        down_part[d] = dot_tn(columns, gout_ref[...].reshape(tokens, D)).astype(LOW)
    down_grads.phase(0)

    halves = scatter.result()
    down_grads.phase(1)
    gain_grad = jnp.zeros((1, D), F32)
    for j in range(2):
        by_middle, by_gain = norm_back(halves[j], middle_ref[j], params_ref[:, D : 2 * D])
        gain_grad = gain_grad + by_gain
        grad = gout_ref[y, c, j, x].astype(F32) + by_middle
        gmid_ref[j] = grad
        gmid_low_ref[j] = grad.astype(LOW)
    gain_out_ref[...] = gain_grad
    down_grads.phase(2)
    mixed = dot_nt(gmid_low_ref[...].reshape(256, D), proj_ref[...])
    for u in range(4):
        columns = slice(2 * HW * u, 2 * HW * (u + 1))
        a0, a1 = mixed[:128, columns], mixed[128:, columns]
        packed[2 * u] = jnp.where(half, a0, pltpu.roll(a1, HW, 1)).astype(LOW)
        packed[2 * u + 1] = jnp.where(half, pltpu.roll(a0, HW, 1), a1).astype(LOW)
    swapping = swap_start(packed, swapped_ref, *sems[6:9], x, y, c)
    for d in range(4):
        rows = n2_ref[:, :, :, :, :, d * 384 : d * 384 + 384].reshape(tokens, 384)
        grads = dot_tn(rows, ggu_ref[...].reshape(tokens, 1024))
        gu_grad_ref[d] = grads.astype(LOW).reshape(8, 48, 1024)
    down_grads.phase(3)
    swap_wait(swapping)
    down_grads.finish()
    down_grad_ref[...] = down_part[pl.ds(z, 1)][0]


def ffn_layer(packed_mixed, proj_full, x, params, gateup_mine, gu_first, gout, down_t, collective_id):
    return pl.pallas_call(
        ffn_kernel,
        out_shape=[
            shape_of((2, 128, D), LOW),
            shape_of((2, 128, D)),
            shape_of((2, 2, 2, 2, 128, 512), LOW),
            shape_of((2, 128, D)),
            shape_of((2, 128, D), LOW),
            shape_of((1, D)),
            shape_of((8, 128, 2 * HW), LOW),
            shape_of((4, 8, 48, 1024), LOW),
            shape_of((128, D), LOW),
        ],
        in_specs=[ANY, ANY, VM, VM] + [ANY] * 4,
        out_specs=[VM] * 6 + [ANY] + [VM] * 2,
        scratch_shapes=[
            pltpu.VMEM((8, 128, 2 * HW), LOW), pltpu.VMEM((2, 128, D), LOW),
            pltpu.VMEM((2, 2, 2, 2, 128, D), LOW), pltpu.VMEM((2, 2, 2, 2, 128, D), LOW),
            pltpu.VMEM((512, D), LOW), pltpu.VMEM((D, D), LOW), pltpu.VMEM((4, 8, 48, 1024), LOW),
            pltpu.VMEM((2, 2, 2, 2, 128, 1024), LOW), pltpu.VMEM((8, 128, 2 * HW), LOW),
            pltpu.VMEM((4, 128, D), LOW), pltpu.VMEM((3, 128, D), LOW), pltpu.VMEM((3, 128, D), LOW),
        ]
        + scatter_scratch(128, D) + scatter_sems() + swap_sems() + line_sems(1) + [DMA((5,))]
        + swap_sems() + line_sems(1) + gather_sems(),
        compiler_params=comm_params(collective_id),
        name="ffn_layer",
    )(packed_mixed, proj_full, x, params, gateup_mine, gu_first, gout, down_t)


def backward_kernel(
    gmix_ref, raw_ref, q_ref, k_ref, v_ref, att_ref, col_ref, crow_ref, logit_ref,
    params_ref, hidden_ref, down_ref, middle_ref, gu_grad_ref, mixed_ref, gmid_low_ref,
    gp_ref, gains_ref, bias_ref, result_ref, gu_out_ref, proj_out_ref,
    do, dq, dk, dv, grow, gcol, gu_part, land_up, land_down, proj_part, *rest,
):
    bufs, more, sems = rest[:7], rest[7:14], rest[14:]
    z, x, y, c = place()
    s = pl.program_id(0)

    def product(px, py, pc):
        return dot_nn(hidden_ref[py, pc, :, px].reshape(256, 512), down_ref[...]).reshape(2, 128, D)

    def proj_product(px, py, pc):
        return proj_part[:, px * 4 + py * 2 + pc].reshape(2, 96, D).astype(F32)

    output = Scatter(product, bufs, sems[0:6], x, y, c)
    proj = Scatter(proj_product, more, sems[6:12], x, y, c)
    gu_grads = LineReduce(gu_part, lambda h: (slice(4 * h, 4 * h + 4),), 2, land_up, land_down, sems[12:16], z)
    load = pltpu.make_async_copy(gu_grad_ref, gu_part, sems[16])
    store = pltpu.make_async_copy(gu_part.at[z], gu_out_ref, sems[16])
    def begin():
        load.start()
        greet(z, x, y, c, line=True)
        load.wait()
        gu_grads.phase(0)
        for d in range(4):
            columns = mixed_ref[:, :, d * 384 : d * 384 + 384].reshape(256, 384)
            grads = dot_tn(columns, gmid_low_ref[...].reshape(256, D))
            proj_part[d] = grads.astype(LOW).reshape(8, 48, D)
        proj.stage(0)

    def proj_end():
        first, second = proj.result()
        proj_out_ref[0:2] = first.astype(LOW).reshape(2, 48, D)
        proj_out_ref[2:4] = second.astype(LOW).reshape(2, 48, D)

    def end():
        first, second = output.result()
        for j, half in enumerate((first, second)):
            result_ref[j] = (middle_ref[j] + half).astype(LOW)
        gu_grads.phase(3)
        store.start()
        gu_grads.finish()
        store.wait()

    hooks = {
        (0, 0): begin, (0, 1): lambda: proj.stage(1), (0, 2): lambda: proj.stage(2), (0, 3): lambda: proj.stage(3),
        (0, 4): lambda: output.stage(0), (0, 5): lambda: output.stage(1), (0, 6): lambda: gu_grads.phase(1, (0,)),
        (0, 7): lambda: proj.stage(4), (0, 8): lambda: output.stage(2), (0, 9): lambda: output.stage(3),
        (0, 11): lambda: gu_grads.phase(1, (1,)), (0, 13): proj_end,
        (1, 1): lambda: gu_grads.phase(2, (0,)), (1, 3): lambda: output.stage(4),
        (1, 6): lambda: gu_grads.phase(2, (1,)), (1, 13): end,
    }

    def hook(n):
        for step in range(2):
            if (step, n) in hooks:
                pl.when(s == step)(hooks[step, n])

    hook(0)
    for cc in range(2):
        for xx in range(2):
            halves = split_halves(gmix_ref[xx, 0, cc].astype(F32))
            for j in range(2):
                dq[pl.ds((cc * 4 + 2 * j + xx) * 128, 128)] = halves[j]
    _, gate = split_halves(raw_ref[0, :, 2 * HW :])
    gate = jax.nn.sigmoid(gate)
    do[...] = (dq[...] * gate).astype(LOW)
    grad_gate = dq[...] * att_ref[0] * gate * (1.0 - gate)
    dk[...] = jnp.zeros_like(dk)
    dv[...] = jnp.zeros_like(dv)
    grow[...] = jnp.zeros_like(grow)
    for i in range(SEQ // QB):
        rows = slice(i * QB, (i + 1) * QB)
        q, grad = q_ref[0, rows], do[rows]
        delta_all = head_sums(grad.astype(F32) * att_ref[0, rows])
        grad_q = jnp.zeros((QB, PAD), F32)
        for h in range(HEADS):
            mh = head_mask(h)
            qh = jnp.where(mh, q, jnp.zeros((), LOW))
            gh = jnp.where(mh, grad, jnp.zeros((), LOW))
            delta = delta_all[:, h * HD : h * HD + 1]
            by_query = jnp.zeros((QB, PAD), F32)
            by_row = jnp.zeros((1, QB), F32)
            for start, count, own in segments(i):
                keys = slice(start, start + count)
                k, v = k_ref[0, keys], v_ref[0, keys]
                ones = jnp.ones((8, count), LOW)
                scores = dot_nt(qh, k) - crow_ref[0, h : h + 1, keys] + col_ref[0, rows, h : h + 1]
                p = jnp.exp(causal(scores) if own else scores)
                ds = (p * (dot_nt(gh, v) - delta)).astype(LOW)
                by_query = by_query + dot_nn(ds, k)
                dk[keys] += dot_tn(ds, qh)
                dv[keys] += dot_tn(p.astype(LOW), gh)
                by_row = by_row + dot_nt(ones, ds)[:1]
                grow[h : h + 1, keys] += dot_nn(ones[:, :QB], ds)[:1]
            grad_q = jnp.where(mh, by_query, grad_q)
            gcol[h : h + 1, rows] = by_row
            hook(1 + i * HEADS + h)
        dq[rows] = grad_q * scale_dot
    q_raw, k_raw = split_halves(raw_ref[0, :, : 2 * HW])
    q_grad, q_gain = head_norm_back(dq[...], q_raw, head_gain(params_ref, False))
    k_grad, k_gain = head_norm_back(dk[...], k_raw, head_gain(params_ref, True))
    gp_ref[0, :, : 2 * HW] = join_halves(q_grad, k_grad).astype(LOW)
    gp_ref[0, :, 2 * HW : 4 * HW] = join_halves(dv[...], grad_gate).astype(LOW)
    gains_ref[0] = jnp.concatenate([q_gain, k_gain, jnp.zeros((6, PAD), F32)], axis=0)
    head = lax.broadcasted_iota(jnp.int32, (8, SEQ), 0) < HEADS
    change = jnp.where(head, gcol[...] - grow[...], 0.0)
    logits = logit_ref[0]
    grad_logits = running_sum(change, True) * jax.nn.sigmoid(-logits)
    bias_ref[0] = jnp.broadcast_to(jnp.sum(grad_logits, axis=1, keepdims=True), (8, 128))
    parts = pieces_of(grad_logits)
    gp_ref[0, :, 4 * HW :] = columns_of(jnp.concatenate([parts[a] for a, _ in PAIRS], axis=0)).astype(LOW)
    hook(13)


def attention_backward(
    gmix, raw, q, k, v, att, col, crow, logits, params, hidden, down_t, middle, gu_grad,
    mixed, gmid_low, collective_id,
):
    return pl.pallas_call(
        backward_kernel,
        grid=(2,),
        in_specs=[packed_spec(1), seq_spec(SEQ, 4 * HW, 1)]
        + [seq_spec(SEQ, PAD, 1)] * 4
        + [seq_spec(SEQ, 8, 1), seq_spec(8, SEQ), seq_spec(8, SEQ)]
        + [VM, VM, VM, VM, ANY, VM, VM],
        out_specs=[seq_spec(SEQ, 4 * HW + 128, 1), seq_spec(8, PAD), seq_spec(8, 128), VM, ANY, VM],
        scratch_shapes=[pltpu.VMEM((SEQ, PAD), LOW)]
        + [pltpu.VMEM((SEQ, PAD), F32)] * 3
        + [pltpu.VMEM((8, SEQ), F32)] * 2
        + [pltpu.VMEM((4, 8, 48, 1024), LOW)]
        + [pltpu.VMEM((3, 8, 48, 1024), LOW)] * 2
        + [pltpu.VMEM((4, 8, 48, D), LOW)]
        + scatter_scratch(128, D) + scatter_scratch(96, D)
        + scatter_sems() * 2 + line_sems(2) + [DMA],
        out_shape=[
            shape_of((2, SEQ, 4 * HW + 128), LOW), shape_of((2, 8, PAD)), shape_of((2, 8, 128)),
            shape_of((2, 128, D), LOW), shape_of((8, 48, 1024), LOW), shape_of((4, 48, D), LOW),
        ],
        compiler_params=comm_params(collective_id),
        name="attention_backward",
    )(
        gmix, raw, q, k, v, att, col, crow, logits, params, hidden, down_t, middle, gu_grad,
        mixed, gmid_low,
    )


def close_kernel(
    gp_any, normed_any, wq_any, wf_ref, x_ref, params_ref, gmid_ref, gu_ref, result_ref,
    gains_ref, bias_ref, ffn_gain_ref,
    grad_ref, out_ref, small_ref, q_out_ref, gu_out_ref,
    gp_ref, normed_ref, wq_ref, grad_own, q_part, land_up, land_down, forget, small, zbuf, zsum, *rest,
):
    bufs, sems = rest[:7], rest[7:]
    z, x, y, c = place()
    t = x * 4 + y * 2 + c
    loads = [
        pltpu.make_async_copy(gp_any, gp_ref, sems[20].at[0]),
        pltpu.make_async_copy(normed_any, normed_ref, sems[20].at[1]),
        pltpu.make_async_copy(wq_any, wq_ref, sems[20].at[2]),
    ]
    for load in loads:
        load.start()
    greet(z, x, y, c, column=True, line=True, plane=True)
    column_start(result_ref, out_ref, *sems[21:24], z, c)
    tokens = 2 * SEQ

    def product(px, py, pc):
        rows = gp_ref[py, pc, :, px].reshape(256, 4 * HW + 128)
        part = dot_nt(rows[:, : 4 * HW], wq_ref[...]) + dot_nt(rows[:, 4 * HW :], wf_ref[...])
        return part.reshape(2, 128, D)

    grads = Scatter(product, bufs, sems[0:6], x, y, c)
    line = LineReduce(q_part, lambda h: (slice(4 * h, 4 * h + 4),), 2, land_up, land_down, sems[9:13], z)

    def weight_grads(d):
        columns = normed_ref[:, :, :, :, :, d * 384 : d * 384 + 384].reshape(tokens, 384)
        part = dot_tn(columns, gp_ref[...].reshape(tokens, 4 * HW + 128))
        q_part[d] = part[:, : 4 * HW].astype(LOW).reshape(8, 48, 4 * HW)
        forget[d * 384 : d * 384 + 384] = part[:, 4 * HW :]

    for load in loads:
        load.wait()
    grads.stage(0)
    weight_grads(3)
    grads.stage(1)
    weight_grads(0)
    line.begin(0)
    grads.stage(2)
    weight_grads(2)
    grads.stage(3)
    weight_grads(1)
    line.begin(1)
    line.begin(2)
    grads.stage(4)
    gu_swap = swap_start(gu_ref, gu_out_ref, *sems[6:9], x, y, c)
    line.phase(1)
    lane = lanes(D)
    rows = forget[...].T
    rows = rows[0:8] + rows[24:32] + rows[40:48]
    heads = gains_ref[0] + gains_ref[1]
    heads = heads + pltpu.roll(heads, 3 * HD, 1) + pltpu.roll(heads, 2 * HD, 1)
    heads = jnp.concatenate([heads, jnp.zeros((8, D - PAD), F32)], axis=1)
    bias = bias_ref[0] + bias_ref[1]
    gains = jnp.where(lane < HD, heads[0:1], 0.0)
    gains = jnp.where((lane >= HD) & (lane < 2 * HD), pltpu.roll(heads, HD, 1)[1:2], gains)
    for h in range(HEADS):
        gains = jnp.where(lane == 2 * HD + t * HEADS + h, bias[h : h + 1, :1], gains)
    small[0:1] = jnp.zeros((1, D), F32)
    small[1:2] = ffn_gain_ref[...]
    small[2:3] = gains
    for h in range(HEADS):
        small[3 + h : 4 + h] = rows[h : h + 1]
    small[6:8] = jnp.zeros((2, D), F32)
    first, second = grads.result()
    gain_grad = jnp.zeros((1, D), F32)
    for j, grad in enumerate((first, second)):
        by_inputs, by_gain = norm_back(grad, x_ref[j].astype(F32), params_ref[:, :D])
        gain_grad = gain_grad + by_gain
        grad_own[j] = (gmid_ref[j] + by_inputs).astype(LOW)
    column_start(grad_own, grad_ref, *sems[13:16], z, c)
    small[0:1] = gain_grad
    line.phase(2)
    exchange_total(small, zbuf, zsum, small_ref, sems[16:20], z, x, y, c)
    swap_wait(gu_swap)
    line.phase(3)
    q_out_ref[...] = q_part[pl.ds(z, 1)][0]
    column_wait(result_ref, out_ref, *sems[21:24], z, c)
    column_wait(grad_own, grad_ref, *sems[13:16], z, c)
    line.finish()


def close_layer(
    gp, normed, wq, wf, x, params, gmid, gu_grad, result, head_gains, bias_sums, ffn_gain, collective_id
):
    return pl.pallas_call(
        close_kernel,
        out_shape=[
            shape_of((2, 128, D), LOW), shape_of((2, 128, D), LOW), shape_of((8, 8, D)),
            shape_of((8, 48, 4 * HW), LOW), shape_of((8, 48, 1024), LOW),
        ],
        in_specs=[ANY] * 3 + [VM] * 4 + [ANY, ANY] + [VM] * 3,
        out_specs=[ANY, ANY, VM, VM, ANY],
        scratch_shapes=[
            pltpu.VMEM((2, 2, 2, 2, 128, 4 * HW + 128), LOW), pltpu.VMEM((2, 2, 2, 2, 128, D), LOW),
            pltpu.VMEM((D, 4 * HW), LOW),
            pltpu.VMEM((2, 128, D), LOW), pltpu.VMEM((4, 8, 48, 4 * HW), LOW),
            pltpu.VMEM((3, 8, 48, 4 * HW), LOW), pltpu.VMEM((3, 8, 48, 4 * HW), LOW),
            pltpu.VMEM((D, 128), F32), pltpu.VMEM((8, D), F32), pltpu.VMEM((4, 8, D), F32), pltpu.VMEM((8, D), F32),
        ]
        + scatter_scratch(128, D)
        + scatter_sems() + swap_sems() + line_sems(2) + column_sems() + exchange_sems() + [DMA((3,))] + column_sems(),
        compiler_params=comm_params(collective_id),
        name="close_layer",
    )(gp, normed, wq, wf, x, params, gmid, gu_grad, result, head_gains, bias_sums, ffn_gain)


def fast_device(
    block_input,
    cotangent,
    lengths,
    qkvo_weight,
    proj_weight,
    gateup_weight,
    down_weight,
    forget_weight,
    norm_params,
    qkvo_mean,
    qkvo_square,
    proj_mean,
    proj_square,
    gateup_mean,
    gateup_square,
    down_mean,
    down_square,
    forget_mean,
    forget_square,
    params_mean,
    params_square,
):
    rate_proj = rate_dense * (D / max(D // 256, 2)) ** 0.5
    params = norm_params.reshape(1, -1)
    x_own, lens, normed_all, qkvo_t, gateup_mine, forget_cols, proj_mine = open_layer(
        block_input, lengths, params, forget_weight.T, qkvo_weight, gateup_weight, proj_weight, 1
    )
    qkvo_t = qkvo_t.reshape(D, 4 * HW)
    raw, q, k, v, att, col, crow, logits, mixed_packed, proj_full, down_t, gu_first, gout_all = attention_forward(
        params, lens, normed_all.reshape(2, SEQ, D), qkvo_t, forget_cols, proj_mine, down_weight, gateup_mine,
        cotangent, 2,
    )
    proj_full, down_t = proj_full.reshape(D, D), down_t.reshape(512, D)
    mixed, middle, hidden, gmid, gmid_low, ffn_gain, gmix, gateup_part, down_shard = ffn_layer(
        mixed_packed.reshape(8, 128, 2 * HW), proj_full, x_own, params, gateup_mine, gu_first, gout_all, down_t, 3
    )
    gp, head_gains, bias_sums, result, gateup_part, proj_part = attention_backward(
        gmix.reshape(2, 2, 2, 128, 2 * HW), raw, q, k, v, att, col, crow, logits,
        params, hidden, down_t, middle, gateup_part, mixed, gmid_low, 4,
    )
    input_grad, block_output, small, qkvo_part, gateup_part = close_layer(
        gp.reshape(2, 2, 2, 2, 128, 4 * HW + 128), normed_all, qkvo_t, forget_cols, x_own, params, gmid,
        gateup_part, result, head_gains, bias_sums, ffn_gain, 5,
    )
    qkvo_shard, gateup_shard, proj_shard, norm = norm_layer(
        qkvo_part, gateup_part, proj_part, down_shard, small, 6
    )
    updates = adam_layer(
        (rate_proj, rate_dense, rate_dense, rate_dense),
        norm,
        small,
        input_grad,
        block_output,
        (proj_shard, down_shard, qkvo_shard, gateup_shard),
        (
            proj_weight, proj_mean, proj_square, down_weight, down_mean, down_square,
            qkvo_weight, qkvo_mean, qkvo_square, gateup_weight, gateup_mean, gateup_square,
        ),
        (
            forget_weight.T, forget_mean.T, forget_square.T,
            params, params_mean.reshape(1, -1), params_square.reshape(1, -1),
        ),
    )
    input_grad, block_output, *updates = updates
    proj_new, down_new, qkvo_new, gateup_new = (updates[i : i + 3] for i in (0, 3, 6, 9))
    forget_new = [value.T for value in updates[12:15]]
    params_new = [value.reshape(-1) for value in updates[15:18]]
    return (
        block_output, input_grad, norm[0, 0],
        *qkvo_new, *proj_new, *gateup_new, *down_new, *forget_new, *params_new,
    )


def solution(mesh):
    seq_size, dp_size = mesh.shape["seq"], mesh.shape["dp"]
    if (seq_size, dp_size) == (8, 4):
        inner = Mesh(mesh.devices.reshape(4, 2, 2, 2), ("z", "x", "y", "c"))
        seq, dp = ("z", "x"), ("y", "c")
        device_function = fast_device
    else:
        inner, seq, dp = mesh, ("seq",), ("dp",)
        device_function = general_device
    tokens, rows, copied = P(dp, seq, None), P(seq + dp, None), P()
    return jax.shard_map(
        device_function,
        mesh=inner,
        in_specs=(tokens, tokens, P(dp)) + (rows,) * 4 + (copied,) * 2 + (rows,) * 8 + (copied,) * 4,
        out_specs=(tokens, tokens, copied) + (rows,) * 12 + (copied,) * 6,
        check_vma=False,
    )
```

```python
import functools

import jax
import jax.numpy as jnp
from jax import lax
from jax.experimental import pallas as pl
from jax.experimental.pallas import tpu as pltpu
from jax.sharding import Mesh
from jax.sharding import PartitionSpec as P

D = 1536
H = 24
HD = 64
FF = 4096
STEP = 10


eps_norm = 1e-06
beta_one = 0.9
beta_two = 0.95
rate_dense = 0.06
rate_small = 0.6
decay_dense = 0.1
adam_eps = 1e-08
neg_large = -1e30
highest = lax.Precision.HIGHEST


def entering(value, axis, join, neutral, backward):
    count, mine = (lax.axis_size(axis), lax.axis_index(axis))
    pieces = lax.all_gather(value, axis)
    if backward:
        pieces = pieces[::-1]
        mine = count - 1 - mine
    running = jnp.full_like(value, 0) + jnp.asarray(neutral, value.dtype)

    def hop(position, running):
        longer = join(running, pieces[position])
        return jnp.where(position < mine, longer, running)

    return lax.fori_loop(0, count - 1, hop, running)


def rms_scale(values, gain_vec):
    return (
        values * lax.rsqrt(jnp.mean(values * values, axis=-1, keepdims=True) + eps_norm) * gain_vec
    )


def heads_in(projected, logits, gain_query, gain_key):
    token_count = projected.shape[0]
    query_raw, key_raw, value_raw, gate_raw = jnp.split(projected, 4, axis=1)
    queries = rms_scale(query_raw.reshape(token_count, H, HD), gain_query)
    keys_out = rms_scale(key_raw.reshape(token_count, H, HD), gain_key)
    return (
        queries,
        keys_out,
        value_raw.reshape(token_count, H, HD),
        jax.nn.sigmoid(gate_raw),
        jax.nn.log_sigmoid(logits),
    )


def swiglu(gateup):
    return jax.nn.silu(gateup[:, :FF]) * gateup[:, FF:]


def add_terms(earlier, later):
    return earlier + later


def contract_rows(left, right):
    return lax.dot_general(
        left, right, (((0,), (0,)), ((), ())), preferred_element_type=jnp.float32
    )


def contract_cols(left, right):
    return lax.dot_general(
        left, right, (((1,), (1,)), ((), ())), preferred_element_type=jnp.float32
    )


def sub_width(piece_len, block_len):
    pieces = piece_len // block_len
    group_size = 1
    while group_size * 2 * block_len <= 256 and pieces % (group_size * 2) == 0:
        group_size = group_size * 2
    return group_size * block_len


def scores_of(query_part, key_part, cumul_query, cumul_key):
    raw_dots = jnp.einsum(
        "rqhd,rkhd->rhqk", query_part, key_part, preferred_element_type=jnp.float32
    )
    return raw_dots * HD ** (-0.5) + cumul_query[:, :, :, None] - cumul_key[:, :, None, :]


def allowed_of(query_pos, key_pos, lengths):
    causal = key_pos[None, None, :] <= query_pos[None, :, None]
    inside = key_pos[None, None, :] < lengths[:, None, None]
    return (causal & inside)[:, None]


def adam_update(weight, gradient, mean_old, square_old, learn_rate, decay_rate):
    mean_new = beta_one * mean_old + (1.0 - beta_one) * gradient
    square_new = beta_two * square_old + (1.0 - beta_two) * gradient * gradient
    moved = (
        mean_new
        / (1.0 - beta_one**STEP)
        / (jnp.sqrt(square_new / (1.0 - beta_two**STEP)) + adam_eps)
    )
    return (weight - learn_rate * (moved + decay_rate * weight), mean_new, square_new)


def general_device(
    block_input,
    cotangent,
    lengths,
    qkvo_weight,
    proj_weight,
    gateup_weight,
    down_weight,
    forget_weight,
    norm_params,
    qkvo_mean,
    qkvo_square,
    proj_mean,
    proj_square,
    gateup_mean,
    gateup_square,
    down_mean,
    down_square,
    forget_mean,
    forget_square,
    params_mean,
    params_square,
):
    rows_here = block_input.shape[0]
    block_len = block_input.shape[1]
    token_count = rows_here * block_len
    cycle_index = lax.axis_index("seq")
    my_start = cycle_index * block_len
    positions = my_start + jnp.arange(block_len, dtype=jnp.int32)
    last_pos = my_start + block_len - 1
    longest = jnp.max(lengths)
    head_shape = (rows_here, block_len, H, HD)
    scale_dot = HD ** (-0.5)
    rate_proj = rate_dense * (D / max(D // 256, 2)) ** 0.5
    qkvo_full, proj_full, gateup_full, down_full = (
        lax.all_gather(qkvo_weight.astype(jnp.bfloat16), ("seq", "dp"), axis=0, tiled=True),
        lax.all_gather(proj_weight.astype(jnp.bfloat16), ("seq", "dp"), axis=0, tiled=True),
        lax.all_gather(gateup_weight.astype(jnp.bfloat16), ("seq", "dp"), axis=0, tiled=True),
        lax.all_gather(down_weight.astype(jnp.bfloat16), ("seq", "dp"), axis=0, tiled=True),
    )
    gain_attn = norm_params[:D]
    gain_ffn = norm_params[D : 2 * D]
    gain_query = norm_params[2 * D : 2 * D + HD]
    gain_key = norm_params[2 * D + HD : 2 * D + 2 * HD]
    bias_forget = norm_params[2 * D + 2 * HD :]
    inputs = block_input.astype(jnp.float32).reshape(token_count, D)
    normed, norm_pull = jax.vjp(rms_scale, inputs, gain_attn)
    normed_low = normed.astype(jnp.bfloat16)
    normed_back = normed_low.astype(jnp.float32)
    projected = jnp.dot(normed_low, qkvo_full, preferred_element_type=jnp.float32)
    logits = jnp.dot(normed_back, forget_weight, precision=highest) + bias_forget
    head_values, heads_pull = jax.vjp(heads_in, projected, logits, gain_query, gain_key)
    queries, keys_out, values_out, outgate, log_forget = head_values
    query_low = queries.astype(jnp.bfloat16).reshape(head_shape)
    key_low = keys_out.astype(jnp.bfloat16).reshape(head_shape)
    value_low = values_out.astype(jnp.bfloat16).reshape(head_shape)
    local_cumul = jnp.cumsum(log_forget.reshape(rows_here, block_len, H), axis=1)
    offset = entering(
        local_cumul[:, -1, :], "seq", add_terms, jnp.zeros((rows_here, H), jnp.float32), False
    )
    cumul = local_cumul + offset[:, None, :]
    cumul_all = lax.all_gather(cumul, "seq", axis=1, tiled=True)
    cumul_own = cumul.transpose(0, 2, 1)
    start_state = (
        jnp.full((rows_here, H, block_len), neg_large, jnp.float32),
        jnp.zeros((rows_here, H, block_len), jnp.float32),
        jnp.zeros((rows_here, H, block_len, HD), jnp.float32),
    )
    key_piece = lax.all_gather(key_low, "seq", axis=1, tiled=True)
    value_piece = lax.all_gather(value_low, "seq", axis=1, tiled=True)
    piece_len = key_piece.shape[1]
    sub_len = sub_width(piece_len, block_len)

    def forward_update(sub_index, state_now):
        key_start = sub_index * sub_len

        def forward_compute(state_run):
            run_max, run_sum, run_acc = state_run
            key_block = lax.dynamic_slice_in_dim(key_piece, sub_index * sub_len, sub_len, 1)
            value_block = lax.dynamic_slice_in_dim(value_piece, sub_index * sub_len, sub_len, 1)
            cumul_block = lax.dynamic_slice_in_dim(cumul_all, key_start, sub_len, 1).transpose(
                0, 2, 1
            )
            key_pos = key_start + jnp.arange(sub_len, dtype=jnp.int32)
            allowed = allowed_of(positions, key_pos, lengths)
            scores = jnp.where(
                allowed, scores_of(query_low, key_block, cumul_own, cumul_block), neg_large
            )
            new_max = jnp.maximum(run_max, jnp.max(scores, axis=-1))
            factor = jnp.exp(run_max - new_max)
            attn_probs = jnp.where(allowed, jnp.exp(scores - new_max[..., None]), 0.0)
            run_sum = run_sum * factor + jnp.sum(attn_probs, axis=-1)
            run_acc = run_acc * factor[..., None] + jnp.einsum(
                "rhqk,rkhd->rhqd",
                attn_probs.astype(jnp.bfloat16),
                value_block,
                preferred_element_type=jnp.float32,
            )
            return (new_max, run_sum, run_acc)

        is_live = (key_start <= last_pos) & (key_start < longest)
        return lax.cond(is_live, forward_compute, lambda state_run: state_run, state_now)

    run_max, run_sum, run_acc = lax.fori_loop(0, piece_len // sub_len, forward_update, start_state)
    attended = run_acc / run_sum[..., None]
    log_total = run_max + jnp.log(run_sum)
    attended_rows = attended.transpose(0, 2, 1, 3).reshape(token_count, D)
    mixed_low = (attended_rows * outgate).astype(jnp.bfloat16)
    middle = inputs + jnp.dot(mixed_low, proj_full, preferred_element_type=jnp.float32)
    normed_two, norm_two_pull = jax.vjp(rms_scale, middle, gain_ffn)
    normed_two_low = normed_two.astype(jnp.bfloat16)
    gateup = jnp.dot(normed_two_low, gateup_full, preferred_element_type=jnp.float32)
    hidden, swiglu_pull = jax.vjp(swiglu, gateup)
    hidden_low = hidden.astype(jnp.bfloat16)
    result = middle + jnp.dot(hidden_low, down_full, preferred_element_type=jnp.float32)
    block_output = result.astype(jnp.bfloat16).reshape(rows_here, block_len, D)
    valid = (positions[None, :] < lengths[:, None]).astype(jnp.float32)
    grad_out = (cotangent.astype(jnp.float32) * valid[:, :, None]).reshape(token_count, D)
    grad_out_low = grad_out.astype(jnp.bfloat16)
    grad_down_w = contract_rows(hidden_low, grad_out_low)
    grad_hidden = contract_cols(grad_out_low, down_full)
    grad_gateup_low = swiglu_pull(grad_hidden)[0].astype(jnp.bfloat16)
    grad_gateup_w = contract_rows(normed_two_low, grad_gateup_low)
    grad_normed_two = contract_cols(grad_gateup_low, gateup_full)
    grad_middle_part, grad_gain_ffn = norm_two_pull(grad_normed_two)
    grad_middle = grad_out + grad_middle_part
    grad_middle_low = grad_middle.astype(jnp.bfloat16)
    grad_proj_w = contract_rows(mixed_low, grad_middle_low)
    grad_mixed = contract_cols(grad_middle_low, proj_full)
    grad_outgate = grad_mixed * attended_rows
    grad_att_low = (grad_mixed * outgate).astype(jnp.bfloat16).reshape(head_shape)
    delta = jnp.sum(
        grad_att_low.astype(jnp.float32) * attended.transpose(0, 2, 1, 3), axis=-1
    ).transpose(0, 2, 1)
    lse_all, delta_all = (
        lax.all_gather(log_total, "seq", axis=2, tiled=True),
        lax.all_gather(delta, "seq", axis=2, tiled=True),
    )
    query_state = (
        jnp.zeros((rows_here, H, block_len, HD), jnp.float32),
        jnp.zeros((rows_here, H, block_len), jnp.float32),
    )
    query_key_piece = lax.all_gather(key_low, "seq", axis=1, tiled=True)
    query_value_piece = lax.all_gather(value_low, "seq", axis=1, tiled=True)
    piece_len = query_key_piece.shape[1]
    query_sub_len = sub_width(piece_len, block_len)

    def query_update(sub_index, state_now):
        key_start = sub_index * query_sub_len

        def query_compute(state_run):
            grad_query, grad_cq = state_run
            key_block = lax.dynamic_slice_in_dim(
                query_key_piece, sub_index * query_sub_len, query_sub_len, 1
            )
            value_block = lax.dynamic_slice_in_dim(
                query_value_piece, sub_index * query_sub_len, query_sub_len, 1
            )
            cumul_block = lax.dynamic_slice_in_dim(
                cumul_all, key_start, query_sub_len, 1
            ).transpose(0, 2, 1)
            key_pos = key_start + jnp.arange(query_sub_len, dtype=jnp.int32)
            allowed = allowed_of(positions, key_pos, lengths)
            scores = jnp.where(
                allowed, scores_of(query_low, key_block, cumul_own, cumul_block), neg_large
            )
            attn_probs = jnp.where(allowed, jnp.exp(scores - log_total[..., None]), 0.0)
            grad_probs = jnp.einsum(
                "rqhd,rkhd->rhqk", grad_att_low, value_block, preferred_element_type=jnp.float32
            )
            scores_low = (attn_probs * (grad_probs - delta[..., None])).astype(jnp.bfloat16)
            grad_query = (
                grad_query
                + jnp.einsum(
                    "rhqk,rkhd->rhqd", scores_low, key_block, preferred_element_type=jnp.float32
                )
                * scale_dot
            )
            grad_cq = grad_cq + jnp.sum(scores_low.astype(jnp.float32), axis=-1)
            return (grad_query, grad_cq)

        is_live = (key_start <= last_pos) & (key_start < longest)
        return lax.cond(is_live, query_compute, lambda state_run: state_run, state_now)

    grad_query, grad_cq = lax.fori_loop(0, piece_len // query_sub_len, query_update, query_state)
    key_state = (
        jnp.zeros((rows_here, H, block_len, HD), jnp.float32),
        jnp.zeros((rows_here, H, block_len, HD), jnp.float32),
        jnp.zeros((rows_here, H, block_len), jnp.float32),
    )
    query_piece = lax.all_gather(query_low, "seq", axis=1, tiled=True)
    dout_piece = lax.all_gather(grad_att_low, "seq", axis=1, tiled=True)
    piece_len = query_piece.shape[1]
    key_sub_len = sub_width(piece_len, block_len)

    def key_update(sub_index, state_now):
        query_start = sub_index * key_sub_len

        def key_compute(state_run):
            grad_key, grad_value, grad_ck = state_run
            query_block = lax.dynamic_slice_in_dim(
                query_piece, sub_index * key_sub_len, key_sub_len, 1
            )
            dout_block = lax.dynamic_slice_in_dim(
                dout_piece, sub_index * key_sub_len, key_sub_len, 1
            )
            lse_block = lax.dynamic_slice_in_dim(lse_all, query_start, key_sub_len, 2)
            delta_block = lax.dynamic_slice_in_dim(delta_all, query_start, key_sub_len, 2)
            cumul_block = lax.dynamic_slice_in_dim(
                cumul_all, query_start, key_sub_len, 1
            ).transpose(0, 2, 1)
            query_pos = query_start + jnp.arange(key_sub_len, dtype=jnp.int32)
            allowed = allowed_of(query_pos, positions, lengths)
            scores = jnp.where(
                allowed, scores_of(query_block, key_low, cumul_block, cumul_own), neg_large
            )
            attn_probs = jnp.where(allowed, jnp.exp(scores - lse_block[..., None]), 0.0)
            grad_value = grad_value + jnp.einsum(
                "rhqk,rqhd->rhkd",
                attn_probs.astype(jnp.bfloat16),
                dout_block,
                preferred_element_type=jnp.float32,
            )
            grad_probs = jnp.einsum(
                "rqhd,rkhd->rhqk", dout_block, value_low, preferred_element_type=jnp.float32
            )
            scores_low = (attn_probs * (grad_probs - delta_block[..., None])).astype(jnp.bfloat16)
            grad_key = (
                grad_key
                + jnp.einsum(
                    "rhqk,rqhd->rhkd", scores_low, query_block, preferred_element_type=jnp.float32
                )
                * scale_dot
            )
            grad_ck = grad_ck - jnp.sum(scores_low.astype(jnp.float32), axis=2)
            return (grad_key, grad_value, grad_ck)

        is_live = query_start + key_sub_len - 1 >= my_start
        return lax.cond(is_live, key_compute, lambda state_run: state_run, state_now)

    grad_key, grad_value, grad_ck = lax.fori_loop(
        0, piece_len // key_sub_len, key_update, key_state
    )
    grad_cumul = (grad_cq + grad_ck).transpose(0, 2, 1)
    local_suffix = jnp.flip(jnp.cumsum(jnp.flip(grad_cumul, axis=1), axis=1), axis=1)
    suffix = entering(
        local_suffix[:, 0, :], "seq", add_terms, jnp.zeros((rows_here, H), jnp.float32), True
    )
    grad_log_forget = (local_suffix + suffix[:, None, :]).reshape(token_count, H)
    grad_queries = grad_query.transpose(0, 2, 1, 3).reshape(token_count, H, HD)
    grad_keys = grad_key.transpose(0, 2, 1, 3).reshape(token_count, H, HD)
    grad_values = grad_value.transpose(0, 2, 1, 3).reshape(token_count, H, HD)
    grad_projected, grad_logits, grad_gain_query, grad_gain_key = heads_pull(
        (grad_queries, grad_keys, grad_values, grad_outgate, grad_log_forget)
    )
    grad_projected_low = grad_projected.astype(jnp.bfloat16)
    grad_qkvo_w = contract_rows(normed_low, grad_projected_low)
    grad_forget_w = lax.dot_general(
        normed_back,
        grad_logits,
        (((0,), (0,)), ((), ())),
        precision=highest,
        preferred_element_type=jnp.float32,
    )
    grad_bias = jnp.sum(grad_logits, axis=0)
    grad_normed = contract_cols(grad_projected_low, qkvo_full) + jnp.dot(
        grad_logits, forget_weight.T, precision=highest
    )
    grad_inputs_part, grad_gain_attn = norm_pull(grad_normed)
    input_grad = (grad_middle + grad_inputs_part).reshape(rows_here, block_len, D)
    qkvo_shard, proj_shard, gateup_shard, down_shard = (
        lax.psum_scatter(grad_qkvo_w, ("seq", "dp"), scatter_dimension=0, tiled=True),
        lax.psum_scatter(grad_proj_w, ("seq", "dp"), scatter_dimension=0, tiled=True),
        lax.psum_scatter(grad_gateup_w, ("seq", "dp"), scatter_dimension=0, tiled=True),
        lax.psum_scatter(grad_down_w, ("seq", "dp"), scatter_dimension=0, tiled=True),
    )
    shard_squares = (
        jnp.sum(qkvo_shard * qkvo_shard)
        + jnp.sum(proj_shard * proj_shard)
        + jnp.sum(gateup_shard * gateup_shard)
        + jnp.sum(down_shard * down_shard)
    )
    small_grads = jnp.concatenate(
        [grad_gain_attn, grad_gain_ffn, grad_gain_query, grad_gain_key, grad_bias]
    )
    small_total, forget_total, square_total = lax.psum(
        (small_grads, grad_forget_w, shard_squares), ("seq", "dp")
    )
    grad_norm = jnp.sqrt(
        square_total + jnp.sum(small_total * small_total) + jnp.sum(forget_total * forget_total)
    )
    clip_factor = 1.0 / jnp.maximum(grad_norm, 1.0)
    qkvo_new, qkvo_m, qkvo_v = adam_update(
        qkvo_weight, qkvo_shard * clip_factor, qkvo_mean, qkvo_square, rate_dense, decay_dense
    )
    proj_new, proj_m, proj_v = adam_update(
        proj_weight, proj_shard * clip_factor, proj_mean, proj_square, rate_proj, decay_dense
    )
    gateup_new, gateup_m, gateup_v = adam_update(
        gateup_weight,
        gateup_shard * clip_factor,
        gateup_mean,
        gateup_square,
        rate_dense,
        decay_dense,
    )
    down_new, down_m, down_v = adam_update(
        down_weight, down_shard * clip_factor, down_mean, down_square, rate_dense, decay_dense
    )
    forget_new, forget_m, forget_v = adam_update(
        forget_weight,
        forget_total * clip_factor,
        forget_mean,
        forget_square,
        rate_dense,
        decay_dense,
    )
    params_new, params_m, params_v = adam_update(
        norm_params, small_total * clip_factor, params_mean, params_square, rate_small, 0.0
    )
    return (
        block_output,
        input_grad,
        grad_norm,
        qkvo_new,
        qkvo_m,
        qkvo_v,
        proj_new,
        proj_m,
        proj_v,
        gateup_new,
        gateup_m,
        gateup_v,
        down_new,
        down_m,
        down_v,
        forget_new,
        forget_m,
        forget_v,
        params_new,
        params_m,
        params_v,
    )


QB = 256
HEADS = 3
HW = HEADS * HD
PAD = 256
SEQ = 1024
LOW = jnp.bfloat16
F32 = jnp.float32
scale_dot = HD**-0.5
DEV = pl.DeviceIdType.MESH
ANY = pl.BlockSpec(memory_space=pl.ANY)
VM = pl.BlockSpec(memory_space=pltpu.VMEM)
SM = pl.BlockSpec(memory_space=pltpu.SMEM)
DMA = pltpu.SemaphoreType.DMA
PAIRS = ((0, 0), (0, 1), (0, 2), (1, 0), (1, 1), (2, 0))


def shape_of(shape, dtype=F32):
    return jax.ShapeDtypeStruct(shape, dtype)


def dot_nt(a, b):
    return lax.dot_general(a, b, (((1,), (1,)), ((), ())), preferred_element_type=F32)


def dot_tn(a, b):
    return lax.dot_general(a, b, (((0,), (0,)), ((), ())), preferred_element_type=F32)


def dot_nn(a, b):
    return jnp.dot(a, b, preferred_element_type=F32)


def place():
    return tuple(lax.axis_index(a) for a in ("z", "x", "y", "c"))


def other(index, differs):
    return 1 - index if differs else index


def group_peer(d, x, y, c):
    px, py, pc = other(x, d & 4), other(y, d & 2), other(c, d & 1)
    return {"x": px, "y": py, "c": pc}, px * 4 + py * 2 + pc


def greet(z, x, y, c, column=False, line=False, plane=False):
    barrier = pltpu.get_barrier_semaphore()

    def signal(peer):
        pl.semaphore_signal(barrier, inc=1, device_id=peer, device_id_type=DEV)

    for d in range(1, 8):
        signal(group_peer(d, x, y, c)[0])
    count = 7
    if column:
        away = z // 2 - c
        count = count + 1 + away * away
        for r in range(2):
            pl.when(jnp.logical_not((away == 0) & (2 * c + r == z)))(
                functools.partial(signal, {"z": 2 * c + r, "c": z // 2})
            )
    if line:
        count = count + 1 + z * (3 - z) // 2
        pl.when(z < 3)(functools.partial(signal, {"z": z + 1}))
        pl.when(z > 0)(functools.partial(signal, {"z": z - 1}))
    if plane:
        count = count + 3
        for d in range(1, 4):
            signal({"z": lax.rem(z + d, 4)})
    pl.semaphore_wait(barrier, count)


def remote(src, dst, send_sem, recv_sem, peer):
    return pltpu.make_async_remote_copy(
        src_ref=src, dst_ref=dst, send_sem=send_sem, recv_sem=recv_sem, device_id=peer, device_id_type=DEV
    )


VMEM_BYTES = 63 * 1024 * 1024


def comm_params(collective_id):
    return pltpu.CompilerParams(collective_id=collective_id, has_side_effects=True, vmem_limit_bytes=VMEM_BYTES)


def swap_start(src, dst, send_sem, recv_sem, local_sem, x, y, c):
    me = x * 4 + y * 2 + c
    own = pltpu.make_async_copy(src.at[me], dst.at[me], local_sem)
    own.start()
    copies = []
    for d in (4, 2, 6, 5, 3, 7, 1):
        peer, number = group_peer(d, x, y, c)
        copy = remote(src.at[number], dst.at[me], send_sem.at[d], recv_sem.at[d], peer)
        copy.start()
        copies.append(copy)
    return own, copies


def swap_wait(started):
    own, copies = started
    own.wait()
    for copy in copies:
        copy.wait()


def swap_sems():
    return [DMA((8,)), DMA((8,)), DMA]


def column_start(src, dst, send, recv, local, z, c):
    slot = lax.rem(z, 2)
    for r in range(2):
        keep = (z // 2 == c) & (2 * c + r == z)

        @pl.when(keep)
        def _():
            pltpu.make_async_copy(src.at[r], dst.at[slot], local).start()

        @pl.when(jnp.logical_not(keep))
        def _():
            peer = {"z": 2 * c + r, "c": z // 2}
            remote(src.at[r], dst.at[slot], send.at[r], recv.at[slot], peer).start()


def column_wait(src, dst, send, recv, local, z, c):
    slot = lax.rem(z, 2)
    for r in range(2):
        keep = (z // 2 == c) & (2 * c + r == z)
        peer = {"z": 2 * c + r, "c": z // 2}

        @pl.when(keep)
        def _():
            pltpu.make_async_copy(src.at[r], dst.at[slot], local).wait()

        @pl.when(jnp.logical_not(keep))
        def _():
            remote(src.at[r], dst.at[slot], send.at[r], recv.at[slot], peer).wait_send()
            remote(src.at[r], dst.at[r], send.at[r], recv.at[r], peer).wait_recv()


def column_sems():
    return [DMA((2,)), DMA((2,)), DMA]


class LineGather:
    def __init__(self, own_at, dst_at, chunks, sems, z):
        self.own_at, self.dst_at, self.chunks, self.z = own_at, dst_at, chunks, z
        self.sems = sems

    def copy(self, k, h, up):
        send, recv = self.sems[0:2] if up else self.sems[2:4]
        block = self.z - k if up else self.z + k
        src = self.own_at(h) if k == 0 else self.dst_at(block, h)
        n = k * self.chunks + h
        peer = {"z": self.z + 1 if up else self.z - 1}
        return remote(src, self.dst_at(block, h), send.at[n], recv.at[n], peer)

    def cases(self, k, up):
        z = self.z
        if up:
            return (z < 3) & (z >= k), z >= k + 1
        return (z > 0) & (z + k <= 3), z + k + 1 <= 3

    def send(self, k):
        for h in range(self.chunks):
            for up in (True, False):
                if k > 0:
                    self.wait_one(k - 1, h, up)

                @pl.when(self.cases(k, up)[0])
                def _():
                    self.copy(k, h, up).start()

    def wait_one(self, k, h, up):
        @pl.when(self.cases(k, up)[1])
        def _():
            self.copy(k, h, up).wait_recv()

    def finish(self):
        for h in range(self.chunks):
            for up in (True, False):
                self.wait_one(2, h, up)
        for k in range(3):
            for h in range(self.chunks):
                for up in (True, False):

                    @pl.when(self.cases(k, up)[0])
                    def _():
                        self.copy(k, h, up).wait_send()


def line_sems(chunks):
    return [DMA((3 * chunks,))] * 4


class LineReduce:
    def __init__(self, part, chunk, chunks, land_up, land_down, sems, z):
        self.part, self.chunk, self.chunks, self.z = part, chunk, chunks, z
        self.lands = {True: land_up, False: land_down}
        self.sems = {True: sems[0:2], False: sems[2:4]}

    def copy(self, m, h, up):
        dest = 3 - m if up else m
        send, recv = self.sems[up]
        n = m * self.chunks + h
        peer = {"z": self.z + 1 if up else self.z - 1}
        land = self.lands[up].at[(m, *self.chunk(h))]
        return remote(self.part.at[(dest, *self.chunk(h))], land, send.at[n], recv.at[n], peer)

    def add(self, m, h, up):
        dest = 3 - m if up else m
        at = self.chunk(h)
        here, come = (dest, *at), (m, *at)
        total = self.part[here].astype(F32) + self.lands[up][come].astype(F32)
        self.part[here] = total.astype(LOW)

    def begin(self, m):
        for up in (True, False):

            @pl.when(self.z == (0 if up else 3))
            def _():
                for h in range(self.chunks):
                    self.copy(m, h, up).start()

    def phase(self, p, chunks=None):
        chunks = range(self.chunks) if chunks is None else chunks
        if p == 0:
            for m in range(3):
                self.begin(m)
            return
        for m in range(3):
            for hops in range(1, 4 - m):
                if p != hops + m:
                    continue
                for up in (True, False):

                    @pl.when(self.z == (hops if up else 3 - hops))
                    def _():
                        for h in chunks:
                            self.copy(m, h, up).wait_recv()
                            self.add(m, h, up)
                            if hops < 3 - m:
                                self.copy(m, h, up).start()

    def finish(self):
        for m in range(3):
            for h in range(self.chunks):
                for up in (True, False):
                    dest = 3 - m if up else m

                    @pl.when(self.z < dest if up else self.z > dest)
                    def _():
                        self.copy(m, h, up).wait_send()


class Gather:
    def __init__(self, src_at, dst_at, sems, x, y, c):
        send_x, recv_x, send_y, recv_y, send_c, recv_c, local = sems
        ox, oy = 1 - x, 1 - y
        xp, yp, cp = {"x": ox}, {"y": oy}, {"c": 1 - c}

        def own(j, send, recv, peer):
            return remote(src_at(j), dst_at(x, y, c, j), send.at[j], recv.at[j], peer)

        def onward(px, py, j, k, send, recv, peer):
            block = dst_at(px, py, c, j)
            return remote(block, block, send.at[k], recv.at[k], peer)

        self.x = [own(j, send_x, recv_x, xp) for j in range(2)]
        self.y = [own(j, send_y, recv_y, yp) for j in range(2)]
        self.c = [own(j, send_c, recv_c, cp) for j in range(2)]
        self.local = [pltpu.make_async_copy(src_at(j), dst_at(x, y, c, j), local.at[j]) for j in range(2)]
        self.diag_y = onward(ox, y, 0, 2, send_y, recv_y, yp)
        self.diag_x = onward(x, oy, 1, 2, send_x, recv_x, xp)
        order = ((ox, y, 0), (x, oy, 1), (ox, y, 1), (x, oy, 0), (ox, oy, 0), (ox, oy, 1))
        self.pass_c = [onward(*p, k + 2, send_c, recv_c, cp) for k, p in enumerate(order)]

    def start(self):
        for copy in (self.x[0], self.y[1], self.x[1], self.y[0], self.c[0], self.c[1], *self.local):
            copy.start()

    def forward(self):
        self.x[0].wait_recv()
        self.diag_y.start()
        self.pass_c[0].start()
        self.y[1].wait_recv()
        self.diag_x.start()
        self.pass_c[1].start()

    def forward_rest(self):
        self.x[1].wait_recv()
        self.pass_c[2].start()
        self.y[0].wait_recv()
        self.pass_c[3].start()

    def finish(self):
        self.diag_y.wait_recv()
        self.pass_c[4].start()
        self.diag_x.wait_recv()
        self.pass_c[5].start()
        for copy in (*self.x, *self.y, *self.c, self.diag_x, self.diag_y, *self.pass_c):
            copy.wait_send()
        for copy in (*self.c, *self.pass_c):
            copy.wait_recv()
        for copy in self.local:
            copy.wait()


def gather_sems():
    return [DMA((3,)), DMA((3,)), DMA((3,)), DMA((3,)), DMA((8,)), DMA((8,)), DMA((2,))]


def natural(ref):
    return lambda x, y, c, j: ref.at[y, c, j, x]


class Scatter:
    def __init__(self, product, bufs, sems, x, y, c):
        self.product, self.own_c = product, c
        self.to_core, self.from_core, self.to_x, self.from_x, self.to_y, self.from_y, self.kept = bufs
        send_c, recv_c, send_x, recv_x, send_y, recv_y = sems
        ox, oy = 1 - x, 1 - y
        xp, yp, cp = {"x": ox}, {"y": oy}, {"c": 1 - c}
        self.places = ((ox, oy), (ox, y), (x, oy), (x, y))

        def copies(src, dst, send, recv, peer, count):
            return [remote(src.at[k], dst.at[k], send.at[k], recv.at[k], peer) for k in range(count)]

        self.c = [
            remote(self.to_core.at[k % 2], self.from_core.at[k], send_c.at[k], recv_c.at[k], cp) for k in range(4)
        ]
        self.x = copies(self.to_x, self.from_x, send_x, recv_x, xp, 3)
        self.y = copies(self.to_y, self.from_y, send_y, recv_y, yp, 3)

    def to_partner(self, k):
        if k >= 2:
            self.c[k - 2].wait_send()
        self.to_core[k % 2] = self.product(*self.places[k], 1 - self.own_c).astype(LOW)
        self.c[k].start()

    def summed(self, k):
        own = self.product(*self.places[k], self.own_c)
        self.c[k].wait_recv()
        return own + self.from_core[k].astype(F32)

    def close(self, k):
        total = self.summed(k)
        if k == 0:
            self.to_x[0] = total[0].astype(LOW)
            self.x[0].start()
            self.to_y[0] = total[1].astype(LOW)
            self.y[0].start()
        elif k == 1:
            self.to_x[1] = total[0].astype(LOW)
            self.x[1].start()
            self.kept[0] = total[1]
        elif k == 2:
            self.to_y[1] = total[1].astype(LOW)
            self.y[1].start()
            self.kept[1] = total[0]
        else:
            self.y[0].wait_recv()
            self.to_x[2] = (self.kept[0] + self.from_y[0].astype(F32)).astype(LOW)
            self.x[2].start()
            self.x[0].wait_recv()
            self.to_y[2] = (self.kept[1] + self.from_x[0].astype(F32)).astype(LOW)
            self.y[2].start()
            self.kept[0], self.kept[1] = total[0], total[1]

    def stage(self, k):
        if k < 4:
            self.to_partner(k)
        if k > 0:
            self.close(k - 1)

    def result(self):
        self.x[1].wait_recv()
        first = self.kept[0] + self.from_x[1].astype(F32)
        self.y[1].wait_recv()
        second = self.kept[1] + self.from_y[1].astype(F32)
        self.y[2].wait_recv()
        first = first + self.from_y[2].astype(F32)
        self.x[2].wait_recv()
        second = second + self.from_x[2].astype(F32)
        for copy in (*self.c[2:], *self.x, *self.y):
            copy.wait_send()
        return first, second


def scatter_scratch(rows, width):
    return (
        [pltpu.VMEM((2, 2, rows, width), LOW), pltpu.VMEM((4, 2, rows, width), LOW)]
        + [pltpu.VMEM((3, rows, width), LOW)] * 4
        + [pltpu.VMEM((2, rows, width), F32)]
    )


def scatter_sems():
    return [DMA((4,)), DMA((4,)), DMA((3,)), DMA((3,)), DMA((3,)), DMA((3,))]


def exchange_start(in_ref, zbuf, sems, z):
    send, recv = sems
    zbuf[pl.ds(z, 1)] = in_ref[...][None]
    copies = []
    for i in range(3):
        copies.append(remote(in_ref, zbuf.at[z], send.at[i], recv.at[i], {"z": lax.rem(z + i + 1, 4)}))
        copies[i].start()
    return copies


def exchange_end(copies, zbuf, zsum, gbuf, sems, x, y, c):
    send, recv = sems
    me = x * 4 + y * 2 + c
    for copy in copies:
        copy.wait()
    zsum[...] = zbuf[0] + zbuf[1] + zbuf[2] + zbuf[3]
    gbuf[pl.ds(me, 1)] = zsum[...][None]
    copies = []
    for i in range(7):
        peer = group_peer(i + 1, x, y, c)[0]
        copies.append(remote(zsum, gbuf.at[me], send.at[i], recv.at[i], peer))
        copies[i].start()
    for copy in copies:
        copy.wait()


def exchange_total(in_ref, zbuf, zsum, gbuf, sems, z, x, y, c):
    copies = exchange_start(in_ref, zbuf, sems[0:2], z)
    exchange_end(copies, zbuf, zsum, gbuf, sems[2:4], x, y, c)


def exchange_scratch(rows, width):
    return [pltpu.VMEM((4, rows, width), F32), pltpu.VMEM((rows, width), F32)]


def exchange_sems():
    return [DMA((3,)), DMA((3,)), DMA((7,)), DMA((7,))]


def add_blocks(gbuf, rows):
    total = gbuf[0, rows]
    for i in range(1, 8):
        total = total + gbuf[i, rows]
    return total


def norm_kernel(
    q_part, gu_ref, proj_ref, down_ref, small_ref,
    q_out, gu_out, proj_out, norm_ref, q_swapped, landed, square, zbuf, zsum, gbuf, *sems,
):
    z, x, y, c = place()
    greet(z, x, y, c, plane=True)
    q_swap = swap_start(q_part, q_swapped, *sems[0:3], x, y, c)
    over_z = []
    for i in range(3):
        dest = lax.rem(z + i + 1, 4)
        over_z.append(remote(proj_ref.at[dest], landed.at[i], sems[7].at[i], sems[8].at[i], {"z": dest}))
        over_z[i].start()

    def squares(values):
        return jnp.sum(jnp.sum(values * values, axis=0, keepdims=True), axis=1, keepdims=True)

    sums = squares(add_blocks(small_ref, slice(0, 3)))
    for i in range(8):
        sums = sums + squares(small_ref[i, 3:6])
    shards = squares(down_ref[...].astype(F32))
    for t in range(8):
        grads = gu_ref[t]
        shards = shards + squares(grads.astype(F32))
        for b in range(8):
            column = (b * 8 + t) * 128
            gu_out[:, column : column + 128] = grads[:, b * 128 : b * 128 + 128]
    swap_wait(q_swap)
    for u in range(8):
        shards = shards + squares(q_swapped[u].astype(F32))
    for copy in over_z:
        copy.wait()
    mine = proj_ref[pl.ds(z, 1)][0].astype(F32)
    for i in range(3):
        mine = mine + landed[i].astype(F32)
    proj_out[...] = mine
    shards = shards + squares(mine)
    square[...] = jnp.broadcast_to(shards, (8, 128))
    exchange = exchange_start(square, zbuf, sems[3:5], z)
    half = lanes(2 * HW) < HW
    for u in range(4):
        even, odd = q_swapped[2 * u].astype(F32), q_swapped[2 * u + 1].astype(F32)
        for m in range(2):
            a, b = even[:, 2 * HW * m : 2 * HW * (m + 1)], odd[:, 2 * HW * m : 2 * HW * (m + 1)]
            first = jnp.where(half, a, pltpu.roll(b, HW, 1)).astype(LOW)
            second = jnp.where(half, pltpu.roll(a, HW, 1), b).astype(LOW)
            column = 2 * m * D + 2 * HW * u
            q_out[:, column : column + 2 * HW] = first
            q_out[:, column + D : column + D + 2 * HW] = second
    exchange_end(exchange, zbuf, zsum, gbuf, sems[5:7], x, y, c)
    norm_ref[...] = jnp.sqrt(add_blocks(gbuf, slice(0, 8)) + sums)


def norm_layer(q_part, gu_part, proj_part, down_shard, small, collective_id):
    return pl.pallas_call(
        norm_kernel,
        out_shape=[shape_of((48, 4 * D), LOW), shape_of((48, 2 * FF), LOW), shape_of((48, D)), shape_of((8, 128))],
        in_specs=[ANY] + [VM] * 4,
        out_specs=[VM] * 4,
        scratch_shapes=[
            pltpu.VMEM((8, 48, 4 * HW), LOW), pltpu.VMEM((3, 48, D), LOW), pltpu.VMEM((8, 128), F32)
        ]
        + exchange_scratch(8, 128) + [pltpu.VMEM((8, 8, 128), F32)]
        + swap_sems() + exchange_sems() + [DMA((3,)), DMA((3,))],
        compiler_params=comm_params(collective_id),
        name="norm_layer",
    )(q_part, gu_part, proj_part, down_shard, small)


ADAM_STEP = 512


def adam_kernel(rates, norm_ref, small_ref, grad_ref, out_ref, *refs):
    count = len(rates)
    grads, refs = refs[:count], refs[count:]
    olds, refs = refs[: 3 * count], refs[3 * count :]
    few, refs = refs[:6], refs[6:]
    grad_wide, out_copy, norm_out, refs = refs[0], refs[1], refs[2], refs[3:]
    norm_out[0, 0] = norm_ref[0, 0]
    news, refs = refs[: 3 * count], refs[3 * count :]
    few_new, refs = refs[:6], refs[6:]
    grad_bufs, refs = refs[:count], refs[count:]
    bufs, refs = refs[: 3 * count], refs[3 * count :]
    grad_sem, in_sem, out_sem = refs
    loads = [pltpu.make_async_copy(grads[i], grad_bufs[i], grad_sem.at[i]) for i in range(count)]
    reads = [pltpu.make_async_copy(olds[i], bufs[i], in_sem.at[i]) for i in range(3 * count)]
    writes = [pltpu.make_async_copy(bufs[i], news[i], out_sem.at[i]) for i in range(3 * count)]
    for i in range(count):
        loads[i].start()
        for k in range(3):
            reads[3 * i + k].start()
    clip = 1.0 / jnp.maximum(norm_ref[:1, :1], 1.0)
    for i in range(count):
        loads[i].wait()
        for k in range(3):
            reads[3 * i + k].wait()
        w_ref, m_ref, v_ref = bufs[3 * i : 3 * i + 3]

        @pl.loop(0, w_ref.shape[1] // ADAM_STEP)
        def _(n):
            at = (slice(None), pl.ds(pl.multiple_of(n * ADAM_STEP, ADAM_STEP), ADAM_STEP))
            gradient = grad_bufs[i][at].astype(F32) * clip
            w_ref[at], m_ref[at], v_ref[at] = adam_update(
                w_ref[at], gradient, m_ref[at], v_ref[at], rates[i], decay_dense
            )

        for k in range(3):
            writes[3 * i + k].start()
    grad_wide[...] = grad_ref[...].astype(F32)
    out_copy[...] = out_ref[...]
    for t in range(8):
        for h in range(HEADS):
            at = slice(t * HEADS + h, t * HEADS + h + 1)
            updated = adam_update(
                few[0][at], small_ref[t, 3 + h : 4 + h] * clip, few[1][at], few[2][at], rate_dense, decay_dense
            )
            for k in range(3):
                few_new[k][at] = updated[k]
    small = add_blocks(small_ref, slice(0, 3))
    small = jnp.concatenate([small[0:1], small[1:2], small[2:3]], axis=1)[:, : few[3].shape[0]]
    old = [few[3 + k][...].reshape(1, -1) for k in range(3)]
    updated = adam_update(old[0], small * clip, old[1], old[2], rate_small, 0.0)
    for k in range(3):
        few_new[3 + k][...] = updated[k].reshape(-1)
    for write in writes:
        write.wait()


def adam_layer(rates, norm, small, input_grad, block_output, grads, olds, few):
    count = len(rates)
    return pl.pallas_call(
        functools.partial(adam_kernel, rates),
        out_shape=[shape_of(input_grad.shape), shape_of(block_output.shape, LOW), shape_of((1, 1))]
        + [shape_of(a.shape) for a in (*olds, *few)],
        in_specs=[VM] * 4 + [ANY] * (4 * count) + [VM] * 6,
        out_specs=[VM, VM, SM] + [ANY] * (3 * count) + [VM] * 6,
        scratch_shapes=[pltpu.VMEM(a.shape, a.dtype) for a in grads]
        + [pltpu.VMEM(a.shape, F32) for a in olds]
        + [DMA((count,)), DMA((3 * count,)), DMA((3 * count,))],
        compiler_params=pltpu.CompilerParams(vmem_limit_bytes=VMEM_BYTES),
        name="adam",
    )(norm, small, input_grad, block_output, *grads, *olds, *few)


def row_scale(values):
    return lax.rsqrt(jnp.mean(values * values, axis=-1, keepdims=True) + eps_norm)


def norm_back(grad, values, gain_vec):
    r = row_scale(values)
    u = grad * gain_vec
    by_values = r * u - values * (r * r * r) * jnp.mean(values * u, axis=-1, keepdims=True)
    return by_values, jnp.sum(grad * values * r, axis=0, keepdims=True)


def open_kernel(
    x_ref, lens_ref, params_ref, forget_ref, wq_ref, wg_ref, wp_ref,
    xo_ref, lo_ref, normed_ref, qkvo_ref, gu_ref, wf_ref, proj_ref,
    normed_own, wq_low, wg_low, wp_low, len_tile, *sems,
):
    z, x, y, c = place()
    t = x * 4 + y * 2 + c
    greet(z, x, y, c, column=True, line=True)
    column_start(x_ref, xo_ref, *sems[0:3], z, c)
    half = lanes(2 * HW) < HW
    for u in range(4):
        for m in range(2):
            column = 2 * m * D + 2 * HW * u
            a, b = wq_ref[:, column : column + 2 * HW], wq_ref[:, column + D : column + D + 2 * HW]
            at = slice(2 * HW * m, 2 * HW * (m + 1))
            wq_low[2 * u, :, at] = jnp.where(half, a, pltpu.roll(b, HW, 1)).astype(LOW)
            wq_low[2 * u + 1, :, at] = jnp.where(half, pltpu.roll(a, HW, 1), b).astype(LOW)
    qkvo_swap = swap_start(wq_low, qkvo_ref.at[z], *sems[3:6], x, y, c)
    row = lax.broadcasted_iota(jnp.int32, (8, 128), 0)
    tile = jnp.where(row == 0, lens_ref[0].astype(F32), lens_ref[1].astype(F32))
    for d in range(8):
        len_tile[d] = tile
    lens = swap_start(len_tile, lo_ref, *sems[6:9], x, y, c)
    wp_low[...] = wp_ref[...].astype(LOW)
    own_proj = pltpu.make_async_copy(wp_low, proj_ref.at[z], sems[9])
    own_proj.start()
    for d in range(8):
        for b in range(8):
            column = (b * 8 + d) * 128
            wg_low[d, :, b * 128 : b * 128 + 128] = wg_ref[:, column : column + 128].astype(LOW)
    proj = LineGather(lambda h: wp_low, lambda k, h: proj_ref.at[k], 1, sems[10:14], z)
    qkvo = LineGather(
        lambda h: qkvo_ref.at[z, 4 * h : 4 * h + 4], lambda k, h: qkvo_ref.at[k, 4 * h : 4 * h + 4], 2,
        sems[14:18], z,
    )
    swap_wait(qkvo_swap)
    qkvo.send(0)
    proj.send(0)
    sub = lax.broadcasted_iota(jnp.int32, (8, D), 0)
    mine = jnp.zeros((8, D), F32)
    for d in range(8):
        for h in range(HEADS):
            mine = jnp.where((sub == h) & (t == d), forget_ref[d * HEADS + h : d * HEADS + h + 1], mine)
    parts = pieces_of(mine)
    wf_ref[...] = columns_of(jnp.concatenate([parts[b] for _, b in PAIRS], axis=0)).astype(LOW)
    column_wait(x_ref, xo_ref, *sems[0:3], z, c)
    for j in range(2):
        rows = xo_ref[j].astype(F32)
        normed_own[j] = (rows * row_scale(rows) * params_ref[:, :D]).astype(LOW)
    normed = Gather(lambda j: normed_own.at[j], natural(normed_ref), sems[18:25], x, y, c)
    normed.start()
    gu_swap = swap_start(wg_low, gu_ref, *sems[25:28], x, y, c)
    qkvo.send(1)
    proj.send(1)
    normed.forward()
    normed.forward_rest()
    qkvo.send(2)
    proj.send(2)
    normed.finish()
    qkvo.finish()
    proj.finish()
    own_proj.wait()
    swap_wait(gu_swap)
    swap_wait(lens)


def open_layer(x, lengths, params, forget, qkvo_weight, gateup_weight, proj_weight, collective_id):
    return pl.pallas_call(
        open_kernel,
        out_shape=[
            shape_of(x.shape, LOW),
            shape_of((8, 8, 128)),
            shape_of((2, 2, 2, 2, 128, D), LOW),
            shape_of((4, 8, 48, 4 * HW), LOW),
            shape_of((8, 48, 1024), LOW),
            shape_of((D, 128), LOW),
            shape_of((4, 48, D), LOW),
        ],
        in_specs=[ANY, SM, VM, VM, VM, VM, VM],
        out_specs=[VM] + [ANY] * 4 + [VM, ANY],
        scratch_shapes=[
            pltpu.VMEM((2, 128, D), LOW), pltpu.VMEM((8, 48, 4 * HW), LOW), pltpu.VMEM((8, 48, 1024), LOW),
            pltpu.VMEM((48, D), LOW), pltpu.VMEM((8, 8, 128), F32),
        ]
        + column_sems() + swap_sems() * 2 + [DMA] + line_sems(1) + line_sems(2) + gather_sems() + swap_sems(),
        compiler_params=comm_params(collective_id),
        name="open_layer",
    )(x, lengths, params, forget, qkvo_weight, gateup_weight, proj_weight)


def length_of(len_ref, z, x, sequence):
    tile = len_ref[pl.ds(x * 4 + sequence * 2 + z // 2, 1)][0]
    row = lax.broadcasted_iota(jnp.int32, (8, 128), 0) == lax.rem(z, 2)
    return jnp.sum(jnp.where(row, tile, 0.0), axis=0, keepdims=True)[:, :1]


def head_gain(params_ref, key):
    both = params_ref[:, 2 * D : 2 * D + 128]
    both = pltpu.roll(both, HD, 1) if key else both
    one = jnp.concatenate([jnp.where(lanes(128) < HD, both, 0.0), jnp.zeros((1, 128), F32)], axis=1)
    return one + pltpu.roll(one, HD, 1) + pltpu.roll(one, 2 * HD, 1)


def lanes(width):
    return lax.broadcasted_iota(jnp.int32, (1, width), 1)


def head_mask(h):
    lane = lanes(PAD)
    return (lane >= h * HD) & (lane < (h + 1) * HD)


def split_halves(pair):
    valid = lanes(PAD) < HW
    first = jnp.where(valid, pair[:, :PAD], 0.0)
    second = jnp.where(valid, pltpu.roll(pair, HW, 1)[:, :PAD], 0.0)
    return first, second


def join_halves(first, second):
    tail = jnp.zeros((first.shape[0], 128), F32)
    first = jnp.concatenate([first, tail], axis=1)
    second = pltpu.roll(jnp.concatenate([second, tail], axis=1), HW, 1)
    return jnp.where(lanes(2 * HW) < HW, first, second)


def head_sums(values):
    row = lax.broadcasted_iota(jnp.int32, (PAD, PAD), 0) // HD
    column = lax.broadcasted_iota(jnp.int32, (PAD, PAD), 1) // HD
    ones = jnp.where(row == column, 1.0, 0.0).astype(LOW)
    high = values.astype(LOW)
    return dot_nn(high, ones) + dot_nn((values - high.astype(F32)).astype(LOW), ones)


def head_scale(values):
    return lax.rsqrt(head_sums(values * values) / HD + eps_norm)


def head_norm_back(grad, values, gain_vec):
    r = head_scale(values)
    u = grad * gain_vec
    by_values = r * u - values * (r * r * r) * (head_sums(values * u) / HD)
    return by_values, jnp.sum(grad * values * r, axis=0, keepdims=True)


def running_sum(rows, backward):
    lane = lanes(SEQ)
    step = 1
    while step < SEQ:
        if backward:
            rows = rows + jnp.where(lane < SEQ - step, pltpu.roll(rows, SEQ - step, 1), 0.0)
        else:
            rows = rows + jnp.where(lane >= step, pltpu.roll(rows, step, 1), 0.0)
        step *= 2
    return rows


def columns_of(rows):
    return jnp.concatenate([rows, jnp.zeros((128 - rows.shape[0], rows.shape[1]), F32)], axis=0).T


def pieces_of(value):
    high = value.astype(LOW).astype(F32)
    middle = (value - high).astype(LOW).astype(F32)
    return high, middle, value - high - middle


def segments(i):
    return (((0, i * QB, False),) if i else ()) + ((i * QB, QB, True),)


def causal(scores):
    query = lax.broadcasted_iota(jnp.int32, (QB, QB), 0)
    key = lax.broadcasted_iota(jnp.int32, (QB, QB), 1)
    return jnp.where(key <= query, scores, neg_large)


EARLY = 2


def forward_kernel(
    params_smem, len_ref, normed_ref, wq_any, wf_ref, params_ref, wp_ref, wd_ref, gu_ref, ct_ref,
    raw_ref, q_ref, k_ref, v_ref, att_ref, col_ref, crow_ref, logit_ref, swapped_ref, projall_ref,
    down_ref, gu_first_ref, gout_ref, ct_own, wd_low, mixed_ref, wq_ref, *sems,
):
    z, x, y, c = place()
    s = pl.program_id(0)
    me = x * 4 + y * 2 + c
    swap_send, swap_recv, swap_local = sems[27:30]
    own_mixed = pltpu.make_async_copy(mixed_ref.at[x, y, c], swapped_ref.at[me], swap_local)

    def mixed_copy(d):
        peer = group_peer(d, x, y, c)[0]
        src = mixed_ref.at[peer["x"], peer["y"], peer["c"]]
        return remote(src, swapped_ref.at[me], swap_send.at[d], swap_recv.at[d], peer)

    def send_mixed(sequence):
        @pl.when(y == sequence)
        def _():
            own_mixed.start()
            for d in (4, 5, 1):
                mixed_copy(d).start()

        @pl.when(y != sequence)
        def _():
            for d in (2, 6, 3, 7):
                mixed_copy(d).start()
    length = length_of(len_ref, z, x, s)

    def piece(px, py, pc, j):
        return projall_ref.at[2 * j : 2 * j + 2, px * 4 + py * 2 + pc]

    proj = Gather(lambda j: wp_ref.at[2 * j : 2 * j + 2], piece, sems[:7], x, y, c)
    gout = Gather(lambda j: ct_own.at[j], natural(gout_ref), sems[7:14], x, y, c)
    down = LineGather(lambda h: wd_low, lambda k, h: down_ref.at[k], 1, sems[14:18], z)
    gateup = LineGather(lambda h: gu_ref.at[0:EARLY], lambda k, h: gu_first_ref.at[k], 1, sems[18:22], z)
    own_down = pltpu.make_async_copy(wd_low, down_ref.at[z], sems[22])
    own_gateup = pltpu.make_async_copy(gu_ref.at[0:EARLY], gu_first_ref.at[z], sems[23])

    fetch = pltpu.make_async_copy(wq_any, wq_ref, sems[30])

    def begin():
        fetch.start()
        greet(z, x, y, c, column=True, line=True)
        column_start(ct_ref, ct_own, *sems[24:27], z, c)
        proj.start()
        fetch.wait()
        wd_low[...] = wd_ref[...].astype(LOW)
        own_down.start()
        own_gateup.start()

    def turn():
        column_wait(ct_ref, ct_own, *sems[24:27], z, c)
        own_length = length_of(len_ref, z, x, y)
        for j in range(2):
            position = (2 * (2 * c + j) + x) * 128 + lax.broadcasted_iota(jnp.int32, (128, 1), 0)
            valid = position.astype(F32) < own_length
            ct_own[j] = jnp.where(valid, ct_own[j].astype(F32), 0.0).astype(LOW)
        gout.start()
        down.send(0)
        gateup.send(0)

    def half_way():
        send_mixed(0)
        proj.finish()

    def end():
        send_mixed(1)
        gout.finish()
        down.finish()
        gateup.finish()
        own_down.wait()
        own_gateup.wait()
        own_mixed.wait()
        for d in range(1, 8):
            mixed_copy(d).wait()

    hooks = {
        (0, 0): begin, (0, 2): proj.forward, (0, 8): proj.forward_rest, (0, 10): turn, (0, 15): half_way,
        (1, 1): lambda: down.send(1), (1, 2): gout.forward, (1, 4): lambda: gateup.send(1),
        (1, 8): gout.forward_rest, (1, 10): lambda: down.send(2), (1, 13): lambda: gateup.send(2), (1, 15): end,
    }

    def hook(n):
        for step in range(2):
            if (step, n) in hooks:
                pl.when(s == step)(hooks[step, n])

    hook(0)
    normed = normed_ref[0]
    raw = dot_nn(normed, wq_ref[...])
    raw_ref[0] = raw
    hook(1)
    q_raw, k_raw = split_halves(raw[:, : 2 * HW])
    v, gate = split_halves(raw[:, 2 * HW :])
    q = (q_raw * head_scale(q_raw) * head_gain(params_ref, False)).astype(LOW) * jnp.asarray(scale_dot, LOW)
    k = (k_raw * head_scale(k_raw) * head_gain(params_ref, True)).astype(LOW)
    v = v.astype(LOW)
    q_ref[0], k_ref[0], v_ref[0] = q, k, v
    pieces = dot_nn(normed, wf_ref[...]).T
    sub = lax.broadcasted_iota(jnp.int32, (8, 1), 0)
    bias = jnp.zeros((8, 1), F32)
    for h in range(HEADS):
        first_bias = 2 * D + 2 * HD + (x * 4 + y * 2 + c) * HEADS
        bias = jnp.where(sub == h, params_smem[first_bias + h], bias)
    logits = pieces[0:8] + pieces[8:16] + pieces[16:24] + bias
    logit_ref[0] = logits
    log_forget = jnp.minimum(logits, 0.0) - jnp.log1p(jnp.exp(-jnp.abs(logits)))
    inside = lanes(SEQ).astype(F32) < length
    crow = jnp.where(inside, running_sum(log_forget, False), -neg_large)
    crow_ref[0] = crow
    hook(2)
    for i in range(SEQ // QB):
        rows = slice(i * QB, (i + 1) * QB)
        att = jnp.zeros((QB, PAD), F32)
        for h in range(HEADS):
            mh = head_mask(h)
            qh = jnp.where(mh, q[rows], jnp.zeros((), LOW))
            parts = []
            for start, count, own in segments(i):
                keys = slice(start, start + count)
                scores = dot_nt(qh, k[keys]) - crow[h : h + 1, keys]
                parts.append((keys, causal(scores) if own else scores))
            tops = [jnp.max(scores, axis=-1, keepdims=True) for _, scores in parts]
            top = functools.reduce(jnp.maximum, tops)
            total = jnp.zeros((QB, 1), F32)
            out = jnp.zeros((QB, PAD), F32)
            for keys, scores in parts:
                p = jnp.exp(scores - top)
                total = total + jnp.sum(p, axis=-1, keepdims=True)
                out = out + dot_nn(p.astype(LOW), v[keys])
            att = jnp.where(mh, out / total, att)
            col_ref[0, rows, h : h + 1] = -(top + jnp.log(total))
            hook(3 + i * HEADS + h)
        att_ref[0, rows, :] = att
    mixed = att_ref[0] * jax.nn.sigmoid(gate)
    for cc in range(2):
        for xx in range(2):
            first, second = (mixed[(cc * 4 + 2 * j + xx) * 128 :][:128] for j in range(2))
            mixed_ref[xx, pl.ds(s, 1), cc] = join_halves(first, second).astype(LOW)[None]
    hook(15)


def seq_spec(rows, width, buffers=2):
    return pl.BlockSpec((1, rows, width), lambda s: (s, 0, 0), pipeline_mode=pl.Buffered(buffers))


def packed_spec(buffers=2):
    return pl.BlockSpec(
        (2, 1, 2, 128, 2 * HW), lambda s: (0, s, 0, 0, 0), pipeline_mode=pl.Buffered(buffers)
    )


def attention_forward(params, lens, normed, wq, wf, proj_mine, down_weight, gateup_mine, cotangent, collective_id):
    return pl.pallas_call(
        forward_kernel,
        grid=(2,),
        in_specs=[SM, VM, seq_spec(SEQ, D), ANY, VM, VM, ANY, VM, ANY, ANY],
        out_specs=[seq_spec(SEQ, 4 * HW)]
        + [seq_spec(SEQ, PAD)] * 4
        + [seq_spec(SEQ, 8), seq_spec(8, SEQ), seq_spec(8, SEQ)]
        + [ANY] * 5,
        out_shape=[shape_of((2, SEQ, 4 * HW))]
        + [shape_of((2, SEQ, PAD), LOW)] * 3
        + [shape_of((2, SEQ, PAD))]
        + [shape_of((2, SEQ, 8))]
        + [shape_of((2, 8, SEQ))] * 2
        + [shape_of((8, 128, 2 * HW), LOW), shape_of((4, 8, 48, D), LOW), shape_of((4, 128, D), LOW)]
        + [shape_of((4, EARLY, 48, 1024), LOW), shape_of((2, 2, 2, 2, 128, D), LOW)],
        scratch_shapes=[
            pltpu.VMEM((2, 128, D), LOW), pltpu.VMEM((128, D), LOW), pltpu.VMEM((2, 2, 2, 128, 2 * HW), LOW),
            pltpu.VMEM((D, 4 * HW), LOW),
        ]
        + gather_sems() * 2 + line_sems(1) * 2 + [DMA, DMA] + column_sems() + swap_sems() + [DMA],
        compiler_params=comm_params(collective_id),
        name="attention_forward",
    )(params[0], lens, normed, wq, wf, params, proj_mine, down_weight, gateup_mine, cotangent)


def ffn_kernel(
    mixed_swapped, proj_any, x_ref, params_ref, gu_mine_ref, gu_first_ref, gout_any, down_any,
    mixed_ref, middle_ref, hidden_ref, gmid_ref, gmid_low_ref, gain_out_ref, swapped_ref, gu_grad_ref, down_grad_ref,
    n2_own, n2_ref, gout_ref, down_ref, proj_ref, gu_all, ggu_ref, packed, down_part,
    land_up, land_down, *rest,
):
    bufs, sems = rest[:7], rest[7:]
    z, x, y, c = place()
    loads = [
        pltpu.make_async_copy(proj_any, proj_ref, sems[13].at[0]),
        pltpu.make_async_copy(gu_first_ref, gu_all.at[:, 0:EARLY], sems[13].at[1]),
        pltpu.make_async_copy(gu_mine_ref.at[EARLY:8], gu_all.at[z, EARLY:8], sems[13].at[2]),
        pltpu.make_async_copy(down_any, down_ref, sems[13].at[3]),
        pltpu.make_async_copy(gout_any, gout_ref, sems[13].at[4]),
    ]
    for load in loads:
        load.start()
    greet(z, x, y, c, line=True)
    line = LineGather(
        lambda h: gu_mine_ref.at[EARLY:8], lambda k, h: gu_all.at[k, EARLY:8], 1, sems[14:18], z
    )
    line.send(0)
    half = lanes(2 * HW) < HW
    for u in range(4):
        even, odd = mixed_swapped[2 * u].astype(F32), mixed_swapped[2 * u + 1].astype(F32)
        columns = slice(2 * HW * u, 2 * HW * (u + 1))
        mixed_ref[0, :, columns] = jnp.where(half, even, pltpu.roll(odd, HW, 1)).astype(LOW)
        mixed_ref[1, :, columns] = jnp.where(half, pltpu.roll(even, HW, 1), odd).astype(LOW)
    loads[0].wait()
    middle = dot_nn(mixed_ref[...].reshape(256, D), proj_ref[...]) + x_ref[...].reshape(256, D).astype(F32)
    middle_ref[...] = middle.reshape(2, 128, D)
    n2_own[...] = (middle * row_scale(middle) * params_ref[:, D : 2 * D]).astype(LOW).reshape(2, 128, D)
    gather = Gather(lambda j: n2_own.at[j], natural(n2_ref), sems[18:25], x, y, c)
    gather.start()
    line.send(1)
    gather.forward()
    line.send(2)
    gather.forward_rest()
    gather.finish()
    line.finish()
    for load in loads[1:]:
        load.wait()
    down_grads = LineReduce(down_part, lambda h: (), 1, land_up, land_down, sems[9:13], z)
    gu_ref = gu_all
    def product(px, py, pc):
        rows = n2_ref[py, pc, :, px].reshape(256, D)
        gateup = dot_nn(rows, gu_ref[...].reshape(D, 1024))
        gate, up = gateup[:, :512], gateup[:, 512:]
        s = jax.nn.sigmoid(gate)
        silu = gate * s
        hidden_ref[py, pc, :, px] = (silu * up).astype(LOW).reshape(2, 128, 512)
        grad_hidden = dot_nt(gout_ref[py, pc, :, px].reshape(256, D), down_ref[...])
        by_gate = grad_hidden * up * (s + silu * (1.0 - s))
        grads = jnp.concatenate([by_gate, grad_hidden * silu], axis=1).astype(LOW)
        ggu_ref[py, pc, :, px] = grads.reshape(2, 128, 1024)
        return dot_nt(grads, gu_ref[...].reshape(D, 1024)).reshape(2, 128, D)

    scatter = Scatter(product, bufs, sems[:6], x, y, c)
    for k in range(4):
        scatter.to_partner(k)
        scatter.close(k)
    tokens = 2 * SEQ
    for d in (3, 0, 2, 1):
        columns = hidden_ref[:, :, :, :, :, d * 128 : d * 128 + 128].reshape(tokens, 128)
        down_part[d] = dot_tn(columns, gout_ref[...].reshape(tokens, D)).astype(LOW)
    down_grads.phase(0)


    def gateup_grads(d):
        rows = n2_ref[:, :, :, :, :, d * 384 : d * 384 + 384].reshape(tokens, 384)
        grads = dot_tn(rows, ggu_ref[...].reshape(tokens, 1024))
        gu_grad_ref[d] = grads.astype(LOW).reshape(8, 48, 1024)

    gateup_grads(0)
    halves = scatter.result()
    down_grads.phase(1)
    gain_grad = jnp.zeros((1, D), F32)
    for j in range(2):
        by_middle, by_gain = norm_back(halves[j], middle_ref[j], params_ref[:, D : 2 * D])
        gain_grad = gain_grad + by_gain
        grad = gout_ref[y, c, j, x].astype(F32) + by_middle
        gmid_ref[j] = grad
        gmid_low_ref[j] = grad.astype(LOW)
    gain_out_ref[...] = gain_grad
    down_grads.phase(2)
    mixed = dot_nt(gmid_low_ref[...].reshape(256, D), proj_ref[...])
    for u in range(4):
        columns = slice(2 * HW * u, 2 * HW * (u + 1))
        a0, a1 = mixed[:128, columns], mixed[128:, columns]
        packed[2 * u] = jnp.where(half, a0, pltpu.roll(a1, HW, 1)).astype(LOW)
        packed[2 * u + 1] = jnp.where(half, pltpu.roll(a0, HW, 1), a1).astype(LOW)
    swapping = swap_start(packed, swapped_ref, *sems[6:9], x, y, c)
    for d in range(1, 4):
        gateup_grads(d)
    down_grads.phase(3)
    swap_wait(swapping)
    down_grads.finish()
    down_grad_ref[...] = down_part[pl.ds(z, 1)][0]


def ffn_layer(mixed_swapped, proj_full, x, params, gateup_mine, gu_first, gout, down_t, collective_id):
    return pl.pallas_call(
        ffn_kernel,
        out_shape=[
            shape_of((2, 128, D), LOW),
            shape_of((2, 128, D)),
            shape_of((2, 2, 2, 2, 128, 512), LOW),
            shape_of((2, 128, D)),
            shape_of((2, 128, D), LOW),
            shape_of((1, D)),
            shape_of((8, 128, 2 * HW), LOW),
            shape_of((4, 8, 48, 1024), LOW),
            shape_of((128, D), LOW),
        ],
        in_specs=[VM, ANY, VM, VM] + [ANY] * 4,
        out_specs=[VM] * 6 + [ANY] + [VM] * 2,
        scratch_shapes=[
            pltpu.VMEM((2, 128, D), LOW),
            pltpu.VMEM((2, 2, 2, 2, 128, D), LOW), pltpu.VMEM((2, 2, 2, 2, 128, D), LOW),
            pltpu.VMEM((512, D), LOW), pltpu.VMEM((D, D), LOW), pltpu.VMEM((4, 8, 48, 1024), LOW),
            pltpu.VMEM((2, 2, 2, 2, 128, 1024), LOW), pltpu.VMEM((8, 128, 2 * HW), LOW),
            pltpu.VMEM((4, 128, D), LOW), pltpu.VMEM((3, 128, D), LOW), pltpu.VMEM((3, 128, D), LOW),
        ]
        + scatter_scratch(128, D) + scatter_sems() + swap_sems() + line_sems(1) + [DMA((5,))]
        + line_sems(1) + gather_sems(),
        compiler_params=comm_params(collective_id),
        name="ffn_layer",
    )(mixed_swapped, proj_full, x, params, gateup_mine, gu_first, gout, down_t)


def backward_kernel(
    gmix_ref, raw_ref, q_ref, k_ref, v_ref, att_ref, col_ref, crow_ref, logit_ref,
    params_ref, hidden_ref, down_ref, middle_ref, gu_grad_ref, mixed_ref, gmid_low_ref,
    gp_ref, gains_ref, bias_ref, result_ref, gu_out_ref, proj_out_ref,
    do, dq, dk, dv, grow, gcol, gu_part, land_up, land_down, proj_part, *rest,
):
    bufs, more, sems = rest[:7], rest[7:14], rest[14:]
    z, x, y, c = place()
    s = pl.program_id(0)

    def product(px, py, pc):
        return dot_nn(hidden_ref[py, pc, :, px].reshape(256, 512), down_ref[...]).reshape(2, 128, D)

    def proj_product(px, py, pc):
        return proj_part[:, px * 4 + py * 2 + pc].reshape(2, 96, D).astype(F32)

    output = Scatter(product, bufs, sems[0:6], x, y, c)
    proj = Scatter(proj_product, more, sems[6:12], x, y, c)
    gu_grads = LineReduce(gu_part, lambda h: (slice(4 * h, 4 * h + 4),), 2, land_up, land_down, sems[12:16], z)
    load = pltpu.make_async_copy(gu_grad_ref, gu_part, sems[16])
    store = pltpu.make_async_copy(gu_part.at[z], gu_out_ref, sems[16])
    def begin():
        load.start()
        greet(z, x, y, c, line=True)
        load.wait()
        gu_grads.phase(0)
        for d in range(4):
            columns = mixed_ref[:, :, d * 384 : d * 384 + 384].reshape(256, 384)
            grads = dot_tn(columns, gmid_low_ref[...].reshape(256, D))
            proj_part[d] = grads.astype(LOW).reshape(8, 48, D)
        proj.stage(0)

    def proj_end():
        first, second = proj.result()
        proj_out_ref[0:2] = first.astype(LOW).reshape(2, 48, D)
        proj_out_ref[2:4] = second.astype(LOW).reshape(2, 48, D)

    def end():
        first, second = output.result()
        for j, half in enumerate((first, second)):
            result_ref[j] = (middle_ref[j] + half).astype(LOW)
        gu_grads.phase(3)
        store.start()
        gu_grads.finish()
        store.wait()

    hooks = {
        (0, 0): begin, (0, 1): lambda: proj.stage(1), (0, 2): lambda: proj.stage(2), (0, 3): lambda: proj.stage(3),
        (0, 4): lambda: output.stage(0), (0, 5): lambda: output.stage(1), (0, 6): lambda: gu_grads.phase(1, (0,)),
        (0, 7): lambda: proj.stage(4), (0, 8): lambda: output.stage(2), (0, 9): lambda: output.stage(3),
        (0, 11): lambda: gu_grads.phase(1, (1,)), (0, 13): proj_end,
        (1, 1): lambda: gu_grads.phase(2, (0,)), (1, 3): lambda: output.stage(4),
        (1, 6): lambda: gu_grads.phase(2, (1,)), (1, 13): end,
    }

    def hook(n):
        for step in range(2):
            if (step, n) in hooks:
                pl.when(s == step)(hooks[step, n])

    hook(0)
    for cc in range(2):
        for xx in range(2):
            halves = split_halves(gmix_ref[xx, 0, cc].astype(F32))
            for j in range(2):
                dq[pl.ds((cc * 4 + 2 * j + xx) * 128, 128)] = halves[j]
    _, gate = split_halves(raw_ref[0, :, 2 * HW :])
    gate = jax.nn.sigmoid(gate)
    do[...] = (dq[...] * gate).astype(LOW)
    grad_gate = dq[...] * att_ref[0] * gate * (1.0 - gate)
    dk[...] = jnp.zeros_like(dk)
    dv[...] = jnp.zeros_like(dv)
    grow[...] = jnp.zeros_like(grow)
    for i in range(SEQ // QB):
        rows = slice(i * QB, (i + 1) * QB)
        q, grad = q_ref[0, rows], do[rows]
        delta_all = head_sums(grad.astype(F32) * att_ref[0, rows])
        grad_q = jnp.zeros((QB, PAD), F32)
        for h in range(HEADS):
            mh = head_mask(h)
            qh = jnp.where(mh, q, jnp.zeros((), LOW))
            gh = jnp.where(mh, grad, jnp.zeros((), LOW))
            delta = delta_all[:, h * HD : h * HD + 1]
            by_query = jnp.zeros((QB, PAD), F32)
            by_row = jnp.zeros((1, QB), F32)
            for start, count, own in segments(i):
                keys = slice(start, start + count)
                k, v = k_ref[0, keys], v_ref[0, keys]
                ones = jnp.ones((8, count), LOW)
                scores = dot_nt(qh, k) - crow_ref[0, h : h + 1, keys] + col_ref[0, rows, h : h + 1]
                p = jnp.exp(causal(scores) if own else scores)
                ds = (p * (dot_nt(gh, v) - delta)).astype(LOW)
                by_query = by_query + dot_nn(ds, k)
                dk[keys] += dot_tn(ds, qh)
                dv[keys] += dot_tn(p.astype(LOW), gh)
                by_row = by_row + dot_nt(ones, ds)[:1]
                grow[h : h + 1, keys] += dot_nn(ones[:, :QB], ds)[:1]
            grad_q = jnp.where(mh, by_query, grad_q)
            gcol[h : h + 1, rows] = by_row
            hook(1 + i * HEADS + h)
        dq[rows] = grad_q * scale_dot
    q_raw, k_raw = split_halves(raw_ref[0, :, : 2 * HW])
    q_grad, q_gain = head_norm_back(dq[...], q_raw, head_gain(params_ref, False))
    k_grad, k_gain = head_norm_back(dk[...], k_raw, head_gain(params_ref, True))
    gp_ref[0, :, : 2 * HW] = join_halves(q_grad, k_grad).astype(LOW)
    gp_ref[0, :, 2 * HW : 4 * HW] = join_halves(dv[...], grad_gate).astype(LOW)
    gains_ref[0] = jnp.concatenate([q_gain, k_gain, jnp.zeros((6, PAD), F32)], axis=0)
    head = lax.broadcasted_iota(jnp.int32, (8, SEQ), 0) < HEADS
    change = jnp.where(head, gcol[...] - grow[...], 0.0)
    logits = logit_ref[0]
    grad_logits = running_sum(change, True) * jax.nn.sigmoid(-logits)
    bias_ref[0] = jnp.broadcast_to(jnp.sum(grad_logits, axis=1, keepdims=True), (8, 128))
    parts = pieces_of(grad_logits)
    gp_ref[0, :, 4 * HW :] = columns_of(jnp.concatenate([parts[a] for a, _ in PAIRS], axis=0)).astype(LOW)
    hook(13)


def attention_backward(
    gmix, raw, q, k, v, att, col, crow, logits, params, hidden, down_t, middle, gu_grad,
    mixed, gmid_low, collective_id,
):
    return pl.pallas_call(
        backward_kernel,
        grid=(2,),
        in_specs=[packed_spec(1), seq_spec(SEQ, 4 * HW, 1)]
        + [seq_spec(SEQ, PAD, 1)] * 4
        + [seq_spec(SEQ, 8, 1), seq_spec(8, SEQ), seq_spec(8, SEQ)]
        + [VM, VM, VM, VM, ANY, VM, VM],
        out_specs=[seq_spec(SEQ, 4 * HW + 128, 1), seq_spec(8, PAD), seq_spec(8, 128), VM, ANY, VM],
        scratch_shapes=[pltpu.VMEM((SEQ, PAD), LOW)]
        + [pltpu.VMEM((SEQ, PAD), F32)] * 3
        + [pltpu.VMEM((8, SEQ), F32)] * 2
        + [pltpu.VMEM((4, 8, 48, 1024), LOW)]
        + [pltpu.VMEM((3, 8, 48, 1024), LOW)] * 2
        + [pltpu.VMEM((4, 8, 48, D), LOW)]
        + scatter_scratch(128, D) + scatter_scratch(96, D)
        + scatter_sems() * 2 + line_sems(2) + [DMA],
        out_shape=[
            shape_of((2, SEQ, 4 * HW + 128), LOW), shape_of((2, 8, PAD)), shape_of((2, 8, 128)),
            shape_of((2, 128, D), LOW), shape_of((8, 48, 1024), LOW), shape_of((4, 48, D), LOW),
        ],
        compiler_params=comm_params(collective_id),
        name="attention_backward",
    )(
        gmix, raw, q, k, v, att, col, crow, logits, params, hidden, down_t, middle, gu_grad,
        mixed, gmid_low,
    )


def close_kernel(
    gp_any, normed_any, wq_any, wf_ref, x_ref, params_ref, gmid_ref, gu_ref, result_ref,
    gains_ref, bias_ref, ffn_gain_ref,
    grad_ref, out_ref, small_ref, q_out_ref, gu_out_ref,
    gp_ref, normed_ref, wq_ref, grad_own, q_part, land_up, land_down, forget, small, zbuf, zsum, *rest,
):
    bufs, sems = rest[:7], rest[7:]
    z, x, y, c = place()
    t = x * 4 + y * 2 + c
    loads = [
        pltpu.make_async_copy(gp_any, gp_ref, sems[20].at[0]),
        pltpu.make_async_copy(normed_any, normed_ref, sems[20].at[1]),
        pltpu.make_async_copy(wq_any, wq_ref, sems[20].at[2]),
    ]
    for load in loads:
        load.start()
    greet(z, x, y, c, column=True, line=True, plane=True)
    column_start(result_ref, out_ref, *sems[21:24], z, c)
    tokens = 2 * SEQ

    def product(px, py, pc):
        rows = gp_ref[py, pc, :, px].reshape(256, 4 * HW + 128)
        part = dot_nt(rows[:, : 4 * HW], wq_ref[...]) + dot_nt(rows[:, 4 * HW :], wf_ref[...])
        return part.reshape(2, 128, D)

    grads = Scatter(product, bufs, sems[0:6], x, y, c)
    line = LineReduce(q_part, lambda h: (slice(4 * h, 4 * h + 4),), 2, land_up, land_down, sems[9:13], z)

    def weight_grads(d):
        columns = normed_ref[:, :, :, :, :, d * 384 : d * 384 + 384].reshape(tokens, 384)
        part = dot_tn(columns, gp_ref[...].reshape(tokens, 4 * HW + 128))
        q_part[d] = part[:, : 4 * HW].astype(LOW).reshape(8, 48, 4 * HW)
        forget[d * 384 : d * 384 + 384] = part[:, 4 * HW :]

    for load in loads:
        load.wait()
    grads.stage(0)
    grads.stage(1)
    weight_grads(3)
    weight_grads(0)
    line.begin(0)
    grads.stage(2)
    weight_grads(2)
    weight_grads(1)
    line.begin(1)
    line.begin(2)
    grads.stage(3)
    grads.stage(4)
    gu_swap = swap_start(gu_ref, gu_out_ref, *sems[6:9], x, y, c)
    line.phase(1)
    line.phase(2)
    lane = lanes(D)
    rows = forget[...].T
    rows = rows[0:8] + rows[24:32] + rows[40:48]
    heads = gains_ref[0] + gains_ref[1]
    heads = heads + pltpu.roll(heads, 3 * HD, 1) + pltpu.roll(heads, 2 * HD, 1)
    heads = jnp.concatenate([heads, jnp.zeros((8, D - PAD), F32)], axis=1)
    bias = bias_ref[0] + bias_ref[1]
    gains = jnp.where(lane < HD, heads[0:1], 0.0)
    gains = jnp.where((lane >= HD) & (lane < 2 * HD), pltpu.roll(heads, HD, 1)[1:2], gains)
    for h in range(HEADS):
        gains = jnp.where(lane == 2 * HD + t * HEADS + h, bias[h : h + 1, :1], gains)
    small[0:1] = jnp.zeros((1, D), F32)
    small[1:2] = ffn_gain_ref[...]
    small[2:3] = gains
    for h in range(HEADS):
        small[3 + h : 4 + h] = rows[h : h + 1]
    small[6:8] = jnp.zeros((2, D), F32)
    first, second = grads.result()
    gain_grad = jnp.zeros((1, D), F32)
    for j, grad in enumerate((first, second)):
        by_inputs, by_gain = norm_back(grad, x_ref[j].astype(F32), params_ref[:, :D])
        gain_grad = gain_grad + by_gain
        grad_own[j] = (gmid_ref[j] + by_inputs).astype(LOW)
    column_start(grad_own, grad_ref, *sems[13:16], z, c)
    small[0:1] = gain_grad
    exchange_total(small, zbuf, zsum, small_ref, sems[16:20], z, x, y, c)
    swap_wait(gu_swap)
    line.phase(3)
    q_out_ref[...] = q_part[pl.ds(z, 1)][0]
    column_wait(result_ref, out_ref, *sems[21:24], z, c)
    column_wait(grad_own, grad_ref, *sems[13:16], z, c)
    line.finish()


def close_layer(
    gp, normed, wq, wf, x, params, gmid, gu_grad, result, head_gains, bias_sums, ffn_gain, collective_id
):
    return pl.pallas_call(
        close_kernel,
        out_shape=[
            shape_of((2, 128, D), LOW), shape_of((2, 128, D), LOW), shape_of((8, 8, D)),
            shape_of((8, 48, 4 * HW), LOW), shape_of((8, 48, 1024), LOW),
        ],
        in_specs=[ANY] * 3 + [VM] * 4 + [ANY, ANY] + [VM] * 3,
        out_specs=[ANY, ANY, VM, VM, ANY],
        scratch_shapes=[
            pltpu.VMEM((2, 2, 2, 2, 128, 4 * HW + 128), LOW), pltpu.VMEM((2, 2, 2, 2, 128, D), LOW),
            pltpu.VMEM((D, 4 * HW), LOW),
            pltpu.VMEM((2, 128, D), LOW), pltpu.VMEM((4, 8, 48, 4 * HW), LOW),
            pltpu.VMEM((3, 8, 48, 4 * HW), LOW), pltpu.VMEM((3, 8, 48, 4 * HW), LOW),
            pltpu.VMEM((D, 128), F32), pltpu.VMEM((8, D), F32), pltpu.VMEM((4, 8, D), F32), pltpu.VMEM((8, D), F32),
        ]
        + scatter_scratch(128, D)
        + scatter_sems() + swap_sems() + line_sems(2) + column_sems() + exchange_sems() + [DMA((3,))] + column_sems(),
        compiler_params=comm_params(collective_id),
        name="close_layer",
    )(gp, normed, wq, wf, x, params, gmid, gu_grad, result, head_gains, bias_sums, ffn_gain)


def fast_device(
    block_input,
    cotangent,
    lengths,
    qkvo_weight,
    proj_weight,
    gateup_weight,
    down_weight,
    forget_weight,
    norm_params,
    qkvo_mean,
    qkvo_square,
    proj_mean,
    proj_square,
    gateup_mean,
    gateup_square,
    down_mean,
    down_square,
    forget_mean,
    forget_square,
    params_mean,
    params_square,
):
    rate_proj = rate_dense * (D / max(D // 256, 2)) ** 0.5
    params = norm_params.reshape(1, -1)
    x_own, lens, normed_all, qkvo_t, gateup_mine, forget_cols, proj_mine = open_layer(
        block_input, lengths, params, forget_weight.T, qkvo_weight, gateup_weight, proj_weight, 1
    )
    qkvo_t = qkvo_t.reshape(D, 4 * HW)
    raw, q, k, v, att, col, crow, logits, mixed_swapped, proj_full, down_t, gu_first, gout_all = attention_forward(
        params, lens, normed_all.reshape(2, SEQ, D), qkvo_t, forget_cols, proj_mine, down_weight, gateup_mine,
        cotangent, 2,
    )
    proj_full, down_t = proj_full.reshape(D, D), down_t.reshape(512, D)
    mixed, middle, hidden, gmid, gmid_low, ffn_gain, gmix, gateup_part, down_shard = ffn_layer(
        mixed_swapped, proj_full, x_own, params, gateup_mine, gu_first, gout_all, down_t, 3
    )
    gp, head_gains, bias_sums, result, gateup_part, proj_part = attention_backward(
        gmix.reshape(2, 2, 2, 128, 2 * HW), raw, q, k, v, att, col, crow, logits,
        params, hidden, down_t, middle, gateup_part, mixed, gmid_low, 4,
    )
    input_grad, block_output, small, qkvo_part, gateup_part = close_layer(
        gp.reshape(2, 2, 2, 2, 128, 4 * HW + 128), normed_all, qkvo_t, forget_cols, x_own, params, gmid,
        gateup_part, result, head_gains, bias_sums, ffn_gain, 5,
    )
    qkvo_shard, gateup_shard, proj_shard, norm = norm_layer(
        qkvo_part, gateup_part, proj_part, down_shard, small, 6
    )
    updates = adam_layer(
        (rate_proj, rate_dense, rate_dense, rate_dense),
        norm,
        small,
        input_grad,
        block_output,
        (proj_shard, down_shard, qkvo_shard, gateup_shard),
        (
            proj_weight, proj_mean, proj_square, down_weight, down_mean, down_square,
            qkvo_weight, qkvo_mean, qkvo_square, gateup_weight, gateup_mean, gateup_square,
        ),
        (
            forget_weight.T, forget_mean.T, forget_square.T,
            norm_params, params_mean, params_square,
        ),
    )
    input_grad, block_output, grad_norm, *updates = updates
    proj_new, down_new, qkvo_new, gateup_new = (updates[i : i + 3] for i in (0, 3, 6, 9))
    forget_new = [value.T for value in updates[12:15]]
    params_new = updates[15:18]
    return (
        block_output, input_grad, grad_norm.reshape(()),
        *qkvo_new, *proj_new, *gateup_new, *down_new, *forget_new, *params_new,
    )


def solution(mesh):
    seq_size, dp_size = mesh.shape["seq"], mesh.shape["dp"]
    if (seq_size, dp_size) == (8, 4):
        inner = Mesh(mesh.devices.reshape(4, 2, 2, 2), ("z", "x", "y", "c"))
        seq, dp = ("z", "x"), ("y", "c")
        device_function = fast_device
    else:
        inner, seq, dp = mesh, ("seq",), ("dp",)
        device_function = general_device
    tokens, rows, copied = P(dp, seq, None), P(seq + dp, None), P()
    return jax.shard_map(
        device_function,
        mesh=inner,
        in_specs=(tokens, tokens, P(dp)) + (rows,) * 4 + (copied,) * 2 + (rows,) * 8 + (copied,) * 4,
        out_specs=(tokens, tokens, copied) + (rows,) * 12 + (copied,) * 6,
        check_vma=False,
    )
```

```python
import functools

import jax
import jax.numpy as jnp
from jax import lax
from jax.experimental import pallas as pl
from jax.experimental.pallas import tpu as pltpu
from jax.sharding import Mesh
from jax.sharding import PartitionSpec as P

D = 1536
H = 24
HD = 64
FF = 4096
STEP = 10


eps_norm = 1e-06
beta_one = 0.9
beta_two = 0.95
rate_dense = 0.06
rate_small = 0.6
decay_dense = 0.1
adam_eps = 1e-08
neg_large = -1e30
highest = lax.Precision.HIGHEST


def entering(value, axis, join, neutral, backward):
    count, mine = (lax.axis_size(axis), lax.axis_index(axis))
    pieces = lax.all_gather(value, axis)
    if backward:
        pieces = pieces[::-1]
        mine = count - 1 - mine
    running = jnp.full_like(value, 0) + jnp.asarray(neutral, value.dtype)

    def hop(position, running):
        longer = join(running, pieces[position])
        return jnp.where(position < mine, longer, running)

    return lax.fori_loop(0, count - 1, hop, running)


def rms_scale(values, gain_vec):
    return (
        values * lax.rsqrt(jnp.mean(values * values, axis=-1, keepdims=True) + eps_norm) * gain_vec
    )


def heads_in(projected, logits, gain_query, gain_key):
    token_count = projected.shape[0]
    query_raw, key_raw, value_raw, gate_raw = jnp.split(projected, 4, axis=1)
    queries = rms_scale(query_raw.reshape(token_count, H, HD), gain_query)
    keys_out = rms_scale(key_raw.reshape(token_count, H, HD), gain_key)
    return (
        queries,
        keys_out,
        value_raw.reshape(token_count, H, HD),
        jax.nn.sigmoid(gate_raw),
        jax.nn.log_sigmoid(logits),
    )


def swiglu(gateup):
    return jax.nn.silu(gateup[:, :FF]) * gateup[:, FF:]


def add_terms(earlier, later):
    return earlier + later


def contract_rows(left, right):
    return lax.dot_general(
        left, right, (((0,), (0,)), ((), ())), preferred_element_type=jnp.float32
    )


def contract_cols(left, right):
    return lax.dot_general(
        left, right, (((1,), (1,)), ((), ())), preferred_element_type=jnp.float32
    )


def sub_width(piece_len, block_len):
    pieces = piece_len // block_len
    group_size = 1
    while group_size * 2 * block_len <= 256 and pieces % (group_size * 2) == 0:
        group_size = group_size * 2
    return group_size * block_len


def scores_of(query_part, key_part, cumul_query, cumul_key):
    raw_dots = jnp.einsum(
        "rqhd,rkhd->rhqk", query_part, key_part, preferred_element_type=jnp.float32
    )
    return raw_dots * HD ** (-0.5) + cumul_query[:, :, :, None] - cumul_key[:, :, None, :]


def allowed_of(query_pos, key_pos, lengths):
    causal = key_pos[None, None, :] <= query_pos[None, :, None]
    inside = key_pos[None, None, :] < lengths[:, None, None]
    return (causal & inside)[:, None]


def adam_update(weight, gradient, mean_old, square_old, learn_rate, decay_rate):
    mean_new = beta_one * mean_old + (1.0 - beta_one) * gradient
    square_new = beta_two * square_old + (1.0 - beta_two) * gradient * gradient
    moved = (
        mean_new
        / (1.0 - beta_one**STEP)
        / (jnp.sqrt(square_new / (1.0 - beta_two**STEP)) + adam_eps)
    )
    return (weight - learn_rate * (moved + decay_rate * weight), mean_new, square_new)


def general_device(
    block_input,
    cotangent,
    lengths,
    qkvo_weight,
    proj_weight,
    gateup_weight,
    down_weight,
    forget_weight,
    norm_params,
    qkvo_mean,
    qkvo_square,
    proj_mean,
    proj_square,
    gateup_mean,
    gateup_square,
    down_mean,
    down_square,
    forget_mean,
    forget_square,
    params_mean,
    params_square,
):
    rows_here = block_input.shape[0]
    block_len = block_input.shape[1]
    token_count = rows_here * block_len
    cycle_index = lax.axis_index("seq")
    my_start = cycle_index * block_len
    positions = my_start + jnp.arange(block_len, dtype=jnp.int32)
    last_pos = my_start + block_len - 1
    longest = jnp.max(lengths)
    head_shape = (rows_here, block_len, H, HD)
    scale_dot = HD ** (-0.5)
    rate_proj = rate_dense * (D / max(D // 256, 2)) ** 0.5
    qkvo_full, proj_full, gateup_full, down_full = (
        lax.all_gather(qkvo_weight.astype(jnp.bfloat16), ("seq", "dp"), axis=0, tiled=True),
        lax.all_gather(proj_weight.astype(jnp.bfloat16), ("seq", "dp"), axis=0, tiled=True),
        lax.all_gather(gateup_weight.astype(jnp.bfloat16), ("seq", "dp"), axis=0, tiled=True),
        lax.all_gather(down_weight.astype(jnp.bfloat16), ("seq", "dp"), axis=0, tiled=True),
    )
    gain_attn = norm_params[:D]
    gain_ffn = norm_params[D : 2 * D]
    gain_query = norm_params[2 * D : 2 * D + HD]
    gain_key = norm_params[2 * D + HD : 2 * D + 2 * HD]
    bias_forget = norm_params[2 * D + 2 * HD :]
    inputs = block_input.astype(jnp.float32).reshape(token_count, D)
    normed, norm_pull = jax.vjp(rms_scale, inputs, gain_attn)
    normed_low = normed.astype(jnp.bfloat16)
    normed_back = normed_low.astype(jnp.float32)
    projected = jnp.dot(normed_low, qkvo_full, preferred_element_type=jnp.float32)
    logits = jnp.dot(normed_back, forget_weight, precision=highest) + bias_forget
    head_values, heads_pull = jax.vjp(heads_in, projected, logits, gain_query, gain_key)
    queries, keys_out, values_out, outgate, log_forget = head_values
    query_low = queries.astype(jnp.bfloat16).reshape(head_shape)
    key_low = keys_out.astype(jnp.bfloat16).reshape(head_shape)
    value_low = values_out.astype(jnp.bfloat16).reshape(head_shape)
    local_cumul = jnp.cumsum(log_forget.reshape(rows_here, block_len, H), axis=1)
    offset = entering(
        local_cumul[:, -1, :], "seq", add_terms, jnp.zeros((rows_here, H), jnp.float32), False
    )
    cumul = local_cumul + offset[:, None, :]
    cumul_all = lax.all_gather(cumul, "seq", axis=1, tiled=True)
    cumul_own = cumul.transpose(0, 2, 1)
    start_state = (
        jnp.full((rows_here, H, block_len), neg_large, jnp.float32),
        jnp.zeros((rows_here, H, block_len), jnp.float32),
        jnp.zeros((rows_here, H, block_len, HD), jnp.float32),
    )
    key_piece = lax.all_gather(key_low, "seq", axis=1, tiled=True)
    value_piece = lax.all_gather(value_low, "seq", axis=1, tiled=True)
    piece_len = key_piece.shape[1]
    sub_len = sub_width(piece_len, block_len)

    def forward_update(sub_index, state_now):
        key_start = sub_index * sub_len

        def forward_compute(state_run):
            run_max, run_sum, run_acc = state_run
            key_block = lax.dynamic_slice_in_dim(key_piece, sub_index * sub_len, sub_len, 1)
            value_block = lax.dynamic_slice_in_dim(value_piece, sub_index * sub_len, sub_len, 1)
            cumul_block = lax.dynamic_slice_in_dim(cumul_all, key_start, sub_len, 1).transpose(
                0, 2, 1
            )
            key_pos = key_start + jnp.arange(sub_len, dtype=jnp.int32)
            allowed = allowed_of(positions, key_pos, lengths)
            scores = jnp.where(
                allowed, scores_of(query_low, key_block, cumul_own, cumul_block), neg_large
            )
            new_max = jnp.maximum(run_max, jnp.max(scores, axis=-1))
            factor = jnp.exp(run_max - new_max)
            attn_probs = jnp.where(allowed, jnp.exp(scores - new_max[..., None]), 0.0)
            run_sum = run_sum * factor + jnp.sum(attn_probs, axis=-1)
            run_acc = run_acc * factor[..., None] + jnp.einsum(
                "rhqk,rkhd->rhqd",
                attn_probs.astype(jnp.bfloat16),
                value_block,
                preferred_element_type=jnp.float32,
            )
            return (new_max, run_sum, run_acc)

        is_live = (key_start <= last_pos) & (key_start < longest)
        return lax.cond(is_live, forward_compute, lambda state_run: state_run, state_now)

    run_max, run_sum, run_acc = lax.fori_loop(0, piece_len // sub_len, forward_update, start_state)
    attended = run_acc / run_sum[..., None]
    log_total = run_max + jnp.log(run_sum)
    attended_rows = attended.transpose(0, 2, 1, 3).reshape(token_count, D)
    mixed_low = (attended_rows * outgate).astype(jnp.bfloat16)
    middle = inputs + jnp.dot(mixed_low, proj_full, preferred_element_type=jnp.float32)
    normed_two, norm_two_pull = jax.vjp(rms_scale, middle, gain_ffn)
    normed_two_low = normed_two.astype(jnp.bfloat16)
    gateup = jnp.dot(normed_two_low, gateup_full, preferred_element_type=jnp.float32)
    hidden, swiglu_pull = jax.vjp(swiglu, gateup)
    hidden_low = hidden.astype(jnp.bfloat16)
    result = middle + jnp.dot(hidden_low, down_full, preferred_element_type=jnp.float32)
    block_output = result.astype(jnp.bfloat16).reshape(rows_here, block_len, D)
    valid = (positions[None, :] < lengths[:, None]).astype(jnp.float32)
    grad_out = (cotangent.astype(jnp.float32) * valid[:, :, None]).reshape(token_count, D)
    grad_out_low = grad_out.astype(jnp.bfloat16)
    grad_down_w = contract_rows(hidden_low, grad_out_low)
    grad_hidden = contract_cols(grad_out_low, down_full)
    grad_gateup_low = swiglu_pull(grad_hidden)[0].astype(jnp.bfloat16)
    grad_gateup_w = contract_rows(normed_two_low, grad_gateup_low)
    grad_normed_two = contract_cols(grad_gateup_low, gateup_full)
    grad_middle_part, grad_gain_ffn = norm_two_pull(grad_normed_two)
    grad_middle = grad_out + grad_middle_part
    grad_middle_low = grad_middle.astype(jnp.bfloat16)
    grad_proj_w = contract_rows(mixed_low, grad_middle_low)
    grad_mixed = contract_cols(grad_middle_low, proj_full)
    grad_outgate = grad_mixed * attended_rows
    grad_att_low = (grad_mixed * outgate).astype(jnp.bfloat16).reshape(head_shape)
    delta = jnp.sum(
        grad_att_low.astype(jnp.float32) * attended.transpose(0, 2, 1, 3), axis=-1
    ).transpose(0, 2, 1)
    lse_all, delta_all = (
        lax.all_gather(log_total, "seq", axis=2, tiled=True),
        lax.all_gather(delta, "seq", axis=2, tiled=True),
    )
    query_state = (
        jnp.zeros((rows_here, H, block_len, HD), jnp.float32),
        jnp.zeros((rows_here, H, block_len), jnp.float32),
    )
    query_key_piece = lax.all_gather(key_low, "seq", axis=1, tiled=True)
    query_value_piece = lax.all_gather(value_low, "seq", axis=1, tiled=True)
    piece_len = query_key_piece.shape[1]
    query_sub_len = sub_width(piece_len, block_len)

    def query_update(sub_index, state_now):
        key_start = sub_index * query_sub_len

        def query_compute(state_run):
            grad_query, grad_cq = state_run
            key_block = lax.dynamic_slice_in_dim(
                query_key_piece, sub_index * query_sub_len, query_sub_len, 1
            )
            value_block = lax.dynamic_slice_in_dim(
                query_value_piece, sub_index * query_sub_len, query_sub_len, 1
            )
            cumul_block = lax.dynamic_slice_in_dim(
                cumul_all, key_start, query_sub_len, 1
            ).transpose(0, 2, 1)
            key_pos = key_start + jnp.arange(query_sub_len, dtype=jnp.int32)
            allowed = allowed_of(positions, key_pos, lengths)
            scores = jnp.where(
                allowed, scores_of(query_low, key_block, cumul_own, cumul_block), neg_large
            )
            attn_probs = jnp.where(allowed, jnp.exp(scores - log_total[..., None]), 0.0)
            grad_probs = jnp.einsum(
                "rqhd,rkhd->rhqk", grad_att_low, value_block, preferred_element_type=jnp.float32
            )
            scores_low = (attn_probs * (grad_probs - delta[..., None])).astype(jnp.bfloat16)
            grad_query = (
                grad_query
                + jnp.einsum(
                    "rhqk,rkhd->rhqd", scores_low, key_block, preferred_element_type=jnp.float32
                )
                * scale_dot
            )
            grad_cq = grad_cq + jnp.sum(scores_low.astype(jnp.float32), axis=-1)
            return (grad_query, grad_cq)

        is_live = (key_start <= last_pos) & (key_start < longest)
        return lax.cond(is_live, query_compute, lambda state_run: state_run, state_now)

    grad_query, grad_cq = lax.fori_loop(0, piece_len // query_sub_len, query_update, query_state)
    key_state = (
        jnp.zeros((rows_here, H, block_len, HD), jnp.float32),
        jnp.zeros((rows_here, H, block_len, HD), jnp.float32),
        jnp.zeros((rows_here, H, block_len), jnp.float32),
    )
    query_piece = lax.all_gather(query_low, "seq", axis=1, tiled=True)
    dout_piece = lax.all_gather(grad_att_low, "seq", axis=1, tiled=True)
    piece_len = query_piece.shape[1]
    key_sub_len = sub_width(piece_len, block_len)

    def key_update(sub_index, state_now):
        query_start = sub_index * key_sub_len

        def key_compute(state_run):
            grad_key, grad_value, grad_ck = state_run
            query_block = lax.dynamic_slice_in_dim(
                query_piece, sub_index * key_sub_len, key_sub_len, 1
            )
            dout_block = lax.dynamic_slice_in_dim(
                dout_piece, sub_index * key_sub_len, key_sub_len, 1
            )
            lse_block = lax.dynamic_slice_in_dim(lse_all, query_start, key_sub_len, 2)
            delta_block = lax.dynamic_slice_in_dim(delta_all, query_start, key_sub_len, 2)
            cumul_block = lax.dynamic_slice_in_dim(
                cumul_all, query_start, key_sub_len, 1
            ).transpose(0, 2, 1)
            query_pos = query_start + jnp.arange(key_sub_len, dtype=jnp.int32)
            allowed = allowed_of(query_pos, positions, lengths)
            scores = jnp.where(
                allowed, scores_of(query_block, key_low, cumul_block, cumul_own), neg_large
            )
            attn_probs = jnp.where(allowed, jnp.exp(scores - lse_block[..., None]), 0.0)
            grad_value = grad_value + jnp.einsum(
                "rhqk,rqhd->rhkd",
                attn_probs.astype(jnp.bfloat16),
                dout_block,
                preferred_element_type=jnp.float32,
            )
            grad_probs = jnp.einsum(
                "rqhd,rkhd->rhqk", dout_block, value_low, preferred_element_type=jnp.float32
            )
            scores_low = (attn_probs * (grad_probs - delta_block[..., None])).astype(jnp.bfloat16)
            grad_key = (
                grad_key
                + jnp.einsum(
                    "rhqk,rqhd->rhkd", scores_low, query_block, preferred_element_type=jnp.float32
                )
                * scale_dot
            )
            grad_ck = grad_ck - jnp.sum(scores_low.astype(jnp.float32), axis=2)
            return (grad_key, grad_value, grad_ck)

        is_live = query_start + key_sub_len - 1 >= my_start
        return lax.cond(is_live, key_compute, lambda state_run: state_run, state_now)

    grad_key, grad_value, grad_ck = lax.fori_loop(
        0, piece_len // key_sub_len, key_update, key_state
    )
    grad_cumul = (grad_cq + grad_ck).transpose(0, 2, 1)
    local_suffix = jnp.flip(jnp.cumsum(jnp.flip(grad_cumul, axis=1), axis=1), axis=1)
    suffix = entering(
        local_suffix[:, 0, :], "seq", add_terms, jnp.zeros((rows_here, H), jnp.float32), True
    )
    grad_log_forget = (local_suffix + suffix[:, None, :]).reshape(token_count, H)
    grad_queries = grad_query.transpose(0, 2, 1, 3).reshape(token_count, H, HD)
    grad_keys = grad_key.transpose(0, 2, 1, 3).reshape(token_count, H, HD)
    grad_values = grad_value.transpose(0, 2, 1, 3).reshape(token_count, H, HD)
    grad_projected, grad_logits, grad_gain_query, grad_gain_key = heads_pull(
        (grad_queries, grad_keys, grad_values, grad_outgate, grad_log_forget)
    )
    grad_projected_low = grad_projected.astype(jnp.bfloat16)
    grad_qkvo_w = contract_rows(normed_low, grad_projected_low)
    grad_forget_w = lax.dot_general(
        normed_back,
        grad_logits,
        (((0,), (0,)), ((), ())),
        precision=highest,
        preferred_element_type=jnp.float32,
    )
    grad_bias = jnp.sum(grad_logits, axis=0)
    grad_normed = contract_cols(grad_projected_low, qkvo_full) + jnp.dot(
        grad_logits, forget_weight.T, precision=highest
    )
    grad_inputs_part, grad_gain_attn = norm_pull(grad_normed)
    input_grad = (grad_middle + grad_inputs_part).reshape(rows_here, block_len, D)
    qkvo_shard, proj_shard, gateup_shard, down_shard = (
        lax.psum_scatter(grad_qkvo_w, ("seq", "dp"), scatter_dimension=0, tiled=True),
        lax.psum_scatter(grad_proj_w, ("seq", "dp"), scatter_dimension=0, tiled=True),
        lax.psum_scatter(grad_gateup_w, ("seq", "dp"), scatter_dimension=0, tiled=True),
        lax.psum_scatter(grad_down_w, ("seq", "dp"), scatter_dimension=0, tiled=True),
    )
    shard_squares = (
        jnp.sum(qkvo_shard * qkvo_shard)
        + jnp.sum(proj_shard * proj_shard)
        + jnp.sum(gateup_shard * gateup_shard)
        + jnp.sum(down_shard * down_shard)
    )
    small_grads = jnp.concatenate(
        [grad_gain_attn, grad_gain_ffn, grad_gain_query, grad_gain_key, grad_bias]
    )
    small_total, forget_total, square_total = lax.psum(
        (small_grads, grad_forget_w, shard_squares), ("seq", "dp")
    )
    grad_norm = jnp.sqrt(
        square_total + jnp.sum(small_total * small_total) + jnp.sum(forget_total * forget_total)
    )
    clip_factor = 1.0 / jnp.maximum(grad_norm, 1.0)
    qkvo_new, qkvo_m, qkvo_v = adam_update(
        qkvo_weight, qkvo_shard * clip_factor, qkvo_mean, qkvo_square, rate_dense, decay_dense
    )
    proj_new, proj_m, proj_v = adam_update(
        proj_weight, proj_shard * clip_factor, proj_mean, proj_square, rate_proj, decay_dense
    )
    gateup_new, gateup_m, gateup_v = adam_update(
        gateup_weight,
        gateup_shard * clip_factor,
        gateup_mean,
        gateup_square,
        rate_dense,
        decay_dense,
    )
    down_new, down_m, down_v = adam_update(
        down_weight, down_shard * clip_factor, down_mean, down_square, rate_dense, decay_dense
    )
    forget_new, forget_m, forget_v = adam_update(
        forget_weight,
        forget_total * clip_factor,
        forget_mean,
        forget_square,
        rate_dense,
        decay_dense,
    )
    params_new, params_m, params_v = adam_update(
        norm_params, small_total * clip_factor, params_mean, params_square, rate_small, 0.0
    )
    return (
        block_output,
        input_grad,
        grad_norm,
        qkvo_new,
        qkvo_m,
        qkvo_v,
        proj_new,
        proj_m,
        proj_v,
        gateup_new,
        gateup_m,
        gateup_v,
        down_new,
        down_m,
        down_v,
        forget_new,
        forget_m,
        forget_v,
        params_new,
        params_m,
        params_v,
    )


QB = 256
HEADS = 3
HW = HEADS * HD
PAD = 256
SEQ = 1024
LOW = jnp.bfloat16
F32 = jnp.float32
scale_dot = HD**-0.5
DEV = pl.DeviceIdType.MESH
ANY = pl.BlockSpec(memory_space=pl.ANY)
VM = pl.BlockSpec(memory_space=pltpu.VMEM)
SM = pl.BlockSpec(memory_space=pltpu.SMEM)
DMA = pltpu.SemaphoreType.DMA
PAIRS = ((0, 0), (0, 1), (0, 2), (1, 0), (1, 1), (2, 0))


def shape_of(shape, dtype=F32):
    return jax.ShapeDtypeStruct(shape, dtype)


def dot_nt(a, b):
    return lax.dot_general(a, b, (((1,), (1,)), ((), ())), preferred_element_type=F32)


def dot_tn(a, b):
    return lax.dot_general(a, b, (((0,), (0,)), ((), ())), preferred_element_type=F32)


def dot_nn(a, b):
    return jnp.dot(a, b, preferred_element_type=F32)


def place():
    return tuple(lax.axis_index(a) for a in ("z", "x", "y", "c"))


def other(index, differs):
    return 1 - index if differs else index


def group_peer(d, x, y, c):
    px, py, pc = other(x, d & 4), other(y, d & 2), other(c, d & 1)
    return {"x": px, "y": py, "c": pc}, px * 4 + py * 2 + pc


def greet(z, x, y, c, column=False, line=False, plane=False):
    barrier = pltpu.get_barrier_semaphore()

    def signal(peer):
        pl.semaphore_signal(barrier, inc=1, device_id=peer, device_id_type=DEV)

    for d in range(1, 8):
        signal(group_peer(d, x, y, c)[0])
    count = 7
    if column:
        away = z // 2 - c
        count = count + 1 + away * away
        for r in range(2):
            pl.when(jnp.logical_not((away == 0) & (2 * c + r == z)))(
                functools.partial(signal, {"z": 2 * c + r, "c": z // 2})
            )
    if line:
        count = count + 1 + z * (3 - z) // 2
        pl.when(z < 3)(functools.partial(signal, {"z": z + 1}))
        pl.when(z > 0)(functools.partial(signal, {"z": z - 1}))
    if plane:
        count = count + 3
        for d in range(1, 4):
            signal({"z": lax.rem(z + d, 4)})
    pl.semaphore_wait(barrier, count)


def remote(src, dst, send_sem, recv_sem, peer):
    return pltpu.make_async_remote_copy(
        src_ref=src, dst_ref=dst, send_sem=send_sem, recv_sem=recv_sem, device_id=peer, device_id_type=DEV
    )


VMEM_BYTES = 63 * 1024 * 1024


def comm_params(collective_id):
    return pltpu.CompilerParams(collective_id=collective_id, has_side_effects=True, vmem_limit_bytes=VMEM_BYTES)


def swap_start(src, dst, send_sem, recv_sem, local_sem, x, y, c):
    me = x * 4 + y * 2 + c
    own = pltpu.make_async_copy(src.at[me], dst.at[me], local_sem)
    own.start()
    copies = []
    for d in (4, 2, 6, 5, 3, 7, 1):
        peer, number = group_peer(d, x, y, c)
        copy = remote(src.at[number], dst.at[me], send_sem.at[d], recv_sem.at[d], peer)
        copy.start()
        copies.append(copy)
    return own, copies


def swap_wait(started):
    own, copies = started
    own.wait()
    for copy in copies:
        copy.wait()


def swap_sems():
    return [DMA((8,)), DMA((8,)), DMA]


def column_start(src, dst, send, recv, local, z, c):
    slot = lax.rem(z, 2)
    for r in range(2):
        keep = (z // 2 == c) & (2 * c + r == z)

        @pl.when(keep)
        def _():
            pltpu.make_async_copy(src.at[r], dst.at[slot], local).start()

        @pl.when(jnp.logical_not(keep))
        def _():
            peer = {"z": 2 * c + r, "c": z // 2}
            remote(src.at[r], dst.at[slot], send.at[r], recv.at[slot], peer).start()


def column_wait(src, dst, send, recv, local, z, c):
    slot = lax.rem(z, 2)
    for r in range(2):
        keep = (z // 2 == c) & (2 * c + r == z)
        peer = {"z": 2 * c + r, "c": z // 2}

        @pl.when(keep)
        def _():
            pltpu.make_async_copy(src.at[r], dst.at[slot], local).wait()

        @pl.when(jnp.logical_not(keep))
        def _():
            remote(src.at[r], dst.at[slot], send.at[r], recv.at[slot], peer).wait_send()
            remote(src.at[r], dst.at[r], send.at[r], recv.at[r], peer).wait_recv()


def column_sems():
    return [DMA((2,)), DMA((2,)), DMA]


class LineGather:
    def __init__(self, own_at, dst_at, chunks, sems, z):
        self.own_at, self.dst_at, self.chunks, self.z = own_at, dst_at, chunks, z
        self.sems = sems

    def copy(self, k, h, up):
        send, recv = self.sems[0:2] if up else self.sems[2:4]
        block = self.z - k if up else self.z + k
        src = self.own_at(h) if k == 0 else self.dst_at(block, h)
        n = k * self.chunks + h
        peer = {"z": self.z + 1 if up else self.z - 1}
        return remote(src, self.dst_at(block, h), send.at[n], recv.at[n], peer)

    def cases(self, k, up):
        z = self.z
        if up:
            return (z < 3) & (z >= k), z >= k + 1
        return (z > 0) & (z + k <= 3), z + k + 1 <= 3

    def send(self, k):
        for h in range(self.chunks):
            for up in (True, False):
                if k > 0:
                    self.wait_one(k - 1, h, up)

                @pl.when(self.cases(k, up)[0])
                def _():
                    self.copy(k, h, up).start()

    def wait_one(self, k, h, up):
        @pl.when(self.cases(k, up)[1])
        def _():
            self.copy(k, h, up).wait_recv()

    def finish(self):
        for h in range(self.chunks):
            for up in (True, False):
                self.wait_one(2, h, up)
        for k in range(3):
            for h in range(self.chunks):
                for up in (True, False):

                    @pl.when(self.cases(k, up)[0])
                    def _():
                        self.copy(k, h, up).wait_send()


def line_sems(chunks):
    return [DMA((3 * chunks,))] * 4


class LineReduce:
    def __init__(self, part, chunk, chunks, land_up, land_down, sems, z):
        self.part, self.chunk, self.chunks, self.z = part, chunk, chunks, z
        self.lands = {True: land_up, False: land_down}
        self.sems = {True: sems[0:2], False: sems[2:4]}

    def copy(self, m, h, up):
        dest = 3 - m if up else m
        send, recv = self.sems[up]
        n = m * self.chunks + h
        peer = {"z": self.z + 1 if up else self.z - 1}
        land = self.lands[up].at[(m, *self.chunk(h))]
        return remote(self.part.at[(dest, *self.chunk(h))], land, send.at[n], recv.at[n], peer)

    def add(self, m, h, up):
        dest = 3 - m if up else m
        at = self.chunk(h)
        here, come = (dest, *at), (m, *at)
        total = self.part[here].astype(F32) + self.lands[up][come].astype(F32)
        self.part[here] = total.astype(LOW)

    def begin(self, m):
        for up in (True, False):

            @pl.when(self.z == (0 if up else 3))
            def _():
                for h in range(self.chunks):
                    self.copy(m, h, up).start()

    def phase(self, p, chunks=None):
        chunks = range(self.chunks) if chunks is None else chunks
        if p == 0:
            for m in range(3):
                self.begin(m)
            return
        for m in range(3):
            for hops in range(1, 4 - m):
                if p != hops + m:
                    continue
                for up in (True, False):

                    @pl.when(self.z == (hops if up else 3 - hops))
                    def _():
                        for h in chunks:
                            self.copy(m, h, up).wait_recv()
                            self.add(m, h, up)
                            if hops < 3 - m:
                                self.copy(m, h, up).start()

    def finish(self):
        for m in range(3):
            for h in range(self.chunks):
                for up in (True, False):
                    dest = 3 - m if up else m

                    @pl.when(self.z < dest if up else self.z > dest)
                    def _():
                        self.copy(m, h, up).wait_send()


class Gather:
    def __init__(self, src_at, dst_at, sems, x, y, c):
        send_x, recv_x, send_y, recv_y, send_c, recv_c, local = sems
        ox, oy = 1 - x, 1 - y
        xp, yp, cp = {"x": ox}, {"y": oy}, {"c": 1 - c}

        def own(j, send, recv, peer):
            return remote(src_at(j), dst_at(x, y, c, j), send.at[j], recv.at[j], peer)

        def onward(px, py, j, k, send, recv, peer):
            block = dst_at(px, py, c, j)
            return remote(block, block, send.at[k], recv.at[k], peer)

        self.x = [own(j, send_x, recv_x, xp) for j in range(2)]
        self.y = [own(j, send_y, recv_y, yp) for j in range(2)]
        self.c = [own(j, send_c, recv_c, cp) for j in range(2)]
        self.local = [pltpu.make_async_copy(src_at(j), dst_at(x, y, c, j), local.at[j]) for j in range(2)]
        self.diag_y = onward(ox, y, 0, 2, send_y, recv_y, yp)
        self.diag_x = onward(x, oy, 1, 2, send_x, recv_x, xp)
        order = ((ox, y, 0), (x, oy, 1), (ox, y, 1), (x, oy, 0), (ox, oy, 0), (ox, oy, 1))
        self.pass_c = [onward(*p, k + 2, send_c, recv_c, cp) for k, p in enumerate(order)]

    def start(self):
        for copy in (self.x[0], self.y[1], self.x[1], self.y[0], self.c[0], self.c[1], *self.local):
            copy.start()

    def forward(self):
        self.x[0].wait_recv()
        self.diag_y.start()
        self.pass_c[0].start()
        self.y[1].wait_recv()
        self.diag_x.start()
        self.pass_c[1].start()

    def forward_rest(self):
        self.x[1].wait_recv()
        self.pass_c[2].start()
        self.y[0].wait_recv()
        self.pass_c[3].start()

    def finish(self):
        self.diag_y.wait_recv()
        self.pass_c[4].start()
        self.diag_x.wait_recv()
        self.pass_c[5].start()
        for copy in (*self.x, *self.y, *self.c, self.diag_x, self.diag_y, *self.pass_c):
            copy.wait_send()
        for copy in (*self.c, *self.pass_c):
            copy.wait_recv()
        for copy in self.local:
            copy.wait()


def gather_sems():
    return [DMA((3,)), DMA((3,)), DMA((3,)), DMA((3,)), DMA((8,)), DMA((8,)), DMA((2,))]


def natural(ref):
    return lambda x, y, c, j: ref.at[y, c, j, x]


class Scatter:
    def __init__(self, product, bufs, sems, x, y, c):
        self.product, self.own_c = product, c
        self.to_core, self.from_core, self.to_x, self.from_x, self.to_y, self.from_y, self.kept = bufs
        send_c, recv_c, send_x, recv_x, send_y, recv_y = sems
        ox, oy = 1 - x, 1 - y
        xp, yp, cp = {"x": ox}, {"y": oy}, {"c": 1 - c}
        self.places = ((ox, oy), (ox, y), (x, oy), (x, y))

        def copies(src, dst, send, recv, peer, count):
            return [remote(src.at[k], dst.at[k], send.at[k], recv.at[k], peer) for k in range(count)]

        self.c = [
            remote(self.to_core.at[k % 2], self.from_core.at[k], send_c.at[k], recv_c.at[k], cp) for k in range(4)
        ]
        self.x = copies(self.to_x, self.from_x, send_x, recv_x, xp, 3)
        self.y = copies(self.to_y, self.from_y, send_y, recv_y, yp, 3)

    def to_partner(self, k):
        if k >= 2:
            self.c[k - 2].wait_send()
        self.to_core[k % 2] = self.product(*self.places[k], 1 - self.own_c).astype(LOW)
        self.c[k].start()

    def summed(self, k):
        own = self.product(*self.places[k], self.own_c)
        self.c[k].wait_recv()
        return own + self.from_core[k].astype(F32)

    def close(self, k):
        total = self.summed(k)
        if k == 0:
            self.to_x[0] = total[0].astype(LOW)
            self.x[0].start()
            self.to_y[0] = total[1].astype(LOW)
            self.y[0].start()
        elif k == 1:
            self.to_x[1] = total[0].astype(LOW)
            self.x[1].start()
            self.kept[0] = total[1]
        elif k == 2:
            self.to_y[1] = total[1].astype(LOW)
            self.y[1].start()
            self.kept[1] = total[0]
        else:
            self.y[0].wait_recv()
            self.to_x[2] = (self.kept[0] + self.from_y[0].astype(F32)).astype(LOW)
            self.x[2].start()
            self.x[0].wait_recv()
            self.to_y[2] = (self.kept[1] + self.from_x[0].astype(F32)).astype(LOW)
            self.y[2].start()
            self.kept[0], self.kept[1] = total[0], total[1]

    def stage(self, k):
        if k < 4:
            self.to_partner(k)
        if k > 0:
            self.close(k - 1)

    def result(self):
        self.x[1].wait_recv()
        first = self.kept[0] + self.from_x[1].astype(F32)
        self.y[1].wait_recv()
        second = self.kept[1] + self.from_y[1].astype(F32)
        self.y[2].wait_recv()
        first = first + self.from_y[2].astype(F32)
        self.x[2].wait_recv()
        second = second + self.from_x[2].astype(F32)
        for copy in (*self.c[2:], *self.x, *self.y):
            copy.wait_send()
        return first, second


def scatter_scratch(rows, width):
    return (
        [pltpu.VMEM((2, 2, rows, width), LOW), pltpu.VMEM((4, 2, rows, width), LOW)]
        + [pltpu.VMEM((3, rows, width), LOW)] * 4
        + [pltpu.VMEM((2, rows, width), F32)]
    )


def scatter_sems():
    return [DMA((4,)), DMA((4,)), DMA((3,)), DMA((3,)), DMA((3,)), DMA((3,))]


def exchange_start(in_ref, zbuf, sems, z):
    send, recv = sems
    zbuf[pl.ds(z, 1)] = in_ref[...][None]
    copies = []
    for i in range(3):
        copies.append(remote(in_ref, zbuf.at[z], send.at[i], recv.at[i], {"z": lax.rem(z + i + 1, 4)}))
        copies[i].start()
    return copies


def exchange_end(copies, zbuf, zsum, gbuf, sems, x, y, c):
    send, recv = sems
    me = x * 4 + y * 2 + c
    for copy in copies:
        copy.wait()
    zsum[...] = zbuf[0] + zbuf[1] + zbuf[2] + zbuf[3]
    gbuf[pl.ds(me, 1)] = zsum[...][None]
    copies = []
    for i in range(7):
        peer = group_peer(i + 1, x, y, c)[0]
        copies.append(remote(zsum, gbuf.at[me], send.at[i], recv.at[i], peer))
        copies[i].start()
    for copy in copies:
        copy.wait()


def exchange_total(in_ref, zbuf, zsum, gbuf, sems, z, x, y, c):
    copies = exchange_start(in_ref, zbuf, sems[0:2], z)
    exchange_end(copies, zbuf, zsum, gbuf, sems[2:4], x, y, c)


def exchange_scratch(rows, width):
    return [pltpu.VMEM((4, rows, width), F32), pltpu.VMEM((rows, width), F32)]


def exchange_sems():
    return [DMA((3,)), DMA((3,)), DMA((7,)), DMA((7,))]


def add_blocks(gbuf, rows):
    total = gbuf[0, rows]
    for i in range(1, 8):
        total = total + gbuf[i, rows]
    return total


def norm_kernel(
    q_part, gu_ref, proj_ref, down_ref, small_ref,
    q_out, gu_out, proj_out, norm_ref, q_swapped, landed, square, zbuf, zsum, gbuf, *sems,
):
    z, x, y, c = place()
    greet(z, x, y, c, plane=True)
    q_swap = swap_start(q_part, q_swapped, *sems[0:3], x, y, c)
    over_z = []
    for i in range(3):
        dest = lax.rem(z + i + 1, 4)
        over_z.append(remote(proj_ref.at[dest], landed.at[i], sems[7].at[i], sems[8].at[i], {"z": dest}))
        over_z[i].start()

    def squares(values):
        return jnp.sum(jnp.sum(values * values, axis=0, keepdims=True), axis=1, keepdims=True)

    sums = squares(add_blocks(small_ref, slice(0, 3)))
    for i in range(8):
        sums = sums + squares(small_ref[i, 3:6])
    shards = squares(down_ref[...].astype(F32))
    for t in range(8):
        grads = gu_ref[t]
        shards = shards + squares(grads.astype(F32))
        for b in range(8):
            column = (b * 8 + t) * 128
            gu_out[:, column : column + 128] = grads[:, b * 128 : b * 128 + 128]
    swap_wait(q_swap)
    for u in range(8):
        shards = shards + squares(q_swapped[u].astype(F32))
    for copy in over_z:
        copy.wait()
    mine = proj_ref[pl.ds(z, 1)][0].astype(F32)
    for i in range(3):
        mine = mine + landed[i].astype(F32)
    proj_out[...] = mine
    shards = shards + squares(mine)
    square[...] = jnp.broadcast_to(shards, (8, 128))
    exchange = exchange_start(square, zbuf, sems[3:5], z)
    half = lanes(2 * HW) < HW
    for u in range(4):
        even, odd = q_swapped[2 * u].astype(F32), q_swapped[2 * u + 1].astype(F32)
        for m in range(2):
            a, b = even[:, 2 * HW * m : 2 * HW * (m + 1)], odd[:, 2 * HW * m : 2 * HW * (m + 1)]
            first = jnp.where(half, a, pltpu.roll(b, HW, 1)).astype(LOW)
            second = jnp.where(half, pltpu.roll(a, HW, 1), b).astype(LOW)
            column = 2 * m * D + 2 * HW * u
            q_out[:, column : column + 2 * HW] = first
            q_out[:, column + D : column + D + 2 * HW] = second
    exchange_end(exchange, zbuf, zsum, gbuf, sems[5:7], x, y, c)
    norm_ref[...] = jnp.sqrt(add_blocks(gbuf, slice(0, 8)) + sums)


def norm_layer(q_part, gu_part, proj_part, down_shard, small, collective_id):
    return pl.pallas_call(
        norm_kernel,
        out_shape=[shape_of((48, 4 * D), LOW), shape_of((48, 2 * FF), LOW), shape_of((48, D)), shape_of((8, 128))],
        in_specs=[ANY] + [VM] * 4,
        out_specs=[VM] * 4,
        scratch_shapes=[
            pltpu.VMEM((8, 48, 4 * HW), LOW), pltpu.VMEM((3, 48, D), LOW), pltpu.VMEM((8, 128), F32)
        ]
        + exchange_scratch(8, 128) + [pltpu.VMEM((8, 8, 128), F32)]
        + swap_sems() + exchange_sems() + [DMA((3,)), DMA((3,))],
        compiler_params=comm_params(collective_id),
        name="norm_layer",
    )(q_part, gu_part, proj_part, down_shard, small)


ADAM_STEP = 512


def adam_kernel(rates, norm_ref, small_ref, grad_ref, out_ref, *refs):
    count = len(rates)
    grads, refs = refs[:count], refs[count:]
    olds, refs = refs[: 3 * count], refs[3 * count :]
    few, refs = refs[:6], refs[6:]
    grad_wide, out_copy, norm_out, refs = refs[0], refs[1], refs[2], refs[3:]
    norm_out[0, 0] = norm_ref[0, 0]
    news, refs = refs[: 3 * count], refs[3 * count :]
    few_new, refs = refs[:6], refs[6:]
    grad_bufs, refs = refs[:count], refs[count:]
    bufs, refs = refs[: 3 * count], refs[3 * count :]
    grad_sem, in_sem, out_sem = refs
    def half(ref, n):
        width = ref.shape[1] // 2
        return ref.at[:, n * width : (n + 1) * width]

    units = [(i, n) for i in range(count) for n in range(2)]

    def moved(source, target, sem, i, n, k=0):
        return pltpu.make_async_copy(half(source, n), half(target, n), sem.at[2 * i + n + 2 * count * k])

    loads = {(i, n): moved(grads[i], grad_bufs[i], grad_sem, i, n) for i, n in units}
    reads = {(i, n): [moved(olds[3 * i + k], bufs[3 * i + k], in_sem, i, n, k) for k in range(3)] for i, n in units}
    writes = {(i, n): [moved(bufs[3 * i + k], news[3 * i + k], out_sem, i, n, k) for k in range(3)] for i, n in units}
    for unit in units:
        loads[unit].start()
        for copy in reads[unit]:
            copy.start()
    clip = 1.0 / jnp.maximum(norm_ref[:1, :1], 1.0)
    for unit in units:
        loads[unit].wait()
        for copy in reads[unit]:
            copy.wait()
        i, n = unit
        w_ref, m_ref, v_ref = bufs[3 * i : 3 * i + 3]
        width = w_ref.shape[1] // 2
        step = min(width, ADAM_STEP) if width % ADAM_STEP == 0 else 256

        @pl.loop(0, width // step)
        def _(k):
            at = (slice(None), pl.ds(pl.multiple_of(n * width + k * step, 128), step))
            gradient = grad_bufs[i][at].astype(F32) * clip
            w_ref[at], m_ref[at], v_ref[at] = adam_update(
                w_ref[at], gradient, m_ref[at], v_ref[at], rates[i], decay_dense
            )

        for copy in writes[unit]:
            copy.start()
    grad_wide[...] = grad_ref[...].astype(F32)
    out_copy[...] = out_ref[...]
    for t in range(8):
        for h in range(HEADS):
            at = slice(t * HEADS + h, t * HEADS + h + 1)
            updated = adam_update(
                few[0][at], small_ref[t, 3 + h : 4 + h] * clip, few[1][at], few[2][at], rate_dense, decay_dense
            )
            for k in range(3):
                few_new[k][at] = updated[k]
    small = add_blocks(small_ref, slice(0, 3))
    small = jnp.concatenate([small[0:1], small[1:2], small[2:3]], axis=1)[:, : few[3].shape[0]]
    old = [few[3 + k][...].reshape(1, -1) for k in range(3)]
    updated = adam_update(old[0], small * clip, old[1], old[2], rate_small, 0.0)
    for k in range(3):
        few_new[3 + k][...] = updated[k].reshape(-1)
    for unit in units:
        for copy in writes[unit]:
            copy.wait()


def adam_layer(rates, norm, small, input_grad, block_output, grads, olds, few):
    count = len(rates)
    return pl.pallas_call(
        functools.partial(adam_kernel, rates),
        out_shape=[shape_of(input_grad.shape), shape_of(block_output.shape, LOW), shape_of((1, 1))]
        + [shape_of(a.shape) for a in (*olds, *few)],
        in_specs=[VM] * 4 + [ANY] * (4 * count) + [VM] * 6,
        out_specs=[VM, VM, SM] + [ANY] * (3 * count) + [VM] * 6,
        scratch_shapes=[pltpu.VMEM(a.shape, a.dtype) for a in grads]
        + [pltpu.VMEM(a.shape, F32) for a in olds]
        + [DMA((2 * count,)), DMA((6 * count,)), DMA((6 * count,))],
        compiler_params=pltpu.CompilerParams(vmem_limit_bytes=VMEM_BYTES),
        name="adam",
    )(norm, small, input_grad, block_output, *grads, *olds, *few)


def row_scale(values):
    return lax.rsqrt(jnp.mean(values * values, axis=-1, keepdims=True) + eps_norm)


def norm_back(grad, values, gain_vec):
    r = row_scale(values)
    u = grad * gain_vec
    by_values = r * u - values * (r * r * r) * jnp.mean(values * u, axis=-1, keepdims=True)
    return by_values, jnp.sum(grad * values * r, axis=0, keepdims=True)


def open_kernel(
    x_ref, lens_ref, params_ref, forget_ref, wq_ref, wg_ref, wp_ref,
    xo_ref, lo_ref, normed_ref, qkvo_ref, gu_ref, wf_ref, proj_ref,
    normed_own, wq_low, wg_low, wp_low, len_tile, *sems,
):
    z, x, y, c = place()
    t = x * 4 + y * 2 + c
    greet(z, x, y, c, column=True, line=True)
    column_start(x_ref, xo_ref, *sems[0:3], z, c)
    half = lanes(2 * HW) < HW
    for u in range(4):
        for m in range(2):
            column = 2 * m * D + 2 * HW * u
            a, b = wq_ref[:, column : column + 2 * HW], wq_ref[:, column + D : column + D + 2 * HW]
            at = slice(2 * HW * m, 2 * HW * (m + 1))
            wq_low[2 * u, :, at] = jnp.where(half, a, pltpu.roll(b, HW, 1)).astype(LOW)
            wq_low[2 * u + 1, :, at] = jnp.where(half, pltpu.roll(a, HW, 1), b).astype(LOW)
    qkvo_swap = swap_start(wq_low, qkvo_ref.at[z], *sems[3:6], x, y, c)
    row = lax.broadcasted_iota(jnp.int32, (8, 128), 0)
    tile = jnp.where(row == 0, lens_ref[0].astype(F32), lens_ref[1].astype(F32))
    for d in range(8):
        len_tile[d] = tile
    lens = swap_start(len_tile, lo_ref, *sems[6:9], x, y, c)
    wp_low[...] = wp_ref[...].astype(LOW)
    own_proj = pltpu.make_async_copy(wp_low, proj_ref.at[z], sems[9])
    own_proj.start()
    for d in range(8):
        for b in range(8):
            column = (b * 8 + d) * 128
            wg_low[d, :, b * 128 : b * 128 + 128] = wg_ref[:, column : column + 128].astype(LOW)
    proj = LineGather(lambda h: wp_low, lambda k, h: proj_ref.at[k], 1, sems[10:14], z)
    qkvo = LineGather(
        lambda h: qkvo_ref.at[z, 4 * h : 4 * h + 4], lambda k, h: qkvo_ref.at[k, 4 * h : 4 * h + 4], 2,
        sems[14:18], z,
    )
    swap_wait(qkvo_swap)
    qkvo.send(0)
    proj.send(0)
    sub = lax.broadcasted_iota(jnp.int32, (8, D), 0)
    mine = jnp.zeros((8, D), F32)
    for d in range(8):
        for h in range(HEADS):
            mine = jnp.where((sub == h) & (t == d), forget_ref[d * HEADS + h : d * HEADS + h + 1], mine)
    parts = pieces_of(mine)
    wf_ref[...] = columns_of(jnp.concatenate([parts[b] for _, b in PAIRS], axis=0)).astype(LOW)
    column_wait(x_ref, xo_ref, *sems[0:3], z, c)
    for j in range(2):
        rows = xo_ref[j].astype(F32)
        normed_own[j] = (rows * row_scale(rows) * params_ref[:, :D]).astype(LOW)
    normed = Gather(lambda j: normed_own.at[j], natural(normed_ref), sems[18:25], x, y, c)
    normed.start()
    gu_swap = swap_start(wg_low, gu_ref, *sems[25:28], x, y, c)
    qkvo.send(1)
    proj.send(1)
    normed.forward()
    normed.forward_rest()
    qkvo.send(2)
    proj.send(2)
    normed.finish()
    qkvo.finish()
    proj.finish()
    own_proj.wait()
    swap_wait(gu_swap)
    swap_wait(lens)


def open_layer(x, lengths, params, forget, qkvo_weight, gateup_weight, proj_weight, collective_id):
    return pl.pallas_call(
        open_kernel,
        out_shape=[
            shape_of(x.shape, LOW),
            shape_of((8, 8, 128)),
            shape_of((2, 2, 2, 2, 128, D), LOW),
            shape_of((4, 8, 48, 4 * HW), LOW),
            shape_of((8, 48, 1024), LOW),
            shape_of((D, 128), LOW),
            shape_of((4, 48, D), LOW),
        ],
        in_specs=[ANY, SM, VM, VM, VM, VM, VM],
        out_specs=[VM] + [ANY] * 4 + [VM, ANY],
        scratch_shapes=[
            pltpu.VMEM((2, 128, D), LOW), pltpu.VMEM((8, 48, 4 * HW), LOW), pltpu.VMEM((8, 48, 1024), LOW),
            pltpu.VMEM((48, D), LOW), pltpu.VMEM((8, 8, 128), F32),
        ]
        + column_sems() + swap_sems() * 2 + [DMA] + line_sems(1) + line_sems(2) + gather_sems() + swap_sems(),
        compiler_params=comm_params(collective_id),
        name="open_layer",
    )(x, lengths, params, forget, qkvo_weight, gateup_weight, proj_weight)


def length_of(len_ref, z, x, sequence):
    tile = len_ref[pl.ds(x * 4 + sequence * 2 + z // 2, 1)][0]
    row = lax.broadcasted_iota(jnp.int32, (8, 128), 0) == lax.rem(z, 2)
    return jnp.sum(jnp.where(row, tile, 0.0), axis=0, keepdims=True)[:, :1]


def head_gain(params_ref, key):
    both = params_ref[:, 2 * D : 2 * D + 128]
    both = pltpu.roll(both, HD, 1) if key else both
    one = jnp.concatenate([jnp.where(lanes(128) < HD, both, 0.0), jnp.zeros((1, 128), F32)], axis=1)
    return one + pltpu.roll(one, HD, 1) + pltpu.roll(one, 2 * HD, 1)


def lanes(width):
    return lax.broadcasted_iota(jnp.int32, (1, width), 1)


def head_mask(h):
    lane = lanes(PAD)
    return (lane >= h * HD) & (lane < (h + 1) * HD)


def split_halves(pair):
    valid = lanes(PAD) < HW
    first = jnp.where(valid, pair[:, :PAD], 0.0)
    second = jnp.where(valid, pltpu.roll(pair, HW, 1)[:, :PAD], 0.0)
    return first, second


def join_halves(first, second):
    tail = jnp.zeros((first.shape[0], 128), F32)
    first = jnp.concatenate([first, tail], axis=1)
    second = pltpu.roll(jnp.concatenate([second, tail], axis=1), HW, 1)
    return jnp.where(lanes(2 * HW) < HW, first, second)


def head_sums(values):
    row = lax.broadcasted_iota(jnp.int32, (PAD, PAD), 0) // HD
    column = lax.broadcasted_iota(jnp.int32, (PAD, PAD), 1) // HD
    ones = jnp.where(row == column, 1.0, 0.0).astype(LOW)
    high = values.astype(LOW)
    return dot_nn(high, ones) + dot_nn((values - high.astype(F32)).astype(LOW), ones)


def head_scale(values):
    return lax.rsqrt(head_sums(values * values) / HD + eps_norm)


def head_norm_back(grad, values, gain_vec):
    r = head_scale(values)
    u = grad * gain_vec
    by_values = r * u - values * (r * r * r) * (head_sums(values * u) / HD)
    return by_values, jnp.sum(grad * values * r, axis=0, keepdims=True)


def running_sum(rows, backward):
    lane = lanes(SEQ)
    step = 1
    while step < SEQ:
        if backward:
            rows = rows + jnp.where(lane < SEQ - step, pltpu.roll(rows, SEQ - step, 1), 0.0)
        else:
            rows = rows + jnp.where(lane >= step, pltpu.roll(rows, step, 1), 0.0)
        step *= 2
    return rows


def columns_of(rows):
    return jnp.concatenate([rows, jnp.zeros((128 - rows.shape[0], rows.shape[1]), F32)], axis=0).T


def pieces_of(value):
    high = value.astype(LOW).astype(F32)
    middle = (value - high).astype(LOW).astype(F32)
    return high, middle, value - high - middle


def segments(i):
    return (((0, i * QB, False),) if i else ()) + ((i * QB, QB, True),)


def causal(scores):
    query = lax.broadcasted_iota(jnp.int32, (QB, QB), 0)
    key = lax.broadcasted_iota(jnp.int32, (QB, QB), 1)
    return jnp.where(key <= query, scores, neg_large)


EARLY = 2


def forward_kernel(
    params_smem, len_ref, normed_ref, wq_any, wf_ref, params_ref, wp_ref, wd_ref, gu_ref, ct_ref,
    raw_ref, q_ref, k_ref, v_ref, att_ref, col_ref, crow_ref, logit_ref, swapped_ref, projall_ref,
    down_ref, gu_first_ref, gout_ref, ct_own, wd_low, mixed_ref, wq_ref, *sems,
):
    z, x, y, c = place()
    s = pl.program_id(0)
    me = x * 4 + y * 2 + c
    swap_send, swap_recv, swap_local = sems[27:30]
    own_mixed = pltpu.make_async_copy(mixed_ref.at[x, y, c], swapped_ref.at[me], swap_local)

    def mixed_copy(d):
        peer = group_peer(d, x, y, c)[0]
        src = mixed_ref.at[peer["x"], peer["y"], peer["c"]]
        return remote(src, swapped_ref.at[me], swap_send.at[d], swap_recv.at[d], peer)

    def send_mixed(sequence):
        @pl.when(y == sequence)
        def _():
            own_mixed.start()
            for d in (4, 5, 1):
                mixed_copy(d).start()

        @pl.when(y != sequence)
        def _():
            for d in (2, 6, 3, 7):
                mixed_copy(d).start()
    length = length_of(len_ref, z, x, s)

    def piece(px, py, pc, j):
        return projall_ref.at[2 * j : 2 * j + 2, px * 4 + py * 2 + pc]

    proj = Gather(lambda j: wp_ref.at[2 * j : 2 * j + 2], piece, sems[:7], x, y, c)
    gout = Gather(lambda j: ct_own.at[j], natural(gout_ref), sems[7:14], x, y, c)
    down = LineGather(lambda h: wd_low, lambda k, h: down_ref.at[k], 1, sems[14:18], z)
    gateup = LineGather(lambda h: gu_ref.at[0:EARLY], lambda k, h: gu_first_ref.at[k], 1, sems[18:22], z)
    own_down = pltpu.make_async_copy(wd_low, down_ref.at[z], sems[22])
    own_gateup = pltpu.make_async_copy(gu_ref.at[0:EARLY], gu_first_ref.at[z], sems[23])

    fetch = pltpu.make_async_copy(wq_any, wq_ref, sems[30])

    def begin():
        fetch.start()
        greet(z, x, y, c, column=True, line=True)
        column_start(ct_ref, ct_own, *sems[24:27], z, c)
        proj.start()
        fetch.wait()
        wd_low[...] = wd_ref[...].astype(LOW)
        own_down.start()
        own_gateup.start()

    def turn():
        column_wait(ct_ref, ct_own, *sems[24:27], z, c)
        own_length = length_of(len_ref, z, x, y)
        for j in range(2):
            position = (2 * (2 * c + j) + x) * 128 + lax.broadcasted_iota(jnp.int32, (128, 1), 0)
            valid = position.astype(F32) < own_length
            ct_own[j] = jnp.where(valid, ct_own[j].astype(F32), 0.0).astype(LOW)
        gout.start()
        down.send(0)
        gateup.send(0)

    def half_way():
        send_mixed(0)
        proj.finish()

    def end():
        send_mixed(1)
        gout.finish()
        down.finish()
        gateup.finish()
        own_down.wait()
        own_gateup.wait()
        own_mixed.wait()
        for d in range(1, 8):
            mixed_copy(d).wait()

    hooks = {
        (0, 0): begin, (0, 2): proj.forward, (0, 8): proj.forward_rest, (0, 10): turn, (0, 15): half_way,
        (1, 1): lambda: down.send(1), (1, 2): gout.forward, (1, 4): lambda: gateup.send(1),
        (1, 8): gout.forward_rest, (1, 10): lambda: down.send(2), (1, 13): lambda: gateup.send(2), (1, 15): end,
    }

    def hook(n):
        for step in range(2):
            if (step, n) in hooks:
                pl.when(s == step)(hooks[step, n])

    hook(0)
    normed = normed_ref[0]
    raw = dot_nn(normed, wq_ref[...])
    raw_ref[0] = raw
    hook(1)
    q_raw, k_raw = split_halves(raw[:, : 2 * HW])
    v, gate = split_halves(raw[:, 2 * HW :])
    q = (q_raw * head_scale(q_raw) * head_gain(params_ref, False)).astype(LOW) * jnp.asarray(scale_dot, LOW)
    k = (k_raw * head_scale(k_raw) * head_gain(params_ref, True)).astype(LOW)
    v = v.astype(LOW)
    q_ref[0], k_ref[0], v_ref[0] = q, k, v
    pieces = dot_nn(normed, wf_ref[...]).T
    sub = lax.broadcasted_iota(jnp.int32, (8, 1), 0)
    bias = jnp.zeros((8, 1), F32)
    for h in range(HEADS):
        first_bias = 2 * D + 2 * HD + (x * 4 + y * 2 + c) * HEADS
        bias = jnp.where(sub == h, params_smem[first_bias + h], bias)
    logits = pieces[0:8] + pieces[8:16] + pieces[16:24] + bias
    logit_ref[0] = logits
    log_forget = jnp.minimum(logits, 0.0) - jnp.log1p(jnp.exp(-jnp.abs(logits)))
    inside = lanes(SEQ).astype(F32) < length
    crow = jnp.where(inside, running_sum(log_forget, False), -neg_large)
    crow_ref[0] = crow
    hook(2)
    for i in range(SEQ // QB):
        rows = slice(i * QB, (i + 1) * QB)
        att = jnp.zeros((QB, PAD), F32)
        for h in range(HEADS):
            mh = head_mask(h)
            qh = jnp.where(mh, q[rows], jnp.zeros((), LOW))
            parts = []
            for start, count, own in segments(i):
                keys = slice(start, start + count)
                scores = dot_nt(qh, k[keys]) - crow[h : h + 1, keys]
                parts.append((keys, causal(scores) if own else scores))
            tops = [jnp.max(scores, axis=-1, keepdims=True) for _, scores in parts]
            top = functools.reduce(jnp.maximum, tops)
            total = jnp.zeros((QB, 1), F32)
            out = jnp.zeros((QB, PAD), F32)
            for keys, scores in parts:
                p = jnp.exp(scores - top)
                total = total + jnp.sum(p, axis=-1, keepdims=True)
                out = out + dot_nn(p.astype(LOW), v[keys])
            att = jnp.where(mh, out / total, att)
            col_ref[0, rows, h : h + 1] = -(top + jnp.log(total))
            hook(3 + i * HEADS + h)
        att_ref[0, rows, :] = att
    mixed = att_ref[0] * jax.nn.sigmoid(gate)
    for cc in range(2):
        for xx in range(2):
            first, second = (mixed[(cc * 4 + 2 * j + xx) * 128 :][:128] for j in range(2))
            mixed_ref[xx, pl.ds(s, 1), cc] = join_halves(first, second).astype(LOW)[None]
    hook(15)


def seq_spec(rows, width, buffers=2):
    return pl.BlockSpec((1, rows, width), lambda s: (s, 0, 0), pipeline_mode=pl.Buffered(buffers))


def packed_spec(buffers=2):
    return pl.BlockSpec(
        (2, 1, 2, 128, 2 * HW), lambda s: (0, s, 0, 0, 0), pipeline_mode=pl.Buffered(buffers)
    )


def attention_forward(params, lens, normed, wq, wf, proj_mine, down_weight, gateup_mine, cotangent, collective_id):
    return pl.pallas_call(
        forward_kernel,
        grid=(2,),
        in_specs=[SM, VM, seq_spec(SEQ, D), ANY, VM, VM, ANY, VM, ANY, ANY],
        out_specs=[seq_spec(SEQ, 4 * HW)]
        + [seq_spec(SEQ, PAD)] * 4
        + [seq_spec(SEQ, 8), seq_spec(8, SEQ), seq_spec(8, SEQ)]
        + [ANY] * 5,
        out_shape=[shape_of((2, SEQ, 4 * HW))]
        + [shape_of((2, SEQ, PAD), LOW)] * 3
        + [shape_of((2, SEQ, PAD))]
        + [shape_of((2, SEQ, 8))]
        + [shape_of((2, 8, SEQ))] * 2
        + [shape_of((8, 128, 2 * HW), LOW), shape_of((4, 8, 48, D), LOW), shape_of((4, 128, D), LOW)]
        + [shape_of((4, EARLY, 48, 1024), LOW), shape_of((2, 2, 2, 2, 128, D), LOW)],
        scratch_shapes=[
            pltpu.VMEM((2, 128, D), LOW), pltpu.VMEM((128, D), LOW), pltpu.VMEM((2, 2, 2, 128, 2 * HW), LOW),
            pltpu.VMEM((D, 4 * HW), LOW),
        ]
        + gather_sems() * 2 + line_sems(1) * 2 + [DMA, DMA] + column_sems() + swap_sems() + [DMA],
        compiler_params=comm_params(collective_id),
        name="attention_forward",
    )(params[0], lens, normed, wq, wf, params, proj_mine, down_weight, gateup_mine, cotangent)


def ffn_kernel(
    mixed_swapped, proj_any, x_ref, params_ref, gu_mine_ref, gu_first_ref, gout_any, down_any,
    mixed_ref, middle_ref, hidden_ref, gmid_ref, gmid_low_ref, gain_out_ref, swapped_ref, gu_grad_ref, down_grad_ref,
    n2_own, n2_ref, gout_ref, down_ref, proj_ref, gu_all, ggu_ref, packed, down_part,
    land_up, land_down, *rest,
):
    bufs, sems = rest[:7], rest[7:]
    z, x, y, c = place()
    loads = [
        pltpu.make_async_copy(proj_any, proj_ref, sems[13].at[0]),
        pltpu.make_async_copy(gu_first_ref, gu_all.at[:, 0:EARLY], sems[13].at[1]),
        pltpu.make_async_copy(gu_mine_ref.at[EARLY:8], gu_all.at[z, EARLY:8], sems[13].at[2]),
        pltpu.make_async_copy(down_any, down_ref, sems[13].at[3]),
        pltpu.make_async_copy(gout_any, gout_ref, sems[13].at[4]),
    ]
    for load in loads:
        load.start()
    greet(z, x, y, c, line=True)
    line = LineGather(
        lambda h: gu_mine_ref.at[EARLY:8], lambda k, h: gu_all.at[k, EARLY:8], 1, sems[14:18], z
    )
    line.send(0)
    half = lanes(2 * HW) < HW
    for u in range(4):
        even, odd = mixed_swapped[2 * u].astype(F32), mixed_swapped[2 * u + 1].astype(F32)
        columns = slice(2 * HW * u, 2 * HW * (u + 1))
        mixed_ref[0, :, columns] = jnp.where(half, even, pltpu.roll(odd, HW, 1)).astype(LOW)
        mixed_ref[1, :, columns] = jnp.where(half, pltpu.roll(even, HW, 1), odd).astype(LOW)
    loads[0].wait()
    middle = dot_nn(mixed_ref[...].reshape(256, D), proj_ref[...]) + x_ref[...].reshape(256, D).astype(F32)
    middle_ref[...] = middle.reshape(2, 128, D)
    n2_own[...] = (middle * row_scale(middle) * params_ref[:, D : 2 * D]).astype(LOW).reshape(2, 128, D)
    gather = Gather(lambda j: n2_own.at[j], natural(n2_ref), sems[18:25], x, y, c)
    gather.start()
    line.send(1)
    gather.forward()
    line.send(2)
    gather.forward_rest()
    gather.finish()
    line.finish()
    for load in loads[1:]:
        load.wait()
    down_grads = LineReduce(down_part, lambda h: (), 1, land_up, land_down, sems[9:13], z)
    gu_ref = gu_all
    def product(px, py, pc):
        rows = n2_ref[py, pc, :, px].reshape(256, D)
        gateup = dot_nn(rows, gu_ref[...].reshape(D, 1024))
        gate, up = gateup[:, :512], gateup[:, 512:]
        s = jax.nn.sigmoid(gate)
        silu = gate * s
        hidden_ref[py, pc, :, px] = (silu * up).astype(LOW).reshape(2, 128, 512)
        grad_hidden = dot_nt(gout_ref[py, pc, :, px].reshape(256, D), down_ref[...])
        by_gate = grad_hidden * up * (s + silu * (1.0 - s))
        grads = jnp.concatenate([by_gate, grad_hidden * silu], axis=1).astype(LOW)
        ggu_ref[py, pc, :, px] = grads.reshape(2, 128, 1024)
        return dot_nt(grads, gu_ref[...].reshape(D, 1024)).reshape(2, 128, D)

    scatter = Scatter(product, bufs, sems[:6], x, y, c)
    for k in range(4):
        scatter.to_partner(k)
        scatter.close(k)
    tokens = 2 * SEQ
    for d in (3, 0, 2, 1):
        columns = hidden_ref[:, :, :, :, :, d * 128 : d * 128 + 128].reshape(tokens, 128)
        down_part[d] = dot_tn(columns, gout_ref[...].reshape(tokens, D)).astype(LOW)
    down_grads.phase(0)


    def gateup_grads(d):
        rows = n2_ref[:, :, :, :, :, d * 384 : d * 384 + 384].reshape(tokens, 384)
        grads = dot_tn(rows, ggu_ref[...].reshape(tokens, 1024))
        gu_grad_ref[d] = grads.astype(LOW).reshape(8, 48, 1024)

    gateup_grads(0)
    halves = scatter.result()
    down_grads.phase(1)
    gain_grad = jnp.zeros((1, D), F32)
    for j in range(2):
        by_middle, by_gain = norm_back(halves[j], middle_ref[j], params_ref[:, D : 2 * D])
        gain_grad = gain_grad + by_gain
        grad = gout_ref[y, c, j, x].astype(F32) + by_middle
        gmid_ref[j] = grad
        gmid_low_ref[j] = grad.astype(LOW)
    gain_out_ref[...] = gain_grad
    down_grads.phase(2)
    mixed = dot_nt(gmid_low_ref[...].reshape(256, D), proj_ref[...])
    for u in range(4):
        columns = slice(2 * HW * u, 2 * HW * (u + 1))
        a0, a1 = mixed[:128, columns], mixed[128:, columns]
        packed[2 * u] = jnp.where(half, a0, pltpu.roll(a1, HW, 1)).astype(LOW)
        packed[2 * u + 1] = jnp.where(half, pltpu.roll(a0, HW, 1), a1).astype(LOW)
    swapping = swap_start(packed, swapped_ref, *sems[6:9], x, y, c)
    for d in range(1, 4):
        gateup_grads(d)
    down_grads.phase(3)
    swap_wait(swapping)
    down_grads.finish()
    down_grad_ref[...] = down_part[pl.ds(z, 1)][0]


def ffn_layer(mixed_swapped, proj_full, x, params, gateup_mine, gu_first, gout, down_t, collective_id):
    return pl.pallas_call(
        ffn_kernel,
        out_shape=[
            shape_of((2, 128, D), LOW),
            shape_of((2, 128, D)),
            shape_of((2, 2, 2, 2, 128, 512), LOW),
            shape_of((2, 128, D)),
            shape_of((2, 128, D), LOW),
            shape_of((1, D)),
            shape_of((8, 128, 2 * HW), LOW),
            shape_of((4, 8, 48, 1024), LOW),
            shape_of((128, D), LOW),
        ],
        in_specs=[VM, ANY, VM, VM] + [ANY] * 4,
        out_specs=[VM] * 6 + [ANY] + [VM] * 2,
        scratch_shapes=[
            pltpu.VMEM((2, 128, D), LOW),
            pltpu.VMEM((2, 2, 2, 2, 128, D), LOW), pltpu.VMEM((2, 2, 2, 2, 128, D), LOW),
            pltpu.VMEM((512, D), LOW), pltpu.VMEM((D, D), LOW), pltpu.VMEM((4, 8, 48, 1024), LOW),
            pltpu.VMEM((2, 2, 2, 2, 128, 1024), LOW), pltpu.VMEM((8, 128, 2 * HW), LOW),
            pltpu.VMEM((4, 128, D), LOW), pltpu.VMEM((3, 128, D), LOW), pltpu.VMEM((3, 128, D), LOW),
        ]
        + scatter_scratch(128, D) + scatter_sems() + swap_sems() + line_sems(1) + [DMA((5,))]
        + line_sems(1) + gather_sems(),
        compiler_params=comm_params(collective_id),
        name="ffn_layer",
    )(mixed_swapped, proj_full, x, params, gateup_mine, gu_first, gout, down_t)


def backward_kernel(
    gmix_ref, raw_ref, q_ref, k_ref, v_ref, att_ref, col_ref, crow_ref, logit_ref,
    params_ref, hidden_ref, down_ref, middle_ref, gu_grad_ref, mixed_ref, gmid_low_ref,
    gp_ref, gains_ref, bias_ref, result_ref, gu_out_ref, proj_out_ref,
    do, dq, dk, dv, grow, gcol, gu_part, land_up, land_down, proj_part, *rest,
):
    bufs, more, sems = rest[:7], rest[7:14], rest[14:]
    z, x, y, c = place()
    s = pl.program_id(0)

    def product(px, py, pc):
        return dot_nn(hidden_ref[py, pc, :, px].reshape(256, 512), down_ref[...]).reshape(2, 128, D)

    def proj_product(px, py, pc):
        return proj_part[:, px * 4 + py * 2 + pc].reshape(2, 96, D).astype(F32)

    output = Scatter(product, bufs, sems[0:6], x, y, c)
    proj = Scatter(proj_product, more, sems[6:12], x, y, c)
    gu_grads = LineReduce(gu_part, lambda h: (slice(4 * h, 4 * h + 4),), 2, land_up, land_down, sems[12:16], z)
    load = pltpu.make_async_copy(gu_grad_ref, gu_part, sems[16])
    store = pltpu.make_async_copy(gu_part.at[z], gu_out_ref, sems[16])
    def begin():
        load.start()
        greet(z, x, y, c, line=True)
        load.wait()
        gu_grads.phase(0)
        for d in range(4):
            columns = mixed_ref[:, :, d * 384 : d * 384 + 384].reshape(256, 384)
            grads = dot_tn(columns, gmid_low_ref[...].reshape(256, D))
            proj_part[d] = grads.astype(LOW).reshape(8, 48, D)
        proj.stage(0)

    def proj_end():
        first, second = proj.result()
        proj_out_ref[0:2] = first.astype(LOW).reshape(2, 48, D)
        proj_out_ref[2:4] = second.astype(LOW).reshape(2, 48, D)

    def end():
        first, second = output.result()
        for j, half in enumerate((first, second)):
            result_ref[j] = (middle_ref[j] + half).astype(LOW)
        gu_grads.phase(3)
        store.start()
        gu_grads.finish()
        store.wait()

    hooks = {
        (0, 0): begin, (0, 1): lambda: proj.stage(1), (0, 2): lambda: proj.stage(2), (0, 3): lambda: proj.stage(3),
        (0, 4): lambda: output.stage(0), (0, 5): lambda: output.stage(1), (0, 6): lambda: gu_grads.phase(1, (0,)),
        (0, 7): lambda: proj.stage(4), (0, 8): lambda: output.stage(2), (0, 9): lambda: output.stage(3),
        (0, 11): lambda: gu_grads.phase(1, (1,)), (0, 13): proj_end,
        (1, 1): lambda: gu_grads.phase(2, (0,)), (1, 3): lambda: output.stage(4),
        (1, 6): lambda: gu_grads.phase(2, (1,)), (1, 13): end,
    }

    def hook(n):
        for step in range(2):
            if (step, n) in hooks:
                pl.when(s == step)(hooks[step, n])

    hook(0)
    for cc in range(2):
        for xx in range(2):
            halves = split_halves(gmix_ref[xx, 0, cc].astype(F32))
            for j in range(2):
                dq[pl.ds((cc * 4 + 2 * j + xx) * 128, 128)] = halves[j]
    _, gate = split_halves(raw_ref[0, :, 2 * HW :])
    gate = jax.nn.sigmoid(gate)
    do[...] = (dq[...] * gate).astype(LOW)
    grad_gate = dq[...] * att_ref[0] * gate * (1.0 - gate)
    dk[...] = jnp.zeros_like(dk)
    dv[...] = jnp.zeros_like(dv)
    grow[...] = jnp.zeros_like(grow)
    for i in range(SEQ // QB):
        rows = slice(i * QB, (i + 1) * QB)
        q, grad = q_ref[0, rows], do[rows]
        delta_all = head_sums(grad.astype(F32) * att_ref[0, rows])
        grad_q = jnp.zeros((QB, PAD), F32)
        own_rows = [jnp.zeros((1, QB), F32)] * HEADS
        heads_q = [jnp.where(head_mask(h), q, jnp.zeros((), LOW)) for h in range(HEADS)]
        heads_g = [jnp.where(head_mask(h), grad, jnp.zeros((), LOW)) for h in range(HEADS)]
        stacked_q, stacked_g = jnp.concatenate(heads_q, axis=0), jnp.concatenate(heads_g, axis=0)
        for n, (start, count, own) in enumerate(segments(i)):
            keys = slice(start, start + count)
            k, v = k_ref[0, keys], v_ref[0, keys]
            ones = jnp.ones((8, count), LOW)
            all_p, all_ds = [], []
            for h in range(HEADS):
                scores = dot_nt(heads_q[h], k) - crow_ref[0, h : h + 1, keys] + col_ref[0, rows, h : h + 1]
                p = jnp.exp(causal(scores) if own else scores)
                ds = (p * (dot_nt(heads_g[h], v) - delta_all[:, h * HD : h * HD + 1])).astype(LOW)
                grad_q = grad_q + jnp.where(head_mask(h), dot_nn(ds, k), 0.0)
                own_rows[h] = own_rows[h] + dot_nt(ones, ds)[:1]
                grow[h : h + 1, keys] += dot_nn(ones[:, :QB], ds)[:1]
                all_p.append(p.astype(LOW))
                all_ds.append(ds)
            dk[keys] += dot_tn(jnp.concatenate(all_ds, axis=0), stacked_q)
            dv[keys] += dot_tn(jnp.concatenate(all_p, axis=0), stacked_g)
            hook(1 + i * HEADS + n)
        for h in range(HEADS):
            gcol[h : h + 1, rows] = own_rows[h]
        for n in range(len(segments(i)), HEADS):
            hook(1 + i * HEADS + n)
        dq[rows] = grad_q * scale_dot
    q_raw, k_raw = split_halves(raw_ref[0, :, : 2 * HW])
    q_grad, q_gain = head_norm_back(dq[...], q_raw, head_gain(params_ref, False))
    k_grad, k_gain = head_norm_back(dk[...], k_raw, head_gain(params_ref, True))
    gp_ref[0, :, : 2 * HW] = join_halves(q_grad, k_grad).astype(LOW)
    gp_ref[0, :, 2 * HW : 4 * HW] = join_halves(dv[...], grad_gate).astype(LOW)
    gains_ref[0] = jnp.concatenate([q_gain, k_gain, jnp.zeros((6, PAD), F32)], axis=0)
    head = lax.broadcasted_iota(jnp.int32, (8, SEQ), 0) < HEADS
    change = jnp.where(head, gcol[...] - grow[...], 0.0)
    logits = logit_ref[0]
    grad_logits = running_sum(change, True) * jax.nn.sigmoid(-logits)
    bias_ref[0] = jnp.broadcast_to(jnp.sum(grad_logits, axis=1, keepdims=True), (8, 128))
    parts = pieces_of(grad_logits)
    gp_ref[0, :, 4 * HW :] = columns_of(jnp.concatenate([parts[a] for a, _ in PAIRS], axis=0)).astype(LOW)
    hook(13)


def attention_backward(
    gmix, raw, q, k, v, att, col, crow, logits, params, hidden, down_t, middle, gu_grad,
    mixed, gmid_low, collective_id,
):
    return pl.pallas_call(
        backward_kernel,
        grid=(2,),
        in_specs=[packed_spec(1), seq_spec(SEQ, 4 * HW, 1)]
        + [seq_spec(SEQ, PAD, 1)] * 4
        + [seq_spec(SEQ, 8, 1), seq_spec(8, SEQ), seq_spec(8, SEQ)]
        + [VM, VM, VM, VM, ANY, VM, VM],
        out_specs=[seq_spec(SEQ, 4 * HW + 128, 1), seq_spec(8, PAD), seq_spec(8, 128), VM, ANY, VM],
        scratch_shapes=[pltpu.VMEM((SEQ, PAD), LOW)]
        + [pltpu.VMEM((SEQ, PAD), F32)] * 3
        + [pltpu.VMEM((8, SEQ), F32)] * 2
        + [pltpu.VMEM((4, 8, 48, 1024), LOW)]
        + [pltpu.VMEM((3, 8, 48, 1024), LOW)] * 2
        + [pltpu.VMEM((4, 8, 48, D), LOW)]
        + scatter_scratch(128, D) + scatter_scratch(96, D)
        + scatter_sems() * 2 + line_sems(2) + [DMA],
        out_shape=[
            shape_of((2, SEQ, 4 * HW + 128), LOW), shape_of((2, 8, PAD)), shape_of((2, 8, 128)),
            shape_of((2, 128, D), LOW), shape_of((8, 48, 1024), LOW), shape_of((4, 48, D), LOW),
        ],
        compiler_params=comm_params(collective_id),
        name="attention_backward",
    )(
        gmix, raw, q, k, v, att, col, crow, logits, params, hidden, down_t, middle, gu_grad,
        mixed, gmid_low,
    )


def close_kernel(
    gp_any, normed_any, wq_any, wf_ref, x_ref, params_ref, gmid_ref, gu_ref, result_ref,
    gains_ref, bias_ref, ffn_gain_ref,
    grad_ref, out_ref, small_ref, q_out_ref, gu_out_ref,
    gp_ref, normed_ref, wq_ref, grad_own, q_part, land_up, land_down, forget, small, zbuf, zsum, *rest,
):
    bufs, sems = rest[:7], rest[7:]
    z, x, y, c = place()
    t = x * 4 + y * 2 + c
    loads = [
        pltpu.make_async_copy(gp_any, gp_ref, sems[20].at[0]),
        pltpu.make_async_copy(normed_any, normed_ref, sems[20].at[1]),
        pltpu.make_async_copy(wq_any, wq_ref, sems[20].at[2]),
    ]
    for load in loads:
        load.start()
    greet(z, x, y, c, column=True, line=True, plane=True)
    column_start(result_ref, out_ref, *sems[21:24], z, c)
    tokens = 2 * SEQ

    def product(px, py, pc):
        rows = gp_ref[py, pc, :, px].reshape(256, 4 * HW + 128)
        part = dot_nt(rows[:, : 4 * HW], wq_ref[...]) + dot_nt(rows[:, 4 * HW :], wf_ref[...])
        return part.reshape(2, 128, D)

    grads = Scatter(product, bufs, sems[0:6], x, y, c)
    line = LineReduce(q_part, lambda h: (slice(4 * h, 4 * h + 4),), 2, land_up, land_down, sems[9:13], z)

    def weight_grads(d):
        columns = normed_ref[:, :, :, :, :, d * 384 : d * 384 + 384].reshape(tokens, 384)
        part = dot_tn(columns, gp_ref[...].reshape(tokens, 4 * HW + 128))
        q_part[d] = part[:, : 4 * HW].astype(LOW).reshape(8, 48, 4 * HW)
        forget[d * 384 : d * 384 + 384] = part[:, 4 * HW :]

    for load in loads:
        load.wait()
    grads.stage(0)
    grads.stage(1)
    weight_grads(3)
    weight_grads(0)
    line.begin(0)
    grads.stage(2)
    weight_grads(2)
    weight_grads(1)
    line.begin(1)
    line.begin(2)
    grads.stage(3)
    grads.stage(4)
    gu_swap = swap_start(gu_ref, gu_out_ref, *sems[6:9], x, y, c)
    line.phase(1)
    line.phase(2)
    lane = lanes(D)
    rows = forget[...].T
    rows = rows[0:8] + rows[24:32] + rows[40:48]
    heads = gains_ref[0] + gains_ref[1]
    heads = heads + pltpu.roll(heads, 3 * HD, 1) + pltpu.roll(heads, 2 * HD, 1)
    heads = jnp.concatenate([heads, jnp.zeros((8, D - PAD), F32)], axis=1)
    bias = bias_ref[0] + bias_ref[1]
    gains = jnp.where(lane < HD, heads[0:1], 0.0)
    gains = jnp.where((lane >= HD) & (lane < 2 * HD), pltpu.roll(heads, HD, 1)[1:2], gains)
    for h in range(HEADS):
        gains = jnp.where(lane == 2 * HD + t * HEADS + h, bias[h : h + 1, :1], gains)
    small[0:1] = jnp.zeros((1, D), F32)
    small[1:2] = ffn_gain_ref[...]
    small[2:3] = gains
    for h in range(HEADS):
        small[3 + h : 4 + h] = rows[h : h + 1]
    small[6:8] = jnp.zeros((2, D), F32)
    first, second = grads.result()
    gain_grad = jnp.zeros((1, D), F32)
    for j, grad in enumerate((first, second)):
        by_inputs, by_gain = norm_back(grad, x_ref[j].astype(F32), params_ref[:, :D])
        gain_grad = gain_grad + by_gain
        grad_own[j] = (gmid_ref[j] + by_inputs).astype(LOW)
    column_start(grad_own, grad_ref, *sems[13:16], z, c)
    small[0:1] = gain_grad
    exchange_total(small, zbuf, zsum, small_ref, sems[16:20], z, x, y, c)
    swap_wait(gu_swap)
    line.phase(3)
    q_out_ref[...] = q_part[pl.ds(z, 1)][0]
    column_wait(result_ref, out_ref, *sems[21:24], z, c)
    column_wait(grad_own, grad_ref, *sems[13:16], z, c)
    line.finish()


def close_layer(
    gp, normed, wq, wf, x, params, gmid, gu_grad, result, head_gains, bias_sums, ffn_gain, collective_id
):
    return pl.pallas_call(
        close_kernel,
        out_shape=[
            shape_of((2, 128, D), LOW), shape_of((2, 128, D), LOW), shape_of((8, 8, D)),
            shape_of((8, 48, 4 * HW), LOW), shape_of((8, 48, 1024), LOW),
        ],
        in_specs=[ANY] * 3 + [VM] * 4 + [ANY, ANY] + [VM] * 3,
        out_specs=[ANY, ANY, VM, VM, ANY],
        scratch_shapes=[
            pltpu.VMEM((2, 2, 2, 2, 128, 4 * HW + 128), LOW), pltpu.VMEM((2, 2, 2, 2, 128, D), LOW),
            pltpu.VMEM((D, 4 * HW), LOW),
            pltpu.VMEM((2, 128, D), LOW), pltpu.VMEM((4, 8, 48, 4 * HW), LOW),
            pltpu.VMEM((3, 8, 48, 4 * HW), LOW), pltpu.VMEM((3, 8, 48, 4 * HW), LOW),
            pltpu.VMEM((D, 128), F32), pltpu.VMEM((8, D), F32), pltpu.VMEM((4, 8, D), F32), pltpu.VMEM((8, D), F32),
        ]
        + scatter_scratch(128, D)
        + scatter_sems() + swap_sems() + line_sems(2) + column_sems() + exchange_sems() + [DMA((3,))] + column_sems(),
        compiler_params=comm_params(collective_id),
        name="close_layer",
    )(gp, normed, wq, wf, x, params, gmid, gu_grad, result, head_gains, bias_sums, ffn_gain)


def fast_device(
    block_input,
    cotangent,
    lengths,
    qkvo_weight,
    proj_weight,
    gateup_weight,
    down_weight,
    forget_weight,
    norm_params,
    qkvo_mean,
    qkvo_square,
    proj_mean,
    proj_square,
    gateup_mean,
    gateup_square,
    down_mean,
    down_square,
    forget_mean,
    forget_square,
    params_mean,
    params_square,
):
    rate_proj = rate_dense * (D / max(D // 256, 2)) ** 0.5
    params = norm_params.reshape(1, -1)
    x_own, lens, normed_all, qkvo_t, gateup_mine, forget_cols, proj_mine = open_layer(
        block_input, lengths, params, forget_weight.T, qkvo_weight, gateup_weight, proj_weight, 1
    )
    qkvo_t = qkvo_t.reshape(D, 4 * HW)
    raw, q, k, v, att, col, crow, logits, mixed_swapped, proj_full, down_t, gu_first, gout_all = attention_forward(
        params, lens, normed_all.reshape(2, SEQ, D), qkvo_t, forget_cols, proj_mine, down_weight, gateup_mine,
        cotangent, 2,
    )
    proj_full, down_t = proj_full.reshape(D, D), down_t.reshape(512, D)
    mixed, middle, hidden, gmid, gmid_low, ffn_gain, gmix, gateup_part, down_shard = ffn_layer(
        mixed_swapped, proj_full, x_own, params, gateup_mine, gu_first, gout_all, down_t, 3
    )
    gp, head_gains, bias_sums, result, gateup_part, proj_part = attention_backward(
        gmix.reshape(2, 2, 2, 128, 2 * HW), raw, q, k, v, att, col, crow, logits,
        params, hidden, down_t, middle, gateup_part, mixed, gmid_low, 4,
    )
    input_grad, block_output, small, qkvo_part, gateup_part = close_layer(
        gp.reshape(2, 2, 2, 2, 128, 4 * HW + 128), normed_all, qkvo_t, forget_cols, x_own, params, gmid,
        gateup_part, result, head_gains, bias_sums, ffn_gain, 5,
    )
    qkvo_shard, gateup_shard, proj_shard, norm = norm_layer(
        qkvo_part, gateup_part, proj_part, down_shard, small, 6
    )
    updates = adam_layer(
        (rate_proj, rate_dense, rate_dense, rate_dense),
        norm,
        small,
        input_grad,
        block_output,
        (proj_shard, down_shard, qkvo_shard, gateup_shard),
        (
            proj_weight, proj_mean, proj_square, down_weight, down_mean, down_square,
            qkvo_weight, qkvo_mean, qkvo_square, gateup_weight, gateup_mean, gateup_square,
        ),
        (
            forget_weight.T, forget_mean.T, forget_square.T,
            norm_params, params_mean, params_square,
        ),
    )
    input_grad, block_output, grad_norm, *updates = updates
    proj_new, down_new, qkvo_new, gateup_new = (updates[i : i + 3] for i in (0, 3, 6, 9))
    forget_new = [value.T for value in updates[12:15]]
    params_new = updates[15:18]
    return (
        block_output, input_grad, grad_norm.reshape(()),
        *qkvo_new, *proj_new, *gateup_new, *down_new, *forget_new, *params_new,
    )


def solution(mesh):
    seq_size, dp_size = mesh.shape["seq"], mesh.shape["dp"]
    if (seq_size, dp_size) == (8, 4):
        inner = Mesh(mesh.devices.reshape(4, 2, 2, 2), ("z", "x", "y", "c"))
        seq, dp = ("z", "x"), ("y", "c")
        device_function = fast_device
    else:
        inner, seq, dp = mesh, ("seq",), ("dp",)
        device_function = general_device
    tokens, rows, copied = P(dp, seq, None), P(seq + dp, None), P()
    return jax.shard_map(
        device_function,
        mesh=inner,
        in_specs=(tokens, tokens, P(dp)) + (rows,) * 4 + (copied,) * 2 + (rows,) * 8 + (copied,) * 4,
        out_specs=(tokens, tokens, copied) + (rows,) * 12 + (copied,) * 6,
        check_vma=False,
    )
```
